32 devices in a mesh: group: 2 (over y), adapter: 4 (over z), tensor: 4 (over x, core).
Axes of the slice: x: 2, y: 2, z: 4, core: 2. Of those that a mesh axis runs over, the one named last changes fastest.
Arguments:
- normed_hidden_rows: bfloat16 [24576, 8192], P(('group', 'adapter'), 'tensor'), parts along dimension 0, may hold values from -6 to 6
- key_value_weight: bfloat16 [8192, 2, 1024], P('tensor'), may hold values from -0.0625 to 0.0625
- adapter_down_maps: bfloat16 [24, 8192, 128], P(('group', 'adapter'), 'tensor'), parts along dimension 0, may hold values from -0.0625 to 0.0625
- adapter_up_maps: bfloat16 [24, 2, 64, 1024], P(('group', 'adapter'), None, None, 'tensor'), parts along dimension 0, may hold values from -0.75 to 0.75
- storage_row_table: int32 [24], P('group'), parts along dimension 0, may hold values from 0 to 11, as said below
- adapter_of_request: int32 [96], P(('group', 'adapter')), parts along dimension 0, may hold values from 0 to 11, as said below
- request_token_length: int32 [96], P(('group', 'adapter')), parts along dimension 0, may hold values from 1 to 256, 7680 in all
Outputs:
- kv_states: bfloat16 [24576, 2, 1024], P(('group', 'adapter'), None, 'tensor'), parts along dimension 0
The draws below stay inside these ranges and needn't reach their ends.
There are 2 independent parts, one for each index of `group`. The reference program is written for one: setup_inputs(seed, part) draws one part's arguments, and reference() takes and returns one part's arrays. A program takes and returns all parts, laid end to end along the dimension named above; an argument that names none is the same for every part. Nothing has to cross between parts.
Inputs may be any that keep to these rules, and one draw needn't show every extreme that they name: A permutation: adapter a is stored in row storage_row_table[a] of adapter_down_maps and adapter_up_maps, which lies on index storage_row_table[a] // 3 of adapter. `adapter_of_request`: in each aligned block of 12 requests (those of one index of adapter) the requests fall into groups of exactly 3, only the last group smaller when 3 does not divide 12; the adapters of one group are all stored on one index of adapter, different groups on different indices; requests may share an adapter.
All inputs are finite; a program needn't handle non-finite values. No bound on the sum of `request_token_length` on one device may be relied on, other than what follows from the above.
Results may differ from the reference program's by a relative error of at most 0.013.
Values may be sent and summed in bfloat16 or wider, within the bound.
No kernel may reach another device: no remote copies, remote signals or barrier semaphores. Data moves between devices by JAX's collectives and lax.ppermute only.
A program may use at most 128 MiB of HBM per device.

```python
import math
import jax
import jax.numpy as jnp
import numpy as np
from jax import lax

MODEL_WIDTH = 8192
KEY_VALUE_WIDTH = 1024
ADAPTER_RANK = 64
PREFILL_LEN = 256
REQ_DEV = 12
ADP_DEV = 3
REQUESTS = 48
TOKENS = 12288
ADAPTER_COUNT = 12
CAP = 3
N_TENSOR = 4


def shared_rows(key):
    return jax.random.permutation(key, ADAPTER_COUNT).astype(jnp.int32)


def draw_storage_row_table(key, part):
    slot_table = shared_rows(key)
    return slot_table


def draw_adapter_of_request(key, part):
    slot_table = shared_rows(key)
    key = jax.random.fold_in(key, 13)
    blocks = REQUESTS // REQ_DEV
    holder = jnp.zeros((ADAPTER_COUNT,), jnp.int32).at[slot_table].set(jnp.arange(ADAPTER_COUNT, dtype=jnp.int32))
    key_owner, key_order, key_first, key_second = jax.random.split(key, 4)
    owner_base = jnp.tile(jnp.arange(blocks, dtype=jnp.int32)[None, :], (blocks, 1))
    owner_perm = jax.random.permutation(key_owner, owner_base, axis=1, independent=True)
    group_index = jnp.arange(REQ_DEV, dtype=jnp.int32) // CAP
    owners = owner_perm[:, group_index]
    order_base = jnp.tile(jnp.arange(REQ_DEV, dtype=jnp.int32)[None, :], (blocks, 1))
    shuffle = jax.random.permutation(key_order, order_base, axis=1, independent=True)
    owners = jnp.take_along_axis(owners, shuffle, axis=1)
    first_draw = jax.random.randint(key_first, (blocks, REQ_DEV), 0, ADP_DEV, dtype=jnp.int32)
    second_draw = jax.random.randint(key_second, (blocks, REQ_DEV), 0, ADP_DEV, dtype=jnp.int32)
    local_slot = jnp.minimum(first_draw, second_draw)
    chosen = owners * ADP_DEV + local_slot
    return holder[chosen].reshape(REQUESTS).astype(jnp.int32)


def block_levels(own_key, shape, pieces, least, top_value):
    def one(position, blocks):
        draws = jax.random.uniform(jax.random.fold_in(jax.random.fold_in(own_key, 6), position), (blocks,), jnp.float32, least / len(pieces), top_value / len(pieces))
        return jnp.repeat(jnp.exp(draws), shape[position] // blocks).reshape((-1,) + (1,) * (len(shape) - position - 1))

    factor_of = one(*pieces[0])
    for cut in pieces[1:]:
        factor_of = factor_of * one(*cut)
    return factor_of


def split_up(count, total, limit, slope):
    loads = [(1 << 20) // math.isqrt(rank ** slope) + 1 for rank in range(2, count + 1)]
    surplus, given = total - limit - (count - 1), [1] * (count - 1)
    while surplus > 0:
        candidates = [i for i in range(count - 1) if given[i] < limit]
        mass, remaining = sum([loads[i] for i in candidates]), surplus
        for i in candidates:
            addition = min(limit - given[i], max(1, remaining * loads[i] // mass), surplus)
            given[i] = given[i] + addition
            surplus = surplus - addition
    return np.array([limit] + given)


def uneven(own_key, amount, total, bound, skew):
    if amount == 2:
        one = jax.random.randint(own_key, (), max(1, total - bound), min(bound, total - 1) + 1)
        return jnp.stack([one, total - one])
    lengths = jnp.asarray(split_up(amount, total, bound, skew), jnp.int32)
    pairs = (amount - 1) // 2
    giver, taker = lengths[1:1 + 2 * pairs:2], lengths[2:2 + 2 * pairs:2]
    margin = jnp.minimum(giver - 1, bound - taker)
    passed = jax.random.randint(jax.random.fold_in(own_key, 1), (pairs,), 0, 1 << 20) % (margin + 1)
    lengths = lengths.at[1:1 + 2 * pairs:2].set(giver - passed).at[2:2 + 2 * pairs:2].set(taker + passed)
    return lengths[jax.random.permutation(jax.random.fold_in(own_key, 2), amount)]


def gaussian(rng, dims, deviation, most, cuts=(), held_as=jnp.bfloat16):
    values = jax.random.normal(rng, dims, jnp.float32) * deviation
    if len(cuts) > 0:
        values = block_levels(rng, dims, cuts, -0.22, 0.18) * values
    return jnp.clip(values, min=-most, max=most).astype(held_as)


def setup_inputs(seed: int = 0, part: int = 0) -> dict:
    key_list = jax.random.split(jax.random.key(seed), 8)
    part_splits = jax.random.split(jax.random.fold_in(key_list[7], part), 8)
    normed_hidden_rows = gaussian(part_splits[0], (TOKENS, MODEL_WIDTH), 1.0, 6.0, ((0, 4), (1, 4)))
    key_value_weight = gaussian(key_list[1], (MODEL_WIDTH, 2, KEY_VALUE_WIDTH), MODEL_WIDTH ** -0.5, 0.0625, ((0, 4),))
    adapter_down_maps = gaussian(part_splits[2], (ADAPTER_COUNT, MODEL_WIDTH, 2 * ADAPTER_RANK), MODEL_WIDTH ** -0.5, 0.0625, ((0, 4), (1, 4)))
    adapter_up_maps = gaussian(part_splits[3], (ADAPTER_COUNT, 2, ADAPTER_RANK, KEY_VALUE_WIDTH), ADAPTER_RANK ** -0.5, 0.75, ((0, 4), (3, 4)))
    storage_row_table = draw_storage_row_table(jax.random.fold_in(jax.random.fold_in(key_list[7], part), 71), part)
    adapter_of_request = draw_adapter_of_request(jax.random.fold_in(jax.random.fold_in(key_list[7], part), 71), part)
    request_token_length = uneven(part_splits[6], REQUESTS, REQUESTS * PREFILL_LEN * 5 // 8, PREFILL_LEN, 2).astype(jnp.int32)
    return dict(normed_hidden_rows=normed_hidden_rows, key_value_weight=key_value_weight, adapter_down_maps=adapter_down_maps, adapter_up_maps=adapter_up_maps, storage_row_table=storage_row_table, adapter_of_request=adapter_of_request, request_token_length=request_token_length)


def reference(normed_hidden_rows, key_value_weight, adapter_down_maps, adapter_up_maps, storage_row_table, adapter_of_request, request_token_length):
    shard_cols = MODEL_WIDTH // N_TENSOR
    flat_weight = key_value_weight.reshape(MODEL_WIDTH, 2 * KEY_VALUE_WIDTH)

    def add_shard(shard_index, running):
        columns = lax.dynamic_slice_in_dim(normed_hidden_rows, shard_index * shard_cols, shard_cols, 1)
        weight_rows = lax.dynamic_slice_in_dim(flat_weight, shard_index * shard_cols, shard_cols, 0)
        shard_term = jnp.dot(columns, weight_rows, preferred_element_type=jnp.float32)
        shard_term = lax.optimization_barrier(shard_term.astype(jnp.bfloat16)).astype(jnp.float32)
        return running + shard_term

    base_term = lax.fori_loop(0, N_TENSOR, add_shard, jnp.zeros((TOKENS, 2 * KEY_VALUE_WIDTH), jnp.float32))
    slot_of = storage_row_table[adapter_of_request].astype(jnp.int32)
    token_blocks = normed_hidden_rows.reshape(REQUESTS, PREFILL_LEN, MODEL_WIDTH)

    def one_request(inputs):
        request_rows, request_position = inputs
        down_matrix_rows = adapter_down_maps[request_position]
        rank_products = jnp.dot(request_rows, down_matrix_rows, preferred_element_type=jnp.float32).astype(jnp.bfloat16)
        key_contribution = jnp.dot(rank_products[:, :ADAPTER_RANK], adapter_up_maps[request_position, 0], preferred_element_type=jnp.float32)
        value_contribution = jnp.dot(rank_products[:, ADAPTER_RANK:], adapter_up_maps[request_position, 1], preferred_element_type=jnp.float32)
        return jnp.stack([key_contribution, value_contribution], axis=1)

    adapter_term = lax.map(one_request, (token_blocks, slot_of))
    live_mask = (jnp.arange(PREFILL_LEN, dtype=jnp.int32)[None, :] < request_token_length[:, None]).astype(jnp.float32)
    mixed = (base_term.reshape(REQUESTS, PREFILL_LEN, 2, KEY_VALUE_WIDTH) + adapter_term) * live_mask[:, :, None, None]
    return mixed.reshape(TOKENS, 2, KEY_VALUE_WIDTH).astype(jnp.bfloat16)
```

```python
import jax
import jax.numpy as jnp
from jax import lax
from jax.experimental import pallas as pl
from jax.experimental.pallas import tpu as pltpu
from jax.sharding import PartitionSpec as P

BF = jnp.bfloat16
F32 = jnp.float32
CHUNKS = 4
SMEM = pltpu.SMEM
ORDER, SOURCE, ROW, LENGTH, KEYS = 0, 32, 64, 96, 128
PLAN = 256


def params(mib, **more):
    return pltpu.CompilerParams(vmem_limit_bytes=mib * 1024 * 1024, **more)


def plan_requests(table, adapters, lengths, here, n_z, stored):
    requests = adapters.shape[0]

    def body(table_ref, adapter_ref, length_ref, here_ref, plan_ref):
        me = here_ref[0]

        def key_of(r, carry):
            owner = table_ref[adapter_ref[r]] // stored
            distance = jnp.abs(owner - me)
            plan_ref[KEYS + r] = distance * requests + r
            return carry

        lax.fori_loop(0, requests, key_of, 0)

        def place(r, carry):
            mine = plan_ref[KEYS + r]
            position = lax.fori_loop(
                0,
                requests,
                lambda q, n: n + jnp.where(plan_ref[KEYS + q] < mine, 1, 0),
                jnp.int32(0),
            )
            row = table_ref[adapter_ref[r]]
            owner = row // stored
            source = jnp.where(owner >= me, owner - me, n_z - 1 + me - owner)
            plan_ref[ORDER + position] = r
            plan_ref[SOURCE + position] = source
            plan_ref[ROW + position] = row - owner * stored
            plan_ref[LENGTH + position] = length_ref[r]
            return carry

        lax.fori_loop(0, requests, place, 0)

    return pl.pallas_call(
        body,
        out_shape=jax.ShapeDtypeStruct((PLAN,), jnp.int32),
        in_specs=[pl.BlockSpec(memory_space=SMEM)] * 4,
        out_specs=pl.BlockSpec(memory_space=SMEM),
        name="plan_requests",
    )(table, adapters, lengths, here)


def split_weight(weight, slots):
    features, _, columns = weight.shape
    n_t = slots.shape[0]
    width = columns // n_t
    rows, half = 256, 128

    def body(slot_ref, w_ref, o_ref):
        out_row = lax.broadcasted_iota(jnp.int32, (2 * half, 2 * half), 0)
        in_row = lax.broadcasted_iota(jnp.int32, (2 * half, 2 * half), 1)
        pick = in_row == 2 * (out_row % half) + out_row // half
        pick = pick.astype(F32).astype(BF)
        for b in range(rows // half):
            mixed = w_ref[b * half : (b + 1) * half].reshape(2 * half, columns)
            apart = jnp.dot(pick, mixed, preferred_element_type=F32).astype(BF)
            for t in range(n_t):
                for s in range(2):
                    o_ref[
                        slot_ref[t],
                        b * half : (b + 1) * half,
                        s * width : (s + 1) * width,
                    ] = apart[s * half : (s + 1) * half, t * width : (t + 1) * width]

    return pl.pallas_call(
        body,
        out_shape=jax.ShapeDtypeStruct((n_t, features, 2 * width), BF),
        grid_spec=pltpu.PrefetchScalarGridSpec(
            num_scalar_prefetch=1,
            grid=(features // rows,),
            in_specs=[pl.BlockSpec((rows, 2, columns), lambda i, s: (i, 0, 0))],
            out_specs=pl.BlockSpec((n_t, rows, 2 * width), lambda i, s: (0, i, 0)),
        ),
        compiler_params=params(32),
        cost_estimate=pl.CostEstimate(
            flops=4 * half * features * 2 * columns // 2,
            bytes_accessed=8 * features * columns,
            transcendentals=0,
        ),
        name="split_weight",
    )(slots, weight)


def base_products(plan, hidden, weight, chunk, count, prefill):
    n_t, features, width = weight.shape
    n_x = n_t // 2
    first = chunk * count
    short = prefill // 2

    def body(plan_ref, x_ref, w_ref, send_ref, keep_ref):
        live = plan_ref[LENGTH + first + pl.program_id(0)]

        def products(rows):
            for j in range(n_t):
                out = send_ref if j < n_x else keep_ref
                out[j % n_x, :rows] = jnp.dot(
                    x_ref[:rows], w_ref[j], preferred_element_type=F32
                ).astype(BF)
                if rows < prefill:
                    out[j % n_x, rows:] = jnp.zeros((prefill - rows, width), BF)

        @pl.when(live > short)
        def _():
            products(prefill)

        @pl.when(live <= short)
        def _():
            products(short)

    out = jax.ShapeDtypeStruct((n_x, count * prefill, width), BF)
    block = pl.BlockSpec((n_x, prefill, width), lambda i, p: (0, i, 0))
    return pl.pallas_call(
        body,
        out_shape=(out, out),
        grid_spec=pltpu.PrefetchScalarGridSpec(
            num_scalar_prefetch=1,
            grid=(count,),
            in_specs=[
                pl.BlockSpec(
                    (prefill, features), lambda i, p: (p[ORDER + first + i], 0)
                ),
                pl.BlockSpec((n_t, features, width), lambda i, p: (0, 0, 0)),
            ],
            out_specs=(block, block),
        ),
        compiler_params=params(40),
        cost_estimate=pl.CostEstimate(
            flops=2 * count * prefill * features * width * n_t,
            bytes_accessed=2 * (count * prefill * (features + n_t * width))
            + 2 * n_t * features * width,
            transcendentals=0,
        ),
        name="base_products",
    )(plan, hidden, weight)


def fetch(refs, source, row, target, sem):
    for k, ref in enumerate(refs):

        @pl.when(source == k)
        def _():
            pltpu.make_async_copy(ref.at[row], target, sem).start()


def rank_products(plan, hidden, maps, chunk, count, prefill):
    _, features, ranks = maps[0].shape
    first = chunk * count

    def body(plan_ref, x_ref, *rest):
        refs, (o_ref, held, sems) = rest[: len(maps)], rest[len(maps) :]
        step = pl.program_id(0)

        @pl.when(step == 0)
        def _():
            for i in range(count):
                fetch(
                    refs,
                    plan_ref[SOURCE + first + i],
                    plan_ref[ROW + first + i],
                    held.at[i],
                    sems.at[i],
                )

        pltpu.make_async_copy(refs[0].at[0], held.at[step], sems.at[step]).wait()
        o_ref[...] = jnp.dot(
            x_ref[...], held[step], preferred_element_type=F32
        ).astype(BF)

    return pl.pallas_call(
        body,
        out_shape=jax.ShapeDtypeStruct((count * prefill, ranks), BF),
        grid_spec=pltpu.PrefetchScalarGridSpec(
            num_scalar_prefetch=1,
            grid=(count,),
            in_specs=[
                pl.BlockSpec(
                    (prefill, features), lambda i, p: (p[ORDER + first + i], 0)
                )
            ]
            + [pl.BlockSpec(memory_space=pl.ANY)] * len(maps),
            out_specs=pl.BlockSpec((prefill, ranks), lambda i, p: (i, 0)),
            scratch_shapes=[
                pltpu.VMEM((count, features, ranks), BF),
                pltpu.SemaphoreType.DMA((count,)),
            ],
        ),
        compiler_params=params(32),
        cost_estimate=pl.CostEstimate(
            flops=2 * count * prefill * features * ranks,
            bytes_accessed=2 * count * features * (prefill + ranks),
            transcendentals=0,
        ),
        name="rank_products",
    )(plan, hidden, *maps)


def finish(plan, bases, ranks, maps, before, chunk, count, prefill, shape):
    first = chunk * count
    _, _, depth, columns = maps[0].shape
    half = prefill // 2
    n_base, n_rank, n_map = len(bases), len(ranks), len(maps)

    def body(plan_ref, *rest):
        base_refs, rest = rest[:n_base], rest[n_base:]
        rank_refs, rest = rest[:n_rank], rest[n_rank:]
        map_refs, rest = rest[:n_map], rest[n_map:]
        o_ref, held, sems = rest[-3:]
        step = pl.program_id(0)

        @pl.when(step == 0)
        def _():
            for i in range(count):
                fetch(
                    map_refs,
                    plan_ref[SOURCE + first + i],
                    plan_ref[ROW + first + i],
                    held.at[i],
                    sems.at[i],
                )

        pltpu.make_async_copy(map_refs[0].at[0], held.at[step], sems.at[step]).wait()
        live = plan_ref[LENGTH + first + step]
        up = held[step].reshape(2 * depth, columns)
        mix_row = lax.broadcasted_iota(jnp.int32, (2 * half, 2 * half), 0)
        mix_column = lax.broadcasted_iota(jnp.int32, (2 * half, 2 * half), 1)
        mix = mix_column == mix_row // 2 + half * (mix_row % 2)
        mix = mix.astype(F32).astype(BF)
        twice_row = lax.broadcasted_iota(jnp.int32, (2 * half, half), 0)
        twice_column = lax.broadcasted_iota(jnp.int32, (2 * half, half), 1)
        twice = (twice_column == twice_row // 2).astype(F32).astype(BF)
        lane = lax.broadcasted_iota(jnp.int32, (2 * half, 2 * depth), 1)
        side = lax.broadcasted_iota(jnp.int32, (2 * half, 2 * depth), 0) % 2
        own_side = lane // depth == side
        token = lax.broadcasted_iota(jnp.int32, (2 * half, columns), 0) // 2
        for b in range(2):
            rows = slice(b * half, (b + 1) * half)
            total = jnp.zeros((2 * half, columns), F32)
            for ref in base_refs:
                piece = ref[0, rows] if len(ref.shape) == 3 else ref[rows]
                piece = jnp.concatenate([piece[:, :columns], piece[:, columns:]], 0)
                total += jnp.dot(mix, piece, preferred_element_type=F32)
            rank = rank_refs[0][rows].astype(F32)
            for ref in rank_refs[1:]:
                rank += ref[rows].astype(F32)
            rank = jnp.dot(twice, rank.astype(BF), preferred_element_type=F32)
            rank = jnp.where(own_side, rank, 0.0).astype(BF)
            total += jnp.dot(rank, up, preferred_element_type=F32)
            total = jnp.where(token + b * half < live, total, 0.0)
            o_ref[rows] = total.astype(BF).reshape(half, 2, columns)

    base_specs = [
        pl.BlockSpec((1, prefill, 2 * columns), lambda i, p: (0, i, 0))
        if a.ndim == 3
        else pl.BlockSpec((prefill, 2 * columns), lambda i, p: (i, 0))
        for a in bases
    ]
    operands = [plan, *bases, *ranks, *maps]
    specs = (
        base_specs
        + [pl.BlockSpec((prefill, 2 * depth), lambda i, p: (i, 0))] * n_rank
        + [pl.BlockSpec(memory_space=pl.ANY)] * n_map
    )
    aliases = {}
    if before is not None:
        aliases = {len(operands): 0}
        operands.append(before)
        specs.append(pl.BlockSpec(memory_space=pl.ANY))
    return pl.pallas_call(
        body,
        out_shape=jax.ShapeDtypeStruct(shape, BF),
        grid_spec=pltpu.PrefetchScalarGridSpec(
            num_scalar_prefetch=1,
            grid=(count,),
            in_specs=specs,
            out_specs=pl.BlockSpec(
                (prefill, 2, columns), lambda i, p: (p[ORDER + first + i], 0, 0)
            ),
            scratch_shapes=[
                pltpu.VMEM((count, 2, depth, columns), BF),
                pltpu.SemaphoreType.DMA((count,)),
            ],
        ),
        input_output_aliases=aliases,
        compiler_params=params(32),
        cost_estimate=pl.CostEstimate(
            flops=8 * count * prefill * prefill * 2 * columns,
            bytes_accessed=10 * count * prefill * columns * 2,
            transcendentals=0,
        ),
        name="finish",
    )(*operands)


def solution(mesh):
    n_z, n_t = mesh.shape["adapter"], mesh.shape["tensor"]
    n_x = n_t // 2

    def core_swap(a):
        return lax.ppermute(a, "tensor", [(t, t ^ 1) for t in range(n_t)])

    def chip_shift(a, k):
        return lax.ppermute(
            a,
            "tensor",
            [(2 * x + c, 2 * ((x + k) % n_x) + c) for x in range(n_x) for c in (0, 1)],
        )

    def down_line(a):
        return lax.ppermute(a, "adapter", [(z, z - 1) for z in range(1, n_z)])

    def up_line(a):
        return lax.ppermute(a, "adapter", [(z - 1, z) for z in range(1, n_z)])

    def per_device(hidden, weight, down, up, table, adapters, lengths):
        requests = adapters.shape[0]
        prefill = hidden.shape[0] // requests
        stored = down.shape[0]
        columns = up.shape[3]
        count = requests // CHUNKS
        by_distance = n_z == CHUNKS
        z, t = lax.axis_index("adapter"), lax.axis_index("tensor")
        plan = plan_requests(
            table, adapters, lengths, jnp.reshape(z, (1,)), n_z, stored
        )

        near_down, near_up = [(down, up)], [(down, up)]
        for _ in range(n_z - 1):
            d, u = near_down[-1]
            near_down.append((down_line(d), down_line(u)))
            d, u = near_up[-1]
            near_up.append((up_line(d), up_line(u)))

        def arrived(step, which):
            held = [own[which] for own in near_down[: step + 1]]
            held += [down if which == 0 else up] * (n_z - 1 - step)
            held += [own[which] for own in near_up[1 : step + 1]]
            return held

        dest = jnp.arange(n_t, dtype=jnp.int32)
        away = (dest // 2 - t // 2 + n_x) % n_x
        slots = jnp.where(dest % 2 == t % 2, n_x + away, away)
        split = split_weight(weight, slots)

        shape = (requests * prefill, 2, columns)
        out = None
        bases = []
        for chunk in range(CHUNKS):
            send, keep = base_products(plan, hidden, split, chunk, count, prefill)
            got = core_swap(send)
            pieces = [keep, got]
            for k in range(1, n_x):
                pair = keep[k].astype(F32) + got[k].astype(F32)
                pieces.append(chip_shift(pair.astype(BF), k))
            bases.append(pieces)
        for chunk in range(CHUNKS):
            step = chunk if by_distance else n_z - 1
            part = rank_products(
                plan, hidden, arrived(step, 0), chunk, count, prefill
            )
            pair = part.astype(F32) + core_swap(part).astype(F32)
            pair = pair.astype(BF)
            ranks = [pair] + [chip_shift(pair, k) for k in range(1, n_x)]
            out = finish(
                plan,
                bases[chunk],
                ranks,
                arrived(step, 1),
                out,
                chunk,
                count,
                prefill,
                shape,
            )
        return out

    return jax.shard_map(
        per_device,
        mesh=mesh,
        in_specs=(
            P(("group", "adapter"), "tensor"),
            P("tensor", None, None),
            P(("group", "adapter"), "tensor", None),
            P(("group", "adapter"), None, None, "tensor"),
            P("group"),
            P(("group", "adapter")),
            P(("group", "adapter")),
        ),
        out_specs=P(("group", "adapter"), None, "tensor"),
        check_vma=False,
    )
```

```python
import jax
import jax.numpy as jnp
from jax import lax
from jax.experimental import pallas as pl
from jax.experimental.pallas import tpu as pltpu
from jax.sharding import PartitionSpec as P

BF = jnp.bfloat16
F32 = jnp.float32
BASE_CHUNKS = (4, 4, 4)
RANK_CHUNKS = (6, 3, 3)
SMEM = pltpu.SMEM
LEFT, RIGHT, ORDER, SOURCE, PLACE, MISC = range(6)
STEPS, CORE = 0, 1
ANY = pl.BlockSpec(memory_space=pl.ANY)


def params(mib=60):
    return pltpu.CompilerParams(vmem_limit_bytes=mib * 1024 * 1024)


SMALL = pl.CostEstimate(flops=0, bytes_accessed=0, transcendentals=0)


def pack_maps(down, up):
    stored, features, lanes = down.shape
    _, sides, depth, columns = up.shape
    tiles = columns // lanes
    extra = tiles * sides * depth

    def body(down_ref, up_ref, *rest):
        outs, (held, sems) = rest[:stored], rest[stored:]
        copies = []
        for a in range(stored):
            copies.append(
                pltpu.make_async_copy(
                    down_ref.at[a], outs[a].at[0, pl.ds(0, features)], sems.at[0, a]
                )
            )
            copies[-1].start()
        for a in range(stored):
            flat = up_ref[a].reshape(sides * depth, columns)
            for j in range(tiles):
                held[a, j * sides * depth : (j + 1) * sides * depth] = flat[
                    :, j * lanes : (j + 1) * lanes
                ]
            copies.append(
                pltpu.make_async_copy(
                    held.at[a], outs[a].at[0, pl.ds(features, extra)], sems.at[1, a]
                )
            )
            copies[-1].start()
        for copy in copies:
            copy.wait()

    return pl.pallas_call(
        body,
        out_shape=[jax.ShapeDtypeStruct((1, features + extra, lanes), BF)] * stored,
        in_specs=[ANY, pl.BlockSpec(memory_space=pltpu.VMEM)],
        out_specs=[ANY] * stored,
        scratch_shapes=[
            pltpu.VMEM((stored, extra, lanes), BF),
            pltpu.SemaphoreType.DMA((2, stored)),
        ],
        compiler_params=params(),
        cost_estimate=SMALL,
        name="pack_maps",
    )(down, up)


def plan_moves(rows, here, n_z, stored, limit):
    devices, requests = rows.shape
    wide = (devices, 128)
    square = (requests, 128)
    late = 1 << 20

    def body(rows_ref, here_ref, plan_ref):
        lane = lax.broadcasted_iota(jnp.int32, wide, 1)
        device = lax.broadcasted_iota(jnp.int32, wide, 0)
        z = device % n_z
        owner = lane // stored
        table = rows_ref[...]
        need = jnp.zeros(wide, jnp.int32)
        for r in range(requests):
            need = jnp.where(table[:, r : r + 1] == lane, 1, need)
        exists = lane < n_z * stored
        zeros = jnp.zeros(wide, jnp.int32)
        steps = jnp.int32(0)
        found = jnp.where(owner == z, lane % stored, 0)
        came = zeros
        codes = []
        for way in (-1, 1):
            def toward(a, by, fill):
                pad = jnp.full((by, 128), fill, a.dtype)
                if way < 0:
                    return jnp.concatenate([a[by:], pad], 0)
                return jnp.concatenate([pad, a[:-by]], 0)

            def back(a, by, fill):
                pad = jnp.full((by, 128), fill, a.dtype)
                if way < 0:
                    return jnp.concatenate([pad, a[:-by]], 0)
                return jnp.concatenate([a[by:], pad], 0)

            ahead = z if way < 0 else n_z - 1 - z
            behind = (owner - z) if way < 0 else (z - owner)
            far = zeros
            for hop in range(1, n_z):
                named = (back(need, hop, 0) > 0) & (ahead >= hop)
                far = jnp.where(named, hop, far)
            wanted = exists & (far > 0) & (behind >= 0)
            score = (n_z - far) * 1024 + behind * 32 + lane % stored
            sent = zeros
            got = jnp.where(behind == 0, -9, late)
            code_of = jnp.where(behind == 0, lane % stored, 0)
            code = zeros
            for i in range(limit):
                if i < 2:
                    pick = (behind == 0) & (lane % stored == i) & (ahead > 0) & exists
                else:
                    can = wanted & (sent == 0) & (got <= i - 2)
                    rank = jnp.where(can, score, late)
                    pick = can & (rank == jnp.min(rank, axis=1, keepdims=True))
                take = jnp.sum(
                    jnp.where(pick, code_of, 0), axis=1, keepdims=True
                )
                code = jnp.where(lane == i, take, code)
                chosen = jnp.where(pick, 1, 0)
                sent = sent | chosen
                here_now = (toward(chosen, 1, 0) > 0) & (behind > 0)
                got = jnp.where(here_now & (got == late), i, got)
                code_of = jnp.where(here_now, stored + i, code_of)
            codes.append(code)
            mine = (need > 0) & (behind > 0) & exists
            steps = jnp.maximum(steps, jnp.max(jnp.where(mine, got + 1, 0)))
            shift = 0 if way < 0 else limit
            found = jnp.where(behind > 0, code_of + shift, found)
            came = jnp.where(behind > 0, got + 1, came)

        me = here_ref[0]

        def own(a):
            return jnp.sum(jnp.where(device == me, a, 0), axis=0, keepdims=True)

        left, right, found, came = own(codes[0]), own(codes[1]), own(found), own(came)
        request = lax.broadcasted_iota(jnp.int32, square, 0)
        column = lax.broadcasted_iota(jnp.int32, square, 1)
        named = own(jnp.where(lane < requests, jnp.pad(table, ((0, 0), (0, 128 - requests))), 0))
        diagonal = request == column

        def rows_of(a):
            return jnp.sum(jnp.where(diagonal, a, 0), axis=1, keepdims=True)

        def lanes_of(a):
            return jnp.sum(jnp.where(diagonal, a, 0), axis=0, keepdims=True)

        hit = rows_of(named) == column
        source = jnp.sum(jnp.where(hit, found, 0), axis=1, keepdims=True)
        key = jnp.sum(jnp.where(hit, came, 0), axis=1, keepdims=True)
        key = key * 128 + request[:, :1]
        before = (lanes_of(key) < key) & (column < requests)
        place = jnp.sum(jnp.where(before, 1, 0), axis=1, keepdims=True)
        at = place == column
        order = jnp.sum(jnp.where(at, request, 0), axis=0, keepdims=True)
        source = jnp.sum(jnp.where(at, source, 0), axis=0, keepdims=True)
        first = lax.broadcasted_iota(jnp.int32, (1, 128), 1)
        misc = jnp.where(first == STEPS, steps, here_ref[1])
        plan_ref[LEFT : LEFT + 1] = left
        plan_ref[RIGHT : RIGHT + 1] = right
        plan_ref[ORDER : ORDER + 1] = order
        plan_ref[SOURCE : SOURCE + 1] = source
        plan_ref[PLACE : PLACE + 1] = lanes_of(place)
        plan_ref[MISC : MISC + 1] = misc

    return pl.pallas_call(
        body,
        out_shape=jax.ShapeDtypeStruct((8, 128), jnp.int32),
        in_specs=[
            pl.BlockSpec(memory_space=pltpu.VMEM),
            pl.BlockSpec(memory_space=SMEM),
        ],
        out_specs=pl.BlockSpec(memory_space=pltpu.VMEM),
        cost_estimate=SMALL,
        name="plan_moves",
    )(rows, here)


def fetch(refs, code, target, sem, part=None):
    if len(refs) == 1:
        refs_at = [(refs[0].at[code], None)]
    else:
        refs_at = [(ref.at[0], k) for k, ref in enumerate(refs)]
    for ref, k in refs_at:
        if part is not None:
            ref = ref.at[part]
        copy = pltpu.make_async_copy(ref, target, sem)
        if k is None:
            copy.start()
        else:
            pl.when(code == k)(copy.start)


def choose_maps(plan, step, own, lefts, rights):
    n_own, n_left = len(own), len(lefts)
    shape = own[0].shape

    def body(plan_ref, *refs):
        to_left, to_right, sems = refs[-3:]
        refs = refs[:-3]
        left = refs[:n_own] + refs[n_own : n_own + n_left]
        right = refs[:n_own] + refs[n_own + n_left :]
        fetch(left, plan_ref[LEFT, step], to_left.at[0], sems.at[0])
        fetch(right, plan_ref[RIGHT, step], to_right.at[0], sems.at[1])
        pltpu.make_async_copy(refs[0].at[0], to_left.at[0], sems.at[0]).wait()
        pltpu.make_async_copy(refs[0].at[0], to_right.at[0], sems.at[1]).wait()

    return pl.pallas_call(
        body,
        out_shape=[jax.ShapeDtypeStruct(shape, BF)] * 2,
        grid_spec=pltpu.PrefetchScalarGridSpec(
            num_scalar_prefetch=1,
            grid=(),
            in_specs=[ANY] * (n_own + n_left + len(rights)),
            out_specs=[ANY] * 2,
            scratch_shapes=[pltpu.SemaphoreType.DMA((2,))],
        ),
        compiler_params=params(),
        cost_estimate=SMALL,
        name="choose_maps",
    )(plan, *own, *lefts, *rights)


def split_weight(weight, slots):
    features, _, columns = weight.shape
    n_t = slots.shape[0]
    width = columns // n_t
    rows, half = 256, 128

    def body(slot_ref, w_ref, o_ref):
        out_row = lax.broadcasted_iota(jnp.int32, (2 * half, 2 * half), 0)
        in_row = lax.broadcasted_iota(jnp.int32, (2 * half, 2 * half), 1)
        pick = in_row == 2 * (out_row % half) + out_row // half
        pick = pick.astype(F32).astype(BF)
        for b in range(rows // half):
            mixed = w_ref[b * half : (b + 1) * half].reshape(2 * half, columns)
            apart = jnp.dot(pick, mixed, preferred_element_type=F32).astype(BF)
            for t in range(n_t):
                for s in range(2):
                    o_ref[
                        slot_ref[t],
                        b * half : (b + 1) * half,
                        s * width : (s + 1) * width,
                    ] = apart[s * half : (s + 1) * half, t * width : (t + 1) * width]

    return pl.pallas_call(
        body,
        out_shape=jax.ShapeDtypeStruct((n_t, features, 2 * width), BF),
        grid_spec=pltpu.PrefetchScalarGridSpec(
            num_scalar_prefetch=1,
            grid=(features // rows,),
            in_specs=[pl.BlockSpec((rows, 2, columns), lambda i, s: (i, 0, 0))],
            out_specs=pl.BlockSpec((n_t, rows, 2 * width), lambda i, s: (0, i, 0)),
        ),
        compiler_params=params(),
        cost_estimate=SMALL,
        name="split_weight",
    )(slots, weight)


def base_products(lengths, hidden, weight, first, count, prefill, after):
    n_t, features, width = weight.shape
    n_x = n_t // 2
    short = prefill // 2
    n_after = len(after)

    def body(length_ref, x_ref, w_ref, *rest):
        send_ref, keep_ref = rest[n_after:]
        live = length_ref[first + pl.program_id(0)]

        def products(rows):
            for j in range(n_t):
                out = send_ref if j < n_x else keep_ref
                out[j % n_x, :rows] = jnp.dot(
                    x_ref[:rows], w_ref[j], preferred_element_type=F32
                ).astype(BF)
                if rows < prefill:
                    out[j % n_x, rows:] = jnp.zeros((prefill - rows, width), BF)

        @pl.when(live > short)
        def _():
            products(prefill)

        @pl.when(live <= short)
        def _():
            products(short)

    out = jax.ShapeDtypeStruct((n_x, count * prefill, width), BF)
    block = pl.BlockSpec((n_x, prefill, width), lambda i, p: (0, i, 0))
    return pl.pallas_call(
        body,
        out_shape=(out, out),
        grid_spec=pltpu.PrefetchScalarGridSpec(
            num_scalar_prefetch=1,
            grid=(count,),
            in_specs=[
                pl.BlockSpec((prefill, features), lambda i, p: (first + i, 0)),
                pl.BlockSpec((n_t, features, width), lambda i, p: (0, 0, 0)),
            ]
            + [ANY] * n_after,
            out_specs=(block, block),
        ),
        compiler_params=params(),
        cost_estimate=SMALL,
        name="base_products",
    )(lengths, hidden, weight, *after)


def pair_sum(one, other, index, after):
    _, rows, width = one.shape
    block = rows // 4
    n_after = len(after)

    def body(a_ref, b_ref, *rest):
        rest[n_after][...] = (a_ref[0].astype(F32) + b_ref[0].astype(F32)).astype(BF)

    spec = pl.BlockSpec((1, block, width), lambda i: (index, i, 0))
    return pl.pallas_call(
        body,
        out_shape=jax.ShapeDtypeStruct((rows, width), BF),
        grid=(rows // block,),
        in_specs=[spec, spec] + [ANY] * n_after,
        out_specs=pl.BlockSpec((block, width), lambda i: (i, 0)),
        compiler_params=params(),
        cost_estimate=SMALL,
        name="pair_sum",
    )(one, other, *after)


def rank_products(plan, hidden, maps, first, count, prefill):
    features = hidden.shape[1]
    ranks = maps[0].shape[2]
    half = prefill // 2

    def body(plan_ref, x_ref, *rest):
        refs, rest = rest[: len(maps)], rest[len(maps) :]
        mine_ref, other_ref, held, whole, sems = rest
        step = pl.program_id(0)
        down = pl.ds(0, features)

        @pl.when(step == 0)
        def _():
            for i in range(count):
                fetch(
                    refs, plan_ref[SOURCE, first + i], held.at[i], sems.at[i], down
                )

        pltpu.make_async_copy(
            refs[0].at[0, down], held.at[step], sems.at[step]
        ).wait()
        whole[...] = jnp.dot(x_ref[...], held[step], preferred_element_type=F32)
        core = plan_ref[MISC, CORE]
        at = pl.multiple_of(core * half, half)
        mine_ref[...] = whole[pl.ds(at, half)].astype(BF)
        at = pl.multiple_of((1 - core) * half, half)
        other_ref[...] = whole[pl.ds(at, half)].astype(BF)

    out = jax.ShapeDtypeStruct((count * half, ranks), BF)
    block = pl.BlockSpec((half, ranks), lambda i, p: (i, 0))
    return pl.pallas_call(
        body,
        out_shape=(out, out),
        grid_spec=pltpu.PrefetchScalarGridSpec(
            num_scalar_prefetch=1,
            grid=(count,),
            in_specs=[
                pl.BlockSpec((prefill, features), lambda i, p: (p[ORDER, first + i], 0))
            ]
            + [ANY] * len(maps),
            out_specs=(block, block),
            scratch_shapes=[
                pltpu.VMEM((count, features, ranks), BF),
                pltpu.VMEM((prefill, ranks), F32),
                pltpu.SemaphoreType.DMA((count,)),
            ],
        ),
        compiler_params=params(),
        cost_estimate=SMALL,
        name="rank_products",
    )(plan, hidden, *maps)


def finish(plan, lengths, bases, ranks, maps, prefill, depth, columns):
    requests = lengths.shape[0]
    features = maps[0].shape[1] - 2 * depth * columns // (2 * depth)
    tiles = columns // maps[0].shape[2]
    features = maps[0].shape[1] - tiles * 2 * depth
    half = prefill // 2
    n_base = [len(pieces) for _, _, pieces in bases]
    n_rank, n_map = 2 * len(ranks), len(maps)

    def body(plan_ref, length_ref, *rest):
        base_refs = []
        for n in n_base:
            base_refs.append(rest[:n])
            rest = rest[n:]
        rank_refs, rest = rest[:n_rank], rest[n_rank:]
        map_refs, rest = rest[:n_map], rest[n_map:]
        o_ref, held, sems = rest
        step = pl.program_id(0)
        up_rows = pl.ds(features, tiles * 2 * depth)

        @pl.when(step == 0)
        def _():
            for i in range(requests):
                place = plan_ref[PLACE, i]
                fetch(
                    map_refs, plan_ref[SOURCE, place], held.at[i], sems.at[i], up_rows
                )

        pltpu.make_async_copy(
            map_refs[0].at[0, up_rows], held.at[step], sems.at[step]
        ).wait()
        place = plan_ref[PLACE, step]
        core = plan_ref[MISC, CORE]
        live = length_ref[step]
        up = jnp.concatenate(
            [held[step, j * 2 * depth : (j + 1) * 2 * depth] for j in range(tiles)], 1
        )
        mix_row = lax.broadcasted_iota(jnp.int32, (2 * half, 2 * half), 0)
        mix_column = lax.broadcasted_iota(jnp.int32, (2 * half, 2 * half), 1)
        mix = mix_column == mix_row // 2 + half * (mix_row % 2)
        mix = mix.astype(F32).astype(BF)
        twice_row = lax.broadcasted_iota(jnp.int32, (2 * half, half), 0)
        twice_column = lax.broadcasted_iota(jnp.int32, (2 * half, half), 1)
        twice = (twice_column == twice_row // 2).astype(F32).astype(BF)
        lane = lax.broadcasted_iota(jnp.int32, (2 * half, 2 * depth), 1)
        side = lax.broadcasted_iota(jnp.int32, (2 * half, 2 * depth), 0) % 2
        own_side = lane // depth == side
        token = lax.broadcasted_iota(jnp.int32, (2 * half, columns), 0) // 2

        def rows_for(refs, b):
            rows = slice(b * half, (b + 1) * half)
            total = jnp.zeros((2 * half, columns), F32)
            for ref in refs:
                piece = ref[0, rows] if len(ref.shape) == 3 else ref[rows]
                piece = jnp.concatenate([piece[:, :columns], piece[:, columns:]], 0)
                total += jnp.dot(mix, piece, preferred_element_type=F32)
            rank = None
            below = 0
            for k, (_, count) in enumerate(ranks):
                pair = rank_refs[2 * k : 2 * k + 2]
                value = jnp.where(core == b, pair[0][...], pair[1][...])
                rank = value if k == 0 else jnp.where(place >= below, value, rank)
                below += count
            rank = jnp.dot(twice, rank, preferred_element_type=F32)
            rank = jnp.where(own_side, rank, 0.0).astype(BF)
            total += jnp.dot(rank, up, preferred_element_type=F32)
            total = jnp.where(token + b * half < live, total, 0.0)
            o_ref[rows] = total.astype(BF).reshape(half, 2, columns)

        def nothing(b):
            o_ref[b * half : (b + 1) * half] = jnp.zeros((half, 2, columns), BF)

        for (first, count, _), refs in zip(bases, base_refs):

            @pl.when((step >= first) & (step < first + count))
            def _():
                rows_for(refs, 0)

                @pl.when(live > half)
                def _():
                    rows_for(refs, 1)

                @pl.when(live <= half)
                def _():
                    nothing(1)

    operands, specs = [], []
    for first, count, pieces in bases:

        def at(i, first=first, count=count):
            return jnp.clip(i - first, 0, count - 1)

        for a in pieces:
            operands.append(a)
            if a.ndim == 3:
                specs.append(
                    pl.BlockSpec(
                        (1, prefill, 2 * columns), lambda i, p, n, at=at: (0, at(i), 0)
                    )
                )
            else:
                specs.append(
                    pl.BlockSpec((prefill, 2 * columns), lambda i, p, n, at=at: (at(i), 0))
                )
    below = 0
    for pair, count in ranks:

        def which(i, p, n, below=below, count=count):
            return (jnp.clip(p[PLACE, i] - below, 0, count - 1), 0)

        for a in pair:
            operands.append(a)
            specs.append(pl.BlockSpec((half, 2 * depth), which))
        below += count
    operands += maps
    specs += [ANY] * n_map
    return pl.pallas_call(
        body,
        out_shape=jax.ShapeDtypeStruct((requests * prefill, 2, columns), BF),
        grid_spec=pltpu.PrefetchScalarGridSpec(
            num_scalar_prefetch=2,
            grid=(requests,),
            in_specs=specs,
            out_specs=pl.BlockSpec((prefill, 2, columns), lambda i, p, n: (i, 0, 0)),
            scratch_shapes=[
                pltpu.VMEM((requests, tiles * 2 * depth, maps[0].shape[2]), BF),
                pltpu.SemaphoreType.DMA((requests,)),
            ],
        ),
        compiler_params=params(),
        cost_estimate=SMALL,
        name="finish",
    )(plan, lengths, *operands)


def solution(mesh):
    n_z, n_t = mesh.shape["adapter"], mesh.shape["tensor"]
    n_x = n_t // 2

    def core_swap(a):
        return lax.ppermute(a, "tensor", [(t, t ^ 1) for t in range(n_t)])

    def chip_shift(a, k):
        return lax.ppermute(
            a,
            "tensor",
            [(2 * x + c, 2 * ((x + k) % n_x) + c) for x in range(n_x) for c in (0, 1)],
        )

    def leftward(a):
        return lax.ppermute(a, "adapter", [(z, z - 1) for z in range(1, n_z)])

    def rightward(a):
        return lax.ppermute(a, "adapter", [(z - 1, z) for z in range(1, n_z)])

    def per_device(hidden, weight, down, up, table, adapters, lengths):
        requests = adapters.shape[0]
        prefill = hidden.shape[0] // requests
        stored = down.shape[0]
        depth, columns = up.shape[2:]
        listed = n_z == 4 and requests == 12 and stored == 3
        limit = (n_z - 1) * stored
        g, z, t = (lax.axis_index(a) for a in ("group", "adapter", "tensor"))
        core = t % 2

        own = list(pack_maps(down, up))
        lefts, rights = [], []
        if listed:
            for i in range(2):
                lefts.append(leftward(own[i]))
                rights.append(rightward(own[i]))

        dest = jnp.arange(n_t, dtype=jnp.int32)
        away = (dest // 2 - t // 2 + n_x) % n_x
        slots = jnp.where(dest % 2 == core, n_x + away, away)
        split = split_weight(weight, slots)

        bases = []

        def base(chunk, after):
            first, count = sum(BASE_CHUNKS[:chunk]), BASE_CHUNKS[chunk]
            send, keep = base_products(
                lengths, hidden, split, first, count, prefill, after
            )
            got = core_swap(send)
            bases.append((first, count, [keep, got]))

        def across(chunk, after):
            keep, got = bases[chunk][2]
            for k in range(1, n_x):
                pair = pair_sum(keep, got, k, after)
                bases[chunk][2].append(chip_shift(pair, k))
            return pair

        base(0, ())
        pair = across(0, ())

        hit = adapters[:, None] == jnp.arange(table.shape[0], dtype=jnp.int32)[None, :]
        rows = jnp.sum(jnp.where(hit, table[None, :], 0), axis=1)
        if listed:
            rows = lax.all_gather(rows, ("group", "adapter"))
            here = jnp.stack([g * n_z + z, core])
            plan = plan_moves(rows, here, n_z, stored, limit)

            def pass_on(i):
                return choose_maps(plan, i, own, lefts[: i - 1], rights[: i - 1])

            def step(i):
                a, b = pass_on(i)
                lefts.append(leftward(a))
                rights.append(rightward(b))
                return a

            def maybe(i):
                def go():
                    a, b = pass_on(i)
                    return leftward(a), rightward(b)

                def stay():
                    return jnp.zeros_like(own[0]), jnp.zeros_like(own[0])

                a, b = lax.cond(plan[MISC, STEPS] > i, go, stay)
                lefts.append(a)
                rights.append(b)

            def maps():
                fill = [own[0]] * (limit - len(lefts))
                return own + lefts + fill + rights + fill

        else:
            everything = lax.all_gather(
                jnp.concatenate(own, 0), "adapter", axis=0, tiled=True
            )
            lane = jnp.arange(128, dtype=jnp.int32)
            source = jnp.zeros((128,), jnp.int32).at[:requests].set(rows)
            misc = jnp.where(lane == CORE, core, 0)
            plan = jnp.stack([lane, lane, lane, source, lane, misc, lane, lane])

            def step(i):
                return everything

            def maybe(i):
                pass

            def maps():
                return [everything]

        ranks = []

        def rank(chunk):
            first, count = sum(RANK_CHUNKS[:chunk]), RANK_CHUNKS[chunk]
            mine, other = rank_products(plan, hidden, maps(), first, count, prefill)
            pair = mine.astype(F32) + core_swap(other).astype(F32)
            pair = pair.astype(BF)
            total = pair.astype(F32)
            for k in range(1, n_x):
                total += chip_shift(pair, k).astype(F32)
            total = total.astype(BF)
            ranks.append(((total, core_swap(total)), count))

        step(2)
        last = step(3)
        base(1, (last, pair))
        pair = across(1, ())
        rank(0)
        last = step(4)
        base(2, (last, pair))
        last = step(5)
        across(2, (last,))
        rank(1)
        for i in range(6, limit):
            maybe(i)
        rank(2)
        return finish(plan, lengths, bases, ranks, maps(), prefill, depth, columns)

    return jax.shard_map(
        per_device,
        mesh=mesh,
        in_specs=(
            P(("group", "adapter"), "tensor"),
            P("tensor", None, None),
            P(("group", "adapter"), "tensor", None),
            P(("group", "adapter"), None, None, "tensor"),
            P("group"),
            P(("group", "adapter")),
            P(("group", "adapter")),
        ),
        out_specs=P(("group", "adapter"), None, "tensor"),
        check_vma=False,
    )
```

```python
import jax
import jax.numpy as jnp
from jax import lax
from jax.experimental import pallas as pl
from jax.experimental.pallas import tpu as pltpu
from jax.sharding import PartitionSpec as P

BF = jnp.bfloat16
F32 = jnp.float32
BASE_CHUNKS = (2, 2, 2, 2, 2, 2)
RANK_CHUNKS = 4
SMEM = pltpu.SMEM
ANY = pl.BlockSpec(memory_space=pl.ANY)


def cost(flops, moved):
    return pl.CostEstimate(
        flops=int(flops * 1), bytes_accessed=int(moved * 1), transcendentals=0
    )


ORDER, SOURCE, ROW, LENGTH = range(4)


def params(mib=60):
    return pltpu.CompilerParams(vmem_limit_bytes=mib * 1024 * 1024)


def plan_requests(table, adapters, lengths, here, n_z, stored):
    requests, known = adapters.shape[0], table.shape[0]
    shape = (requests, 128)

    def body(table_ref, adapter_ref, length_ref, here_ref, plan_ref):
        me = here_ref[0]
        request = lax.broadcasted_iota(jnp.int32, shape, 0)
        lane = lax.broadcasted_iota(jnp.int32, shape, 1)
        diagonal = request == lane

        def wide(ref, n):
            return jnp.pad(ref[...], ((0, 0), (0, 128 - n)))

        def down(a):
            return jnp.sum(jnp.where(diagonal, a, 0), axis=1, keepdims=True)

        def across(a):
            return jnp.sum(jnp.where(diagonal, a, 0), axis=0, keepdims=True)

        hit = (down(wide(adapter_ref, requests)) == lane) & (lane < known)
        slot = jnp.sum(jnp.where(hit, wide(table_ref, known), 0), 1, keepdims=True)
        owner = jnp.zeros_like(slot)
        for z in range(1, n_z):
            owner += jnp.where(slot >= z * stored, 1, 0)
        source = jnp.where(owner >= me, owner - me, n_z - 1 + me - owner)
        key = jnp.abs(owner - me) * 128 + request[:, :1]
        before = (across(key) < key) & (lane < requests)
        place = jnp.sum(jnp.where(before, 1, 0), axis=1, keepdims=True)
        at = place == lane

        def placed(a):
            return jnp.sum(jnp.where(at, a, 0), axis=0, keepdims=True)

        plan_ref[ORDER : ORDER + 1] = placed(request)
        plan_ref[SOURCE : SOURCE + 1] = placed(source)
        plan_ref[ROW : ROW + 1] = placed(slot - owner * stored)
        plan_ref[LENGTH : LENGTH + 1] = placed(down(wide(length_ref, requests)))

    vmem = pl.BlockSpec(memory_space=pltpu.VMEM)
    return pl.pallas_call(
        body,
        out_shape=jax.ShapeDtypeStruct((8, 128), jnp.int32),
        in_specs=[vmem, vmem, vmem, pl.BlockSpec(memory_space=SMEM)],
        out_specs=vmem,
        cost_estimate=cost(0, 1 << 20),
        name="plan_requests",
    )(table[None, :], adapters[None, :], lengths[None, :], here)


def split_weight(plan, slots, hidden, weight, count, prefill):
    features, _, columns = weight.shape
    n_t = slots.shape[0]
    n_x = n_t // 2
    width = columns // n_t
    rows, half = 256, 128
    steps = features // rows

    def body(plan_ref, slot_ref, *rest):
        x_refs, (w_ref, o_ref, send_ref, keep_ref, total) = rest[:count], rest[count:]
        step = pl.program_id(0)
        out_row = lax.broadcasted_iota(jnp.int32, (2 * half, 2 * half), 0)
        in_row = lax.broadcasted_iota(jnp.int32, (2 * half, 2 * half), 1)
        pick = in_row == 2 * (out_row % half) + out_row // half
        pick = pick.astype(F32).astype(BF)
        for b in range(rows // half):
            mixed = w_ref[b * half : (b + 1) * half].reshape(2 * half, columns)
            apart = jnp.dot(pick, mixed, preferred_element_type=F32).astype(BF)
            for t in range(n_t):
                for s in range(2):
                    o_ref[
                        slot_ref[t],
                        b * half : (b + 1) * half,
                        s * width : (s + 1) * width,
                    ] = apart[s * half : (s + 1) * half, t * width : (t + 1) * width]

        @pl.when(step == 0)
        def _():
            total[...] = jnp.zeros_like(total)

        for r in range(count):
            for j in range(n_t):
                total[j, r * prefill : (r + 1) * prefill] += jnp.dot(
                    x_refs[r][...], o_ref[j], preferred_element_type=F32
                )

        @pl.when(step == steps - 1)
        def _():
            for j in range(n_t):
                out = send_ref if j < n_x else keep_ref
                out[j % n_x] = total[j].astype(BF)

    out = jax.ShapeDtypeStruct((n_x, count * prefill, 2 * width), BF)
    block = pl.BlockSpec((n_x, count * prefill, 2 * width), lambda i, p, s: (0, 0, 0))
    return pl.pallas_call(
        body,
        out_shape=(jax.ShapeDtypeStruct((n_t, features, 2 * width), BF), out, out),
        grid_spec=pltpu.PrefetchScalarGridSpec(
            num_scalar_prefetch=2,
            grid=(steps,),
            in_specs=[
                pl.BlockSpec((prefill, rows), lambda i, p, s, r=r: (p[ORDER, r], i))
                for r in range(count)
            ]
            + [pl.BlockSpec((rows, 2, columns), lambda i, p, s: (i, 0, 0))],
            out_specs=(
                pl.BlockSpec((n_t, rows, 2 * width), lambda i, p, s: (0, i, 0)),
                block,
                block,
            ),
            scratch_shapes=[pltpu.VMEM((n_t, count * prefill, 2 * width), F32)],
        ),
        compiler_params=params(),
        cost_estimate=cost(2 * count * prefill * features * 2 * columns, 8 * features * columns),
        name="split_weight",
    )(plan, slots, *[hidden] * count, weight)


def base_products(plan, hidden, weight, first, count, prefill, after):
    n_t, features, width = weight.shape
    n_x = n_t // 2
    short = prefill // 2
    n_after = len(after)

    def body(plan_ref, x_ref, w_ref, *rest):
        send_ref, keep_ref = rest[n_after:]
        live = plan_ref[LENGTH, first + pl.program_id(0)]

        def products(rows):
            for j in range(n_t):
                out = send_ref if j < n_x else keep_ref
                out[j % n_x, :rows] = jnp.dot(
                    x_ref[:rows], w_ref[j], preferred_element_type=F32
                ).astype(BF)
                if rows < prefill:
                    out[j % n_x, rows:] = jnp.zeros((prefill - rows, width), BF)

        @pl.when(live > short)
        def _():
            products(prefill)

        @pl.when(live <= short)
        def _():
            products(short)

    out = jax.ShapeDtypeStruct((n_x, count * prefill, width), BF)
    block = pl.BlockSpec((n_x, prefill, width), lambda i, p: (0, i, 0))
    return pl.pallas_call(
        body,
        out_shape=(out, out),
        grid_spec=pltpu.PrefetchScalarGridSpec(
            num_scalar_prefetch=1,
            grid=(count,),
            in_specs=[
                pl.BlockSpec(
                    (prefill, features), lambda i, p: (p[ORDER, first + i], 0)
                ),
                pl.BlockSpec((n_t, features, width), lambda i, p: (0, 0, 0)),
            ]
            + [ANY] * n_after,
            out_specs=(block, block),
        ),
        compiler_params=params(),
        cost_estimate=cost(2 * count * prefill * features * width * n_t, 2 * n_t * features * width),
        name="base_products",
    )(plan, hidden, weight, *after)


def pair_sum(one, other, index, after):
    _, rows, width = one.shape
    block = rows // 2

    n_after = len(after)

    def body(a_ref, b_ref, *rest):
        rest[n_after][...] = (a_ref[0].astype(F32) + b_ref[0].astype(F32)).astype(BF)

    spec = pl.BlockSpec((1, block, width), lambda i: (index, i, 0))
    return pl.pallas_call(
        body,
        out_shape=jax.ShapeDtypeStruct((rows, width), BF),
        grid=(rows // block,),
        in_specs=[spec, spec] + [ANY] * n_after,
        out_specs=pl.BlockSpec((block, width), lambda i: (i, 0)),
        compiler_params=params(),
        cost_estimate=cost(rows * width, 6 * rows * width),
        name="pair_sum",
    )(one, other, *after)


def copy_after(a, after):
    def body(a_ref, *rest):
        rest[-1][...] = a_ref[...]

    vmem = pl.BlockSpec(memory_space=pltpu.VMEM)
    return pl.pallas_call(
        body,
        out_shape=jax.ShapeDtypeStruct(a.shape, a.dtype),
        in_specs=[vmem] + [ANY] * len(after),
        out_specs=vmem,
        compiler_params=params(),
        cost_estimate=cost(0, 4 * a.size),
        name="copy_after",
    )(a, *after)


def fetch(refs, source, row, target, sem):
    for k, ref in refs:

        @pl.when(source == k)
        def _():
            pltpu.make_async_copy(ref.at[row], target, sem).start()


def rank_products(plan, hidden, maps, first, count, prefill, after):
    sources = list(maps)
    _, features, ranks = maps[sources[0]].shape
    n_map, n_after = len(maps), len(after)

    def body(plan_ref, x_ref, *rest):
        refs = list(zip(sources, rest[:n_map]))
        o_ref, held, sems = rest[n_map + n_after :]
        step = pl.program_id(0)

        @pl.when(step == 0)
        def _():
            for i in range(count):
                fetch(
                    refs,
                    plan_ref[SOURCE, first + i],
                    plan_ref[ROW, first + i],
                    held.at[i],
                    sems.at[i],
                )

        pltpu.make_async_copy(rest[0].at[0], held.at[step], sems.at[step]).wait()
        o_ref[...] = jnp.dot(
            x_ref[...], held[step], preferred_element_type=F32
        ).astype(BF)

    return pl.pallas_call(
        body,
        out_shape=jax.ShapeDtypeStruct((count * prefill, ranks), BF),
        grid_spec=pltpu.PrefetchScalarGridSpec(
            num_scalar_prefetch=1,
            grid=(count,),
            in_specs=[
                pl.BlockSpec((prefill, features), lambda i, p: (p[ORDER, first + i], 0))
            ]
            + [ANY] * (n_map + n_after),
            out_specs=pl.BlockSpec((prefill, ranks), lambda i, p: (i, 0)),
            scratch_shapes=[
                pltpu.VMEM((count, features, ranks), BF),
                pltpu.SemaphoreType.DMA((count,)),
            ],
        ),
        compiler_params=params(),
        cost_estimate=cost(2 * count * prefill * features * ranks, 2 * count * features * (prefill + ranks)),
        name="rank_products",
    )(plan, hidden, *maps.values(), *after)


def finish(plan, bases, ranks, maps, before, first, count, prefill, shape):
    sources = list(maps)
    _, _, depth, columns = maps[sources[0]].shape
    half = prefill // 2
    n_map = len(maps)

    def body(plan_ref, *rest):
        base_refs, rank_refs = [], []
        for refs, pieces in ((base_refs, bases), (rank_refs, ranks)):
            for _, _, arrays in pieces:
                refs.append(rest[: len(arrays)])
                rest = rest[len(arrays) :]
        map_refs = list(zip(sources, rest[:n_map]))
        o_ref, held, sems = rest[-3:]
        step = pl.program_id(0)
        at = first + step

        @pl.when(step == 0)
        def _():
            for i in range(count):
                fetch(
                    map_refs,
                    plan_ref[SOURCE, first + i],
                    plan_ref[ROW, first + i],
                    held.at[i],
                    sems.at[i],
                )

        pltpu.make_async_copy(
            map_refs[0][1].at[0], held.at[step], sems.at[step]
        ).wait()
        live = plan_ref[LENGTH, at]
        up = held[step].reshape(2 * depth, columns)
        mix_row = lax.broadcasted_iota(jnp.int32, (2 * half, 2 * half), 0)
        mix_column = lax.broadcasted_iota(jnp.int32, (2 * half, 2 * half), 1)
        mix = mix_column == mix_row // 2 + half * (mix_row % 2)
        mix = mix.astype(F32).astype(BF)
        twice_row = lax.broadcasted_iota(jnp.int32, (2 * half, half), 0)
        twice_column = lax.broadcasted_iota(jnp.int32, (2 * half, half), 1)
        twice = (twice_column == twice_row // 2).astype(F32).astype(BF)
        lane = lax.broadcasted_iota(jnp.int32, (2 * half, 2 * depth), 1)
        side = lax.broadcasted_iota(jnp.int32, (2 * half, 2 * depth), 0) % 2
        own_side = lane // depth == side
        token = lax.broadcasted_iota(jnp.int32, (2 * half, columns), 0) // 2

        def rows_for(refs, b):
            rows = slice(b * half, (b + 1) * half)
            total = jnp.zeros((2 * half, columns), F32)
            for ref in refs:
                piece = ref[0, rows] if len(ref.shape) == 3 else ref[rows]
                piece = jnp.concatenate([piece[:, :columns], piece[:, columns:]], 0)
                total += jnp.dot(mix, piece, preferred_element_type=F32)
            rank = None
            for (start, _, _), pieces in zip(ranks, rank_refs):
                value = pieces[0][rows].astype(F32)
                for ref in pieces[1:]:
                    value += ref[rows].astype(F32)
                rank = value if rank is None else jnp.where(at >= start, value, rank)
            rank = jnp.dot(twice, rank.astype(BF), preferred_element_type=F32)
            rank = jnp.where(own_side, rank, 0.0).astype(BF)
            total += jnp.dot(rank, up, preferred_element_type=F32)
            total = jnp.where(token + b * half < live, total, 0.0)
            o_ref[rows] = total.astype(BF).reshape(half, 2, columns)

        for (start, n, _), refs in zip(bases, base_refs):

            @pl.when((at >= start) & (at < start + n))
            def _():
                rows_for(refs, 0)

                @pl.when(live > half)
                def _():
                    rows_for(refs, 1)

                @pl.when(live <= half)
                def _():
                    o_ref[half:] = jnp.zeros((half, 2, columns), BF)

    operands, specs = [plan], []
    for start, n, pieces in bases + ranks:

        def block(i, p, start=start, n=n):
            return jnp.clip(first + i - start, 0, n - 1)

        for a in pieces:
            operands.append(a)
            if a.ndim == 3:
                specs.append(
                    pl.BlockSpec(
                        (1, prefill, a.shape[2]),
                        lambda i, p, block=block: (0, block(i, p), 0),
                    )
                )
            else:
                specs.append(
                    pl.BlockSpec(
                        (prefill, a.shape[1]),
                        lambda i, p, block=block: (block(i, p), 0),
                    )
                )
    operands += maps.values()
    specs += [ANY] * n_map
    aliases = {}
    if before is not None:
        aliases = {len(operands): 0}
        operands.append(before)
        specs.append(ANY)
    return pl.pallas_call(
        body,
        out_shape=jax.ShapeDtypeStruct(shape, BF),
        grid_spec=pltpu.PrefetchScalarGridSpec(
            num_scalar_prefetch=1,
            grid=(count,),
            in_specs=specs,
            out_specs=pl.BlockSpec(
                (prefill, 2, columns), lambda i, p: (p[ORDER, first + i], 0, 0)
            ),
            scratch_shapes=[
                pltpu.VMEM((count, 2, depth, columns), BF),
                pltpu.SemaphoreType.DMA((count,)),
            ],
        ),
        input_output_aliases=aliases,
        compiler_params=params(),
        cost_estimate=cost(12 * count * prefill * prefill * 2 * columns, 20 * count * prefill * columns),
        name="finish",
    )(*operands)


def solution(mesh):
    n_z, n_t = mesh.shape["adapter"], mesh.shape["tensor"]
    n_x = n_t // 2

    def core_swap(a):
        return lax.ppermute(a, "tensor", [(t, t ^ 1) for t in range(n_t)])

    def chip_shift(a, k):
        return lax.ppermute(
            a,
            "tensor",
            [(2 * x + c, 2 * ((x + k) % n_x) + c) for x in range(n_x) for c in (0, 1)],
        )

    def leftward(a, hops=1):
        return lax.ppermute(a, "adapter", [(z, z - hops) for z in range(hops, n_z)])

    def rightward(a, hops=1):
        return lax.ppermute(a, "adapter", [(z - hops, z) for z in range(hops, n_z)])

    def per_device(hidden, weight, down, up, table, adapters, lengths):
        requests = adapters.shape[0]
        prefill = hidden.shape[0] // requests
        stored = down.shape[0]
        columns = up.shape[3]
        by_distance = n_z == RANK_CHUNKS
        z, t = lax.axis_index("adapter"), lax.axis_index("tensor")
        plan = plan_requests(
            table, adapters, lengths, jnp.reshape(z, (1,)), n_z, stored
        )

        downs = {0: down}
        for hops in range(1, n_z):
            left, right = downs[hops - 1], downs[0 if hops == 1 else n_z + hops - 2]
            downs[hops] = leftward(left)
            downs[n_z - 1 + hops] = rightward(right)

        def within(maps, hops):
            keys = range(hops + 1), range(n_z, n_z + hops)
            return {k: maps[k] for part in keys for k in part}

        dest = jnp.arange(n_t, dtype=jnp.int32)
        away = (dest // 2 - t // 2 + n_x) % n_x
        slots = jnp.where(dest % 2 == t % 2, n_x + away, away)

        bases, pairs = [], []
        waiting = []

        def send_on():
            first, count, keep, got = waiting.pop(0)
            pieces = [keep, got]
            for k in range(1, n_x):
                pairs.append(pair_sum(keep, got, k, waiting[0][2:3] if waiting else []))
                pieces.append(chip_shift(pairs[-1], k))
            bases.append((first, count, pieces))

        split, send, keep = split_weight(
            plan, slots, hidden, weight, BASE_CHUNKS[0], prefill
        )
        waiting.append((0, BASE_CHUNKS[0], keep, core_swap(send)))

        near = [downs[1], downs[n_z]]
        middle = [downs[2], downs[n_z + 1]]
        for chunk in range(1, len(BASE_CHUNKS)):
            first, count = sum(BASE_CHUNKS[:chunk]), BASE_CHUNKS[chunk]
            after = pairs[-1:]
            if chunk == 3:
                after = after + near
            if chunk >= 3:
                after = after + [bases[chunk - 3][2][-1]]
            send, keep = base_products(
                plan, hidden, split, first, count, prefill, after
            )
            waiting.append((first, count, keep, core_swap(send)))
            send_on()

        ups = {0: up}
        late_up = copy_after(up, middle)
        for hops in range(1, n_z):
            ups[hops] = leftward(late_up, hops)
            ups[n_z - 1 + hops] = rightward(late_up, hops)

        ranks = []

        def rank(chunk, after):
            count = requests // RANK_CHUNKS
            hops = chunk if by_distance else n_z - 1
            part = rank_products(
                plan, hidden, within(downs, hops), chunk * count, count, prefill, after
            )
            pair = (part.astype(F32) + core_swap(part).astype(F32)).astype(BF)
            pieces = [pair] + [chip_shift(pair, k) for k in range(1, n_x)]
            ranks.append((chunk * count, count, pieces))

        rank(0, [pairs[-1]])
        send_on()
        rank(1, [pairs[-1]])
        rank(2, [ranks[1][2][0]] + [b[2][-1] for b in bases[2:4]])
        shape = (requests * prefill, 2, columns)
        early = 3 * requests // RANK_CHUNKS
        out = finish(
            plan,
            bases,
            ranks[:3],
            within(ups, 2 if by_distance else n_z - 1),
            None,
            0,
            early,
            prefill,
            shape,
        )
        rank(3, [])
        return finish(
            plan,
            bases[-2:],
            ranks[3:],
            within(ups, n_z - 1),
            out,
            early,
            requests - early,
            prefill,
            shape,
        )

    return jax.shard_map(
        per_device,
        mesh=mesh,
        in_specs=(
            P(("group", "adapter"), "tensor"),
            P("tensor", None, None),
            P(("group", "adapter"), "tensor", None),
            P(("group", "adapter"), None, None, "tensor"),
            P("group"),
            P(("group", "adapter")),
            P(("group", "adapter")),
        ),
        out_specs=P(("group", "adapter"), None, "tensor"),
        check_vma=False,
    )
```

```python
import jax
import jax.numpy as jnp
from jax import lax
from jax.experimental import pallas as pl
from jax.experimental.pallas import tpu as pltpu
from jax.sharding import PartitionSpec as P

BF = jnp.bfloat16
F32 = jnp.float32
BASE_CHUNKS = (3, 4, 5)
RANK_CHUNKS = 4
SMEM = pltpu.SMEM
ANY = pl.BlockSpec(memory_space=pl.ANY)


def cost(flops, moved):
    return pl.CostEstimate(
        flops=int(flops * 0.01), bytes_accessed=int(moved * 0.01), transcendentals=0
    )


ORDER, SOURCE, ROW, LENGTH = range(4)


def params(mib=60):
    return pltpu.CompilerParams(vmem_limit_bytes=mib * 1024 * 1024)


def plan_requests(table, adapters, lengths, here, n_z, stored):
    requests, known = adapters.shape[0], table.shape[0]
    shape = (requests, 128)

    def body(table_ref, adapter_ref, length_ref, here_ref, plan_ref):
        me = here_ref[0]
        request = lax.broadcasted_iota(jnp.int32, shape, 0)
        lane = lax.broadcasted_iota(jnp.int32, shape, 1)
        diagonal = request == lane

        def wide(ref, n):
            return jnp.pad(ref[...], ((0, 0), (0, 128 - n)))

        def down(a):
            return jnp.sum(jnp.where(diagonal, a, 0), axis=1, keepdims=True)

        def across(a):
            return jnp.sum(jnp.where(diagonal, a, 0), axis=0, keepdims=True)

        hit = (down(wide(adapter_ref, requests)) == lane) & (lane < known)
        slot = jnp.sum(jnp.where(hit, wide(table_ref, known), 0), 1, keepdims=True)
        owner = jnp.zeros_like(slot)
        for z in range(1, n_z):
            owner += jnp.where(slot >= z * stored, 1, 0)
        source = jnp.where(owner >= me, owner - me, n_z - 1 + me - owner)
        key = jnp.abs(owner - me) * 128 + request[:, :1]
        before = (across(key) < key) & (lane < requests)
        place = jnp.sum(jnp.where(before, 1, 0), axis=1, keepdims=True)
        at = place == lane

        def placed(a):
            return jnp.sum(jnp.where(at, a, 0), axis=0, keepdims=True)

        plan_ref[ORDER : ORDER + 1] = placed(request)
        plan_ref[SOURCE : SOURCE + 1] = placed(source)
        plan_ref[ROW : ROW + 1] = placed(slot - owner * stored)
        plan_ref[LENGTH : LENGTH + 1] = placed(down(wide(length_ref, requests)))

    vmem = pl.BlockSpec(memory_space=pltpu.VMEM)
    return pl.pallas_call(
        body,
        out_shape=jax.ShapeDtypeStruct((8, 128), jnp.int32),
        in_specs=[vmem, vmem, vmem, pl.BlockSpec(memory_space=SMEM)],
        out_specs=vmem,
        cost_estimate=cost(0, 1 << 20),
        name="plan_requests",
    )(table[None, :], adapters[None, :], lengths[None, :], here)


def split_weight(plan, slots, hidden, weight, count, prefill):
    features, _, columns = weight.shape
    n_t = slots.shape[0]
    n_x = n_t // 2
    width = columns // n_t
    rows, half = 512, 128
    steps = features // rows

    def body(plan_ref, slot_ref, *rest):
        x_refs, (w_ref, o_ref, *send_refs, keep_ref, total) = rest[:count], rest[count:]
        step = pl.program_id(0)
        out_row = lax.broadcasted_iota(jnp.int32, (2 * half, 2 * half), 0)
        in_row = lax.broadcasted_iota(jnp.int32, (2 * half, 2 * half), 1)
        pick = in_row == 2 * (out_row % half) + out_row // half
        pick = pick.astype(F32).astype(BF)
        for b in range(rows // half):
            mixed = w_ref[b * half : (b + 1) * half].reshape(2 * half, columns)
            apart = jnp.dot(pick, mixed, preferred_element_type=F32).astype(BF)
            for t in range(n_t):
                for s in range(2):
                    o_ref[
                        slot_ref[t],
                        b * half : (b + 1) * half,
                        s * width : (s + 1) * width,
                    ] = apart[s * half : (s + 1) * half, t * width : (t + 1) * width]

        @pl.when(step == 0)
        def _():
            total[...] = jnp.zeros_like(total)

        for r in range(count):
            for j in range(n_t):
                total[j, r * prefill : (r + 1) * prefill] += jnp.dot(
                    x_refs[r][...], o_ref[j], preferred_element_type=F32
                )

        @pl.when(step == steps - 1)
        def _():
            for j in range(n_x):
                send_refs[j][...] = total[j].astype(BF)
                keep_ref[j] = total[n_x + j].astype(BF)

    part = (count * prefill, 2 * width)
    split, *sends, keep = pl.pallas_call(
        body,
        out_shape=(
            jax.ShapeDtypeStruct((n_t, features, 2 * width), BF),
            *[jax.ShapeDtypeStruct(part, BF)] * n_x,
            jax.ShapeDtypeStruct((n_x, *part), BF),
        ),
        grid_spec=pltpu.PrefetchScalarGridSpec(
            num_scalar_prefetch=2,
            grid=(steps,),
            in_specs=[
                pl.BlockSpec((prefill, rows), lambda i, p, s, r=r: (p[ORDER, r], i))
                for r in range(count)
            ]
            + [pl.BlockSpec((rows, 2, columns), lambda i, p, s: (i, 0, 0))],
            out_specs=(
                pl.BlockSpec((n_t, rows, 2 * width), lambda i, p, s: (0, i, 0)),
                *[pl.BlockSpec(part, lambda i, p, s: (0, 0))] * n_x,
                pl.BlockSpec((n_x, *part), lambda i, p, s: (0, 0, 0)),
            ),
            scratch_shapes=[pltpu.VMEM((n_t, count * prefill, 2 * width), F32)],
        ),
        compiler_params=params(),
        cost_estimate=cost(2 * count * prefill * features * 2 * columns, 8 * features * columns),
        name="split_weight",
    )(plan, slots, *[hidden] * count, weight)
    return split, sends, keep


def base_products(plan, hidden, weight, first, count, prefill, after):
    n_t, features, width = weight.shape
    n_x = n_t // 2
    short = prefill // 2
    n_after = len(after)

    def body(plan_ref, x_ref, *rest):
        w_refs = rest[:n_t]
        *send_refs, keep_ref = rest[n_t + n_after :]
        live = plan_ref[LENGTH, first + pl.program_id(0)]

        def products(rows):
            for j in range(n_t):
                out = send_refs[j] if j < n_x else keep_ref.at[j - n_x]
                out[:rows] = jnp.dot(
                    x_ref[:rows], w_refs[j][0], preferred_element_type=F32
                ).astype(BF)
                if rows < prefill:
                    out[rows:] = jnp.zeros((prefill - rows, width), BF)

        @pl.when(live > short)
        def _():
            products(prefill)

        @pl.when(live <= short)
        def _():
            products(short)

    part = (count * prefill, width)
    *sends, keep = pl.pallas_call(
        body,
        out_shape=(
            *[jax.ShapeDtypeStruct(part, BF)] * n_x,
            jax.ShapeDtypeStruct((n_x, *part), BF),
        ),
        grid_spec=pltpu.PrefetchScalarGridSpec(
            num_scalar_prefetch=1,
            grid=(count,),
            in_specs=[
                pl.BlockSpec(
                    (prefill, features), lambda i, p: (p[ORDER, first + i], 0)
                ),
            ]
            + [
                pl.BlockSpec((1, features, width), lambda i, p, j=j: (j, 0, 0))
                for j in range(n_t)
            ]
            + [ANY] * n_after,
            out_specs=(
                *[pl.BlockSpec((prefill, width), lambda i, p: (i, 0))] * n_x,
                pl.BlockSpec((n_x, prefill, width), lambda i, p: (0, i, 0)),
            ),
        ),
        compiler_params=params(),
        cost_estimate=cost(2 * count * prefill * features * width * n_t, 2 * n_t * features * width),
        name="base_products",
    )(plan, hidden, *[weight] * n_t, *after)
    return sends, keep


def pair_sum(one, other, index):
    _, rows, width = one.shape
    block = rows // 2

    def body(a_ref, b_ref, o_ref):
        o_ref[...] = (a_ref[0].astype(F32) + b_ref[...].astype(F32)).astype(BF)

    spec = pl.BlockSpec((block, width), lambda i: (i, 0))
    return pl.pallas_call(
        body,
        out_shape=jax.ShapeDtypeStruct((rows, width), BF),
        grid=(rows // block,),
        in_specs=[pl.BlockSpec((1, block, width), lambda i: (index, i, 0)), spec],
        out_specs=spec,
        compiler_params=params(),
        cost_estimate=cost(rows * width, 6 * rows * width),
        name="pair_sum",
    )(one, other)


def copy_after(a, after):
    def body(a_ref, *rest):
        rest[-1][...] = a_ref[...]

    vmem = pl.BlockSpec(memory_space=pltpu.VMEM)
    return pl.pallas_call(
        body,
        out_shape=jax.ShapeDtypeStruct(a.shape, a.dtype),
        in_specs=[vmem] + [ANY] * len(after),
        out_specs=vmem,
        compiler_params=params(),
        cost_estimate=cost(0, 4 * a.size),
        name="copy_after",
    )(a, *after)


def fetch(refs, source, row, target, sem):
    for codes, ref in refs:
        hit = source == codes[0]
        for code in codes[1:]:
            hit |= source == code

        @pl.when(hit)
        def _():
            pltpu.make_async_copy(ref.at[row], target, sem).start()


def rank_products(plan, hidden, maps, first, count, prefill, after):
    sources = list(maps)
    _, features, ranks = maps[sources[0]].shape
    n_map, n_after = len(maps), len(after)

    def body(plan_ref, x_ref, *rest):
        refs = list(zip(sources, rest[:n_map]))
        o_ref, rows, held, sems = rest[n_map + n_after :]
        copies = []
        for i in range(count):
            fetch(
                refs,
                plan_ref[SOURCE, first + i],
                plan_ref[ROW, first + i],
                held.at[i],
                sems.at[0, i],
            )
            at = pl.multiple_of(plan_ref[ORDER, first + i] * prefill, prefill)
            copies.append(
                pltpu.make_async_copy(
                    x_ref.at[pl.ds(at, prefill)], rows.at[i], sems.at[1, i]
                )
            )
            copies[-1].start()
        for i in range(count):
            pltpu.make_async_copy(rest[0].at[0], held.at[i], sems.at[0, i]).wait()
            copies[i].wait()
            o_ref[i * prefill : (i + 1) * prefill] = jnp.dot(
                rows[i], held[i], preferred_element_type=F32
            ).astype(BF)

    return pl.pallas_call(
        body,
        out_shape=jax.ShapeDtypeStruct((count * prefill, ranks), BF),
        grid_spec=pltpu.PrefetchScalarGridSpec(
            num_scalar_prefetch=1,
            grid=(),
            in_specs=[ANY] * (1 + n_map + n_after),
            out_specs=pl.BlockSpec(memory_space=pltpu.VMEM),
            scratch_shapes=[
                pltpu.VMEM((count, prefill, features), BF),
                pltpu.VMEM((count, features, ranks), BF),
                pltpu.SemaphoreType.DMA((2, count)),
            ],
        ),
        compiler_params=params(),
        cost_estimate=cost(2 * count * prefill * features * ranks, 2 * count * features * (prefill + ranks)),
        name="rank_products",
    )(plan, hidden, *maps.values(), *after)


def finish(plan, bases, ranks, maps, before, first, count, prefill, shape):
    sources = list(maps)
    _, _, depth, columns = maps[sources[0]].shape
    half = prefill // 2
    n_map = len(maps)
    n_base = max(len(pieces) for _, _, pieces in bases)
    n_rank = max(len(pieces) for _, _, pieces in ranks)

    def body(plan_ref, *rest):
        base_refs, rank_refs = [], []
        for refs, pieces in ((base_refs, bases), (rank_refs, ranks)):
            for start, n, arrays in pieces:
                refs.append((start, n, rest[: len(arrays)]))
                rest = rest[len(arrays) :]
        map_refs = list(zip(sources, rest[:n_map]))
        o_ref, ups, base_rows, rank_rows, out_rows, sems, out_sems = rest[-7:]

        def start_pieces(refs, at, rows, sem):
            copies = []
            for start, n, arrays in refs:
                if start <= at < start + n:
                    block = pl.ds((at - start) * prefill, prefill)
                    for k, ref in enumerate(arrays):
                        source = ref.at[0, block] if len(ref.shape) == 3 else ref.at[block]
                        copies.append(pltpu.make_async_copy(source, rows.at[k], sem.at[k]))
                        copies[-1].start()
            return copies

        copies = []
        for i in range(count):
            at = first + i
            copies.append(
                start_pieces(base_refs, at, base_rows.at[i], sems.at[i])
                + start_pieces(
                    rank_refs, at, rank_rows.at[i], sems.at[i, pl.ds(n_base, n_rank)]
                )
            )
            fetch(
                map_refs,
                plan_ref[SOURCE, at],
                plan_ref[ROW, at],
                ups.at[i],
                sems.at[i, n_base + n_rank],
            )

        mix_row = lax.broadcasted_iota(jnp.int32, (2 * half, 2 * half), 0)
        mix_column = lax.broadcasted_iota(jnp.int32, (2 * half, 2 * half), 1)
        mix = mix_column == mix_row // 2 + half * (mix_row % 2)
        mix = mix.astype(F32).astype(BF)
        twice_row = lax.broadcasted_iota(jnp.int32, (2 * half, half), 0)
        twice_column = lax.broadcasted_iota(jnp.int32, (2 * half, half), 1)
        twice = (twice_column == twice_row // 2).astype(F32).astype(BF)
        lane = lax.broadcasted_iota(jnp.int32, (2 * half, 2 * depth), 1)
        side = lax.broadcasted_iota(jnp.int32, (2 * half, 2 * depth), 0) % 2
        own_side = lane // depth == side
        token = lax.broadcasted_iota(jnp.int32, (2 * half, columns), 0) // 2

        def rows_for(i, pieces, live, b):
            rows = slice(b * half, (b + 1) * half)
            total = jnp.zeros((2 * half, columns), F32)
            for k in range(pieces):
                piece = base_rows[i, k, rows]
                piece = jnp.concatenate([piece[:, :columns], piece[:, columns:]], 0)
                total += jnp.dot(mix, piece, preferred_element_type=F32)
            rank = rank_rows[i, 0, rows].astype(F32)
            for k in range(1, n_rank):
                rank += rank_rows[i, k, rows].astype(F32)
            rank = jnp.dot(twice, rank.astype(BF), preferred_element_type=F32)
            rank = jnp.where(own_side, rank, 0.0).astype(BF)
            up = ups[i].reshape(2 * depth, columns)
            total += jnp.dot(rank, up, preferred_element_type=F32)
            total = jnp.where(token + b * half < live, total, 0.0)
            out_rows[i, rows] = total.astype(BF).reshape(half, 2, columns)

        outs = []
        for i in range(count):
            for copy in copies[i]:
                copy.wait()
            pltpu.make_async_copy(
                map_refs[0][1].at[0], ups.at[i], sems.at[i, n_base + n_rank]
            ).wait()
            live = plan_ref[LENGTH, first + i]
            rows_for(i, n_base, live, 0)

            @pl.when(live > half)
            def _():
                rows_for(i, n_base, live, 1)

            @pl.when(live <= half)
            def _():
                out_rows[i, half:] = jnp.zeros((half, 2, columns), BF)

            row = pl.multiple_of(plan_ref[ORDER, first + i] * prefill, prefill)
            outs.append(
                pltpu.make_async_copy(
                    out_rows.at[i], o_ref.at[pl.ds(row, prefill)], out_sems.at[i]
                )
            )
            outs[-1].start()
        for copy in outs:
            copy.wait()

    operands = [plan]
    for _, _, pieces in bases + ranks:
        operands += pieces
    operands += maps.values()
    aliases = {}
    if before is not None:
        aliases = {len(operands): 0}
        operands.append(before)
    return pl.pallas_call(
        body,
        out_shape=jax.ShapeDtypeStruct(shape, BF),
        grid_spec=pltpu.PrefetchScalarGridSpec(
            num_scalar_prefetch=1,
            grid=(),
            in_specs=[ANY] * (len(operands) - 1),
            out_specs=ANY,
            scratch_shapes=[
                pltpu.VMEM((count, 2, depth, columns), BF),
                pltpu.VMEM((count, n_base, prefill, 2 * columns), BF),
                pltpu.VMEM((count, n_rank, prefill, 2 * depth), BF),
                pltpu.VMEM((count, prefill, 2, columns), BF),
                pltpu.SemaphoreType.DMA((count, n_base + n_rank + 1)),
                pltpu.SemaphoreType.DMA((count,)),
            ],
        ),
        input_output_aliases=aliases,
        compiler_params=params(),
        cost_estimate=cost(12 * count * prefill * prefill * 2 * columns, 20 * count * prefill * columns),
        name="finish",
    )(*operands)


def solution(mesh):
    n_z, n_t = mesh.shape["adapter"], mesh.shape["tensor"]
    n_x = n_t // 2

    def core_swap(a):
        return lax.ppermute(a, "tensor", [(t, t ^ 1) for t in range(n_t)])

    def chip_shift(a, k):
        return lax.ppermute(
            a,
            "tensor",
            [(2 * x + c, 2 * ((x + k) % n_x) + c) for x in range(n_x) for c in (0, 1)],
        )

    def leftward(a, hops=1):
        return lax.ppermute(a, "adapter", [(z, z - hops) for z in range(hops, n_z)])

    def rightward(a, hops=1):
        return lax.ppermute(a, "adapter", [(z - hops, z) for z in range(hops, n_z)])

    def per_device(hidden, weight, down, up, table, adapters, lengths):
        requests = adapters.shape[0]
        prefill = hidden.shape[0] // requests
        stored = down.shape[0]
        columns = up.shape[3]
        by_distance = n_z == RANK_CHUNKS
        z, t = lax.axis_index("adapter"), lax.axis_index("tensor")
        plan = plan_requests(
            table, adapters, lengths, jnp.reshape(z, (1,)), n_z, stored
        )

        downs = {0: down}
        for hops in range(1, n_z):
            left, right = downs[hops - 1], downs[0 if hops == 1 else n_z + hops - 2]
            downs[hops] = leftward(left)
            downs[n_z - 1 + hops] = rightward(right)

        def within(maps, hops):
            keys = range(hops + 1), range(n_z, n_z + hops)
            return {(k,): maps[k] for part in keys for k in part}

        dest = jnp.arange(n_t, dtype=jnp.int32)
        away = (dest // 2 - t // 2 + n_x) % n_x
        slots = jnp.where(dest % 2 == t % 2, n_x + away, away)

        bases, pairs = [], []

        def exchange(first, count, send, keep):
            beyond = [core_swap(send[k]) for k in range(1, n_x)]
            pieces = [keep, core_swap(send[0])]
            for k in range(1, n_x):
                pairs.append(pair_sum(keep, beyond[k - 1], k))
                pieces.append(chip_shift(pairs[-1], k))
            bases.append((first, count, pieces))

        split, send, keep = split_weight(
            plan, slots, hidden, weight, BASE_CHUNKS[0], prefill
        )
        exchange(0, BASE_CHUNKS[0], send, keep)

        near = [downs[1], downs[n_z]]
        middle = [downs[2], downs[n_z + 1]]
        for chunk in range(1, len(BASE_CHUNKS)):
            first, count = sum(BASE_CHUNKS[:chunk]), BASE_CHUNKS[chunk]
            after = pairs[-1:]
            if chunk == 2:
                after = after + near + [bases[0][2][-1]]
            send, keep = base_products(
                plan, hidden, split, first, count, prefill, after
            )
            exchange(first, count, send, keep)

        ups = {(0,): up}
        late_up = copy_after(up, middle)
        for hops in range(1, n_z):
            ups[hops, 2 * n_z - 1 - hops] = lax.ppermute(
                late_up, "adapter", [(z, (z - hops) % n_z) for z in range(n_z)]
            )

        ranks = []
        count = requests // RANK_CHUNKS

        def rank(chunk, after):
            hops = chunk if by_distance else n_z - 1
            part = rank_products(
                plan, hidden, within(downs, hops), chunk * count, count, prefill, after
            )
            pair = (part.astype(F32) + core_swap(part).astype(F32)).astype(BF)
            pieces = [pair] + [chip_shift(pair, k) for k in range(1, n_x)]
            ranks.append((chunk * count, count, pieces))
            return part

        shape = (requests * prefill, 2, columns)

        def write(out, first, last):
            held = [
                b
                for b in bases
                if b[0] < last * count and b[0] + b[1] > first * count
            ]
            return finish(
                plan,
                held,
                ranks[first:last],
                ups,
                out,
                first * count,
                (last - first) * count,
                prefill,
                shape,
            )

        part = rank(0, pairs[-1:])
        part = rank(1, [part])
        part = rank(2, [part, bases[1][2][-1]])
        out = write(None, 0, 2)
        out = write(out, 2, 3)
        rank(3, [])
        return write(out, 3, 4)

    return jax.shard_map(
        per_device,
        mesh=mesh,
        in_specs=(
            P(("group", "adapter"), "tensor"),
            P("tensor", None, None),
            P(("group", "adapter"), "tensor", None),
            P(("group", "adapter"), None, None, "tensor"),
            P("group"),
            P(("group", "adapter")),
            P(("group", "adapter")),
        ),
        out_specs=P(("group", "adapter"), None, "tensor"),
        check_vma=False,
    )
```

```python
import jax
import jax.numpy as jnp
from jax import lax
from jax.experimental import pallas as pl
from jax.experimental.pallas import tpu as pltpu
from jax.sharding import PartitionSpec as P

BF = jnp.bfloat16
F32 = jnp.float32
BASE_CHUNKS = (3, 5, 4)
RANK_CHUNKS = 4
SMEM = pltpu.SMEM
ANY = pl.BlockSpec(memory_space=pl.ANY)


def cost(flops, moved):
    return pl.CostEstimate(
        flops=int(flops * 0.01), bytes_accessed=int(moved * 0.01), transcendentals=0
    )


ORDER, SOURCE, ROW, LENGTH = range(4)


def params(mib=60):
    return pltpu.CompilerParams(vmem_limit_bytes=mib * 1024 * 1024)


def pack_maps(down, up):
    stored, features, lanes = down.shape
    _, sides, depth, columns = up.shape
    tiles = columns // lanes
    part = sides * depth

    def body(down_ref, up_ref, o_ref, held, sems):
        copies = []
        for a in range(stored):
            copies.append(
                pltpu.make_async_copy(
                    down_ref.at[a], o_ref.at[a, pl.ds(0, features)], sems.at[0, a]
                )
            )
            copies[-1].start()
        for a in range(stored):
            flat = up_ref[a].reshape(part, columns)
            for j in range(tiles):
                held[a, j * part : (j + 1) * part] = flat[:, j * lanes : (j + 1) * lanes]
            copies.append(
                pltpu.make_async_copy(
                    held.at[a],
                    o_ref.at[a, pl.ds(features, tiles * part)],
                    sems.at[1, a],
                )
            )
            copies[-1].start()
        for copy in copies:
            copy.wait()

    return pl.pallas_call(
        body,
        out_shape=jax.ShapeDtypeStruct((stored, features + tiles * part, lanes), BF),
        in_specs=[pl.BlockSpec(memory_space=pltpu.VMEM)] * 2,
        out_specs=ANY,
        scratch_shapes=[
            pltpu.VMEM((stored, tiles * part, lanes), BF),
            pltpu.SemaphoreType.DMA((2, stored)),
        ],
        compiler_params=params(),
        cost_estimate=cost(0, 4 * down.size),
        name="pack_maps",
    )(down, up)


def plan_requests(table, adapters, lengths, here, n_z, stored):
    requests, known = adapters.shape[0], table.shape[0]
    shape = (requests, 128)

    def body(table_ref, adapter_ref, length_ref, here_ref, plan_ref):
        me = here_ref[0]
        request = lax.broadcasted_iota(jnp.int32, shape, 0)
        lane = lax.broadcasted_iota(jnp.int32, shape, 1)
        diagonal = request == lane

        def wide(ref, n):
            return jnp.pad(ref[...], ((0, 0), (0, 128 - n)))

        def down(a):
            return jnp.sum(jnp.where(diagonal, a, 0), axis=1, keepdims=True)

        def across(a):
            return jnp.sum(jnp.where(diagonal, a, 0), axis=0, keepdims=True)

        hit = (down(wide(adapter_ref, requests)) == lane) & (lane < known)
        slot = jnp.sum(jnp.where(hit, wide(table_ref, known), 0), 1, keepdims=True)
        owner = jnp.zeros_like(slot)
        for z in range(1, n_z):
            owner += jnp.where(slot >= z * stored, 1, 0)
        source = jnp.where(owner >= me, owner - me, n_z - 1 + me - owner)
        key = jnp.abs(owner - me) * 128 + request[:, :1]
        before = (across(key) < key) & (lane < requests)
        place = jnp.sum(jnp.where(before, 1, 0), axis=1, keepdims=True)
        at = place == lane

        def placed(a):
            return jnp.sum(jnp.where(at, a, 0), axis=0, keepdims=True)

        plan_ref[ORDER : ORDER + 1] = placed(request)
        plan_ref[SOURCE : SOURCE + 1] = placed(source)
        plan_ref[ROW : ROW + 1] = placed(slot - owner * stored)
        plan_ref[LENGTH : LENGTH + 1] = placed(down(wide(length_ref, requests)))

    vmem = pl.BlockSpec(memory_space=pltpu.VMEM)
    return pl.pallas_call(
        body,
        out_shape=jax.ShapeDtypeStruct((8, 128), jnp.int32),
        in_specs=[vmem, vmem, vmem, pl.BlockSpec(memory_space=SMEM)],
        out_specs=vmem,
        cost_estimate=cost(0, 1 << 20),
        name="plan_requests",
    )(table[None, :], adapters[None, :], lengths[None, :], here)


def split_weight(plan, slots, hidden, weight, count, prefill):
    features, _, columns = weight.shape
    n_t = slots.shape[0]
    n_x = n_t // 2
    width = columns // n_t
    rows, half = 512, 128
    steps = features // rows

    def body(plan_ref, slot_ref, *rest):
        x_refs, (w_ref, o_ref, *send_refs, keep_ref, total) = rest[:count], rest[count:]
        step = pl.program_id(0)
        out_row = lax.broadcasted_iota(jnp.int32, (2 * half, 2 * half), 0)
        in_row = lax.broadcasted_iota(jnp.int32, (2 * half, 2 * half), 1)
        pick = in_row == 2 * (out_row % half) + out_row // half
        pick = pick.astype(F32).astype(BF)
        for b in range(rows // half):
            mixed = w_ref[b * half : (b + 1) * half].reshape(2 * half, columns)
            apart = jnp.dot(pick, mixed, preferred_element_type=F32).astype(BF)
            for t in range(n_t):
                for s in range(2):
                    o_ref[
                        slot_ref[t],
                        b * half : (b + 1) * half,
                        s * width : (s + 1) * width,
                    ] = apart[s * half : (s + 1) * half, t * width : (t + 1) * width]

        @pl.when(step == 0)
        def _():
            total[...] = jnp.zeros_like(total)

        for r in range(count):
            for j in range(n_t):
                total[j, r * prefill : (r + 1) * prefill] += jnp.dot(
                    x_refs[r][...], o_ref[j], preferred_element_type=F32
                )

        @pl.when(step == steps - 1)
        def _():
            send_refs[0][...] = total[0].astype(BF)
            for j in range(1, n_x):
                send_refs[2 * j - 1][...] = total[j, :cut].astype(BF)
                send_refs[2 * j][...] = total[j, cut:].astype(BF)
            for j in range(n_x):
                keep_ref[j] = total[n_x + j].astype(BF)

    part = (count * prefill, 2 * width)
    cut = (count // 2) * prefill
    upper, lower = (cut, 2 * width), (count * prefill - cut, 2 * width)
    outs = [part] + [upper, lower] * (n_x - 1)
    split, *sends, keep = pl.pallas_call(
        body,
        out_shape=(
            jax.ShapeDtypeStruct((n_t, features, 2 * width), BF),
            *[jax.ShapeDtypeStruct(out, BF) for out in outs],
            jax.ShapeDtypeStruct((n_x, *part), BF),
        ),
        grid_spec=pltpu.PrefetchScalarGridSpec(
            num_scalar_prefetch=2,
            grid=(steps,),
            in_specs=[
                pl.BlockSpec((prefill, rows), lambda i, p, s, r=r: (p[ORDER, r], i))
                for r in range(count)
            ]
            + [pl.BlockSpec((rows, 2, columns), lambda i, p, s: (i, 0, 0))],
            out_specs=(
                pl.BlockSpec((n_t, rows, 2 * width), lambda i, p, s: (0, i, 0)),
                *[pl.BlockSpec(out, lambda i, p, s: (0, 0)) for out in outs],
                pl.BlockSpec((n_x, *part), lambda i, p, s: (0, 0, 0)),
            ),
            scratch_shapes=[pltpu.VMEM((n_t, count * prefill, 2 * width), F32)],
        ),
        compiler_params=params(),
        cost_estimate=cost(2 * count * prefill * features * 2 * columns, 8 * features * columns),
        name="split_weight",
    )(plan, slots, *[hidden] * count, weight)
    return split, sends, keep


def base_products(plan, hidden, weight, first, count, prefill, after):
    n_t, features, width = weight.shape
    n_x = n_t // 2
    short = prefill // 2
    n_after = len(after)

    def body(plan_ref, x_ref, *rest):
        w_refs = rest[:n_t]
        *send_refs, keep_ref = rest[n_t + n_after :]
        live = plan_ref[LENGTH, first + pl.program_id(0)]

        def products(rows):
            dead = jnp.zeros((prefill - rows, width), BF)
            for j in range(n_t):
                out = jnp.dot(
                    x_ref[:rows], w_refs[j][0], preferred_element_type=F32
                ).astype(BF)
                if rows < prefill:
                    out = jnp.concatenate([out, dead], 0)
                if j == 0:
                    send_refs[0][...] = out
                elif j >= n_x:
                    keep_ref[j - n_x] = out
                else:

                    @pl.when(pl.program_id(0) < cut)
                    def _():
                        send_refs[2 * j - 1][...] = out

                    @pl.when(pl.program_id(0) >= cut)
                    def _():
                        send_refs[2 * j][...] = out

        @pl.when(live > short)
        def _():
            products(prefill)

        @pl.when(live <= short)
        def _():
            products(short)

    cut = count // 2
    parts = [count] + [cut, count - cut] * (n_x - 1)
    block = (prefill, width)
    places = [lambda i, p: (i, 0)] + [
        lambda i, p: (jnp.minimum(i, cut - 1), 0),
        lambda i, p: (jnp.maximum(i - cut, 0), 0),
    ] * (n_x - 1)
    *sends, keep = pl.pallas_call(
        body,
        out_shape=(
            *[jax.ShapeDtypeStruct((n * prefill, width), BF) for n in parts],
            jax.ShapeDtypeStruct((n_x, count * prefill, width), BF),
        ),
        grid_spec=pltpu.PrefetchScalarGridSpec(
            num_scalar_prefetch=1,
            grid=(count,),
            in_specs=[
                pl.BlockSpec(
                    (prefill, features), lambda i, p: (p[ORDER, first + i], 0)
                ),
            ]
            + [
                pl.BlockSpec((1, features, width), lambda i, p, j=j: (j, 0, 0))
                for j in range(n_t)
            ]
            + [ANY] * n_after,
            out_specs=(
                *[pl.BlockSpec(block, place) for place in places],
                pl.BlockSpec((n_x, prefill, width), lambda i, p: (0, i, 0)),
            ),
        ),
        compiler_params=params(),
        cost_estimate=cost(2 * count * prefill * features * width * n_t, 2 * n_t * features * width),
        name="base_products",
    )(plan, hidden, *[weight] * n_t, *after)
    return sends, keep


def pair_sum(one, others, index, after):
    _, rows, width = one.shape
    cut = others[0].shape[0]

    def body(a_ref, *rest):
        b_refs = rest[:2]
        o_ref, mine, theirs, total, sems, out_sems = rest[2 + len(after) :]
        copies, outs = [], []
        spans = [pl.ds(0, cut), pl.ds(cut, rows - cut)]
        for k, span in enumerate(spans):
            copies.append(
                (
                    pltpu.make_async_copy(
                        a_ref.at[index, span], mine.at[span], sems.at[0, k]
                    ),
                    pltpu.make_async_copy(b_refs[k], theirs.at[span], sems.at[1, k]),
                )
            )
            for copy in copies[-1]:
                copy.start()
        for k, span in enumerate(spans):
            for copy in copies[k]:
                copy.wait()
            value = mine[span].astype(F32) + theirs[span].astype(F32)
            total[span] = value.astype(BF)
            outs.append(
                pltpu.make_async_copy(total.at[span], o_ref.at[span], out_sems.at[k])
            )
            outs[-1].start()
        for copy in outs:
            copy.wait()

    return pl.pallas_call(
        body,
        out_shape=jax.ShapeDtypeStruct((rows, width), BF),
        in_specs=[ANY] * (3 + len(after)),
        out_specs=ANY,
        scratch_shapes=[pltpu.VMEM((rows, width), BF)] * 3
        + [pltpu.SemaphoreType.DMA((2, 2)), pltpu.SemaphoreType.DMA((2,))],
        compiler_params=params(),
        cost_estimate=cost(rows * width, 6 * rows * width),
        name="pair_sum",
    )(one, *others, *after)


def hold(arrays, after):
    n = len(arrays)

    def body(*refs):
        pass

    return pl.pallas_call(
        body,
        out_shape=[jax.ShapeDtypeStruct(a.shape, a.dtype) for a in arrays],
        in_specs=[ANY] * (n + len(after)),
        out_specs=[ANY] * n,
        input_output_aliases={i: i for i in range(n)},
        compiler_params=params(),
        cost_estimate=cost(0, 1 << 20),
        name="hold",
    )(*arrays, *after)


def fetch(refs, source, row, part, target, sem):
    for codes, ref in refs:
        hit = source == codes[0]
        for code in codes[1:]:
            hit |= source == code

        @pl.when(hit)
        def _():
            pltpu.make_async_copy(ref.at[row, part], target, sem).start()


def rank_products(plan, hidden, maps, first, count, prefill, after):
    sources = list(maps)
    features, ranks = hidden.shape[1], maps[sources[0]].shape[2]
    n_map, n_after = len(maps), len(after)
    short = prefill // 2
    down = pl.ds(0, features)

    def body(plan_ref, x_ref, *rest):
        refs = list(zip(sources, rest[:n_map]))
        o_ref, rows, held, sems = rest[n_map + n_after :]
        copies = []
        for i in range(count):
            fetch(
                refs,
                plan_ref[SOURCE, first + i],
                plan_ref[ROW, first + i],
                down,
                held.at[i],
                sems.at[0, i],
            )
            at = pl.multiple_of(plan_ref[ORDER, first + i] * prefill, prefill)
            copies.append(
                pltpu.make_async_copy(
                    x_ref.at[pl.ds(at, prefill)], rows.at[i], sems.at[1, i]
                )
            )
            copies[-1].start()
        for i in range(count):
            pltpu.make_async_copy(
                rest[0].at[0, down], held.at[i], sems.at[0, i]
            ).wait()
            copies[i].wait()
            live = plan_ref[LENGTH, first + i]
            above, below = i * prefill, i * prefill + short

            @pl.when(live > short)
            def _():
                o_ref[above : above + prefill] = jnp.dot(
                    rows[i], held[i], preferred_element_type=F32
                ).astype(BF)

            @pl.when(live <= short)
            def _():
                o_ref[above:below] = jnp.dot(
                    rows[i, :short], held[i], preferred_element_type=F32
                ).astype(BF)
                o_ref[below : below + short] = jnp.zeros((short, ranks), BF)

    return pl.pallas_call(
        body,
        out_shape=jax.ShapeDtypeStruct((count * prefill, ranks), BF),
        grid_spec=pltpu.PrefetchScalarGridSpec(
            num_scalar_prefetch=1,
            grid=(),
            in_specs=[ANY] * (1 + n_map + n_after),
            out_specs=pl.BlockSpec(memory_space=pltpu.VMEM),
            scratch_shapes=[
                pltpu.VMEM((count, prefill, features), BF),
                pltpu.VMEM((count, features, ranks), BF),
                pltpu.SemaphoreType.DMA((2, count)),
            ],
        ),
        compiler_params=params(),
        cost_estimate=cost(2 * count * prefill * features * ranks, 2 * count * features * (prefill + ranks)),
        name="rank_products",
    )(plan, hidden, *maps.values(), *after)


def finish(plan, bases, ranks, maps, before, first, count, prefill, shape):
    sources = list(maps)
    columns, depth = shape[2], ranks[0][2][0].shape[1] // 2
    _, packed, lanes = maps[sources[0]].shape
    tiles = columns // lanes
    extra = tiles * 2 * depth
    up_part = pl.ds(packed - extra, extra)
    half = prefill // 2
    n_map = len(maps)
    n_base = max(len(pieces) for _, _, pieces in bases)
    n_rank = max(len(pieces) for _, _, pieces in ranks)

    def body(plan_ref, *rest):
        base_refs, rank_refs = [], []
        for refs, pieces in ((base_refs, bases), (rank_refs, ranks)):
            for start, n, arrays in pieces:
                refs.append((start, n, rest[: len(arrays)]))
                rest = rest[len(arrays) :]
        map_refs = list(zip(sources, rest[:n_map]))
        o_ref, ups, base_rows, rank_rows, out_rows, sems, out_sems = rest[-7:]

        def start_pieces(refs, at, rows, sem):
            copies = []
            for start, n, arrays in refs:
                if start <= at < start + n:
                    block = pl.ds((at - start) * prefill, prefill)
                    for k, ref in enumerate(arrays):
                        source = ref.at[0, block] if len(ref.shape) == 3 else ref.at[block]
                        copies.append(pltpu.make_async_copy(source, rows.at[k], sem.at[k]))
                        copies[-1].start()
            return copies

        copies = []
        for i in range(count):
            at = first + i
            copies.append(
                start_pieces(base_refs, at, base_rows.at[i], sems.at[i])
                + start_pieces(
                    rank_refs, at, rank_rows.at[i], sems.at[i, pl.ds(n_base, n_rank)]
                )
            )
            fetch(
                map_refs,
                plan_ref[SOURCE, at],
                plan_ref[ROW, at],
                up_part,
                ups.at[i],
                sems.at[i, n_base + n_rank],
            )

        mix_row = lax.broadcasted_iota(jnp.int32, (2 * half, 2 * half), 0)
        mix_column = lax.broadcasted_iota(jnp.int32, (2 * half, 2 * half), 1)
        mix = mix_column == mix_row // 2 + half * (mix_row % 2)
        mix = mix.astype(F32).astype(BF)
        twice_row = lax.broadcasted_iota(jnp.int32, (2 * half, half), 0)
        twice_column = lax.broadcasted_iota(jnp.int32, (2 * half, half), 1)
        twice = (twice_column == twice_row // 2).astype(F32).astype(BF)
        lane = lax.broadcasted_iota(jnp.int32, (2 * half, 2 * depth), 1)
        side = lax.broadcasted_iota(jnp.int32, (2 * half, 2 * depth), 0) % 2
        own_side = lane // depth == side
        token = lax.broadcasted_iota(jnp.int32, (2 * half, columns), 0) // 2

        def rows_for(i, pieces, live, b):
            rows = slice(b * half, (b + 1) * half)
            total = jnp.zeros((2 * half, columns), F32)
            for k in range(pieces):
                piece = base_rows[i, k, rows]
                piece = jnp.concatenate([piece[:, :columns], piece[:, columns:]], 0)
                total += jnp.dot(mix, piece, preferred_element_type=F32)
            rank = rank_rows[i, 0, rows].astype(F32)
            for k in range(1, n_rank):
                rank += rank_rows[i, k, rows].astype(F32)
            rank = jnp.dot(twice, rank.astype(BF), preferred_element_type=F32)
            rank = jnp.where(own_side, rank, 0.0).astype(BF)
            up = jnp.concatenate(
                [ups[i, j * 2 * depth : (j + 1) * 2 * depth] for j in range(tiles)], 1
            )
            total += jnp.dot(rank, up, preferred_element_type=F32)
            total = jnp.where(token + b * half < live, total, 0.0)
            out_rows[i, rows] = total.astype(BF).reshape(half, 2, columns)

        outs = []
        for i in range(count):
            for copy in copies[i]:
                copy.wait()
            pltpu.make_async_copy(
                map_refs[0][1].at[0, up_part], ups.at[i], sems.at[i, n_base + n_rank]
            ).wait()
            live = plan_ref[LENGTH, first + i]
            rows_for(i, n_base, live, 0)

            @pl.when(live > half)
            def _():
                rows_for(i, n_base, live, 1)

            @pl.when(live <= half)
            def _():
                out_rows[i, half:] = jnp.zeros((half, 2, columns), BF)

            row = pl.multiple_of(plan_ref[ORDER, first + i] * prefill, prefill)
            outs.append(
                pltpu.make_async_copy(
                    out_rows.at[i], o_ref.at[pl.ds(row, prefill)], out_sems.at[i]
                )
            )
            outs[-1].start()
        for copy in outs:
            copy.wait()

    operands = [plan]
    for _, _, pieces in bases + ranks:
        operands += pieces
    operands += maps.values()
    aliases = {}
    if before is not None:
        aliases = {len(operands): 0}
        operands.append(before)
    return pl.pallas_call(
        body,
        out_shape=jax.ShapeDtypeStruct(shape, BF),
        grid_spec=pltpu.PrefetchScalarGridSpec(
            num_scalar_prefetch=1,
            grid=(),
            in_specs=[ANY] * (len(operands) - 1),
            out_specs=ANY,
            scratch_shapes=[
                pltpu.VMEM((count, extra, lanes), BF),
                pltpu.VMEM((count, n_base, prefill, 2 * columns), BF),
                pltpu.VMEM((count, n_rank, prefill, 2 * depth), BF),
                pltpu.VMEM((count, prefill, 2, columns), BF),
                pltpu.SemaphoreType.DMA((count, n_base + n_rank + 1)),
                pltpu.SemaphoreType.DMA((count,)),
            ],
        ),
        input_output_aliases=aliases,
        compiler_params=params(),
        cost_estimate=cost(12 * count * prefill * prefill * 2 * columns, 20 * count * prefill * columns),
        name="finish",
    )(*operands)


def solution(mesh):
    n_z, n_t = mesh.shape["adapter"], mesh.shape["tensor"]
    n_x = n_t // 2

    def core_swap(a):
        return lax.ppermute(a, "tensor", [(t, t ^ 1) for t in range(n_t)])

    def chip_shift(a, k):
        return lax.ppermute(
            a,
            "tensor",
            [(2 * x + c, 2 * ((x + k) % n_x) + c) for x in range(n_x) for c in (0, 1)],
        )

    def leftward(a, hops=1):
        return lax.ppermute(a, "adapter", [(z, z - hops) for z in range(hops, n_z)])

    def rightward(a, hops=1):
        return lax.ppermute(a, "adapter", [(z - hops, z) for z in range(hops, n_z)])

    def per_device(hidden, weight, down, up, table, adapters, lengths):
        requests = adapters.shape[0]
        prefill = hidden.shape[0] // requests
        stored = down.shape[0]
        columns = up.shape[3]
        by_distance = n_z == RANK_CHUNKS
        z, t = lax.axis_index("adapter"), lax.axis_index("tensor")
        plan = plan_requests(
            table, adapters, lengths, jnp.reshape(z, (1,)), n_z, stored
        )

        downs = {0: pack_maps(down, up)}

        def relay(hops, after):
            left, right = downs[hops - 1], downs[0 if hops == 1 else n_z + hops - 2]
            if after:
                left, right = hold([left, right], after)
                downs[hops - 1], downs[n_z + hops - 2] = left, right
            downs[hops] = leftward(left)
            downs[n_z - 1 + hops] = rightward(right)

        relay(1, [])

        def within(maps, hops):
            keys = range(hops + 1), range(n_z, n_z + hops)
            return {(k,): maps[k] for part in keys for k in part}

        dest = jnp.arange(n_t, dtype=jnp.int32)
        away = (dest // 2 - t // 2 + n_x) % n_x
        slots = jnp.where(dest % 2 == t % 2, n_x + away, away)

        bases, pairs = [], []

        def send_on(first, count, sends, keep, after):
            got = [core_swap(part) for part in sends[1:]] + [core_swap(sends[0])]
            pieces = [keep, got.pop()]
            for k in range(1, n_x):
                pairs.append(pair_sum(keep, got[2 * k - 2 : 2 * k], k, after))
                pieces.append(chip_shift(pairs[-1], k))
            bases.append((first, count, pieces))

        def base(chunk):
            first, count = sum(BASE_CHUNKS[:chunk]), BASE_CHUNKS[chunk]
            return (first, count) + base_products(
                plan, hidden, split, first, count, prefill, pairs[-1:]
            )

        ranks = []
        count = requests // RANK_CHUNKS

        def rank(chunk, after):
            hops = chunk if by_distance else n_z - 1
            part = rank_products(
                plan, hidden, within(downs, hops), chunk * count, count, prefill, after
            )
            pair = (part.astype(F32) + core_swap(part).astype(F32)).astype(BF)
            pieces = [pair] + [chip_shift(pair, k) for k in range(1, n_x)]
            ranks.append((chunk * count, count, pieces))
            return part

        shape = (requests * prefill, 2, columns)

        def write(out, first, last):
            held = [
                b
                for b in bases
                if b[0] < last * count and b[0] + b[1] > first * count
            ]
            return finish(
                plan,
                held,
                ranks[first:last],
                within(downs, last - 1 if by_distance else n_z - 1),
                out,
                first * count,
                (last - first) * count,
                prefill,
                shape,
            )

        split, sends, keep = split_weight(
            plan, slots, hidden, weight, BASE_CHUNKS[0], prefill
        )
        send_on(0, BASE_CHUNKS[0], sends, keep, [])
        second = base(1)
        if n_z > 2:
            relay(2, [second[3], bases[0][2][-1]])
        send_on(*second, [bases[0][2][-1]])
        third = base(2)
        part = rank(0, [third[3]]) if by_distance else third[3]
        part = rank(1, [part]) if by_distance else part
        for hops in range(3, n_z):
            relay(hops, [part])
        send_on(*third, [part, bases[1][2][-1]])
        if by_distance:
            part = rank(2, [pairs[-1], ranks[0][2][-1]])
        else:
            for chunk in range(3):
                part = rank(chunk, [pairs[-1]])
        out = write(None, 0, 2)
        out = write(out, 2, 3)
        rank(3, [out])
        return write(out, 3, 4)

    return jax.shard_map(
        per_device,
        mesh=mesh,
        in_specs=(
            P(("group", "adapter"), "tensor"),
            P("tensor", None, None),
            P(("group", "adapter"), "tensor", None),
            P(("group", "adapter"), None, None, "tensor"),
            P("group"),
            P(("group", "adapter")),
            P(("group", "adapter")),
        ),
        out_specs=P(("group", "adapter"), None, "tensor"),
        check_vma=False,
    )
```

```python
import jax
import jax.numpy as jnp
from jax import lax
from jax.experimental import pallas as pl
from jax.experimental.pallas import tpu as pltpu
from jax.sharding import PartitionSpec as P

BF = jnp.bfloat16
F32 = jnp.float32
BASE_CHUNKS = (3, 3, 3, 3)
RANK_CHUNKS = 4
SMEM = pltpu.SMEM
PIECE = 2


def pieces_of(count):
    return [(at, min(PIECE, count - at)) for at in range(0, count, PIECE)]


ANY = pl.BlockSpec(memory_space=pl.ANY)


def cost(flops, moved):
    return pl.CostEstimate(
        flops=int(flops * 0.01), bytes_accessed=int(moved * 0.01), transcendentals=0
    )


ORDER, SOURCE, ROW, LENGTH = range(4)


def params(mib=60):
    return pltpu.CompilerParams(vmem_limit_bytes=mib * 1024 * 1024)


def pack_maps(down, up):
    stored, features, lanes = down.shape
    _, sides, depth, columns = up.shape
    tiles = columns // lanes
    part = sides * depth

    def body(down_ref, up_ref, o_ref, held, sems):
        copies = []
        for a in range(stored):
            copies.append(
                pltpu.make_async_copy(
                    down_ref.at[a], o_ref.at[a, pl.ds(0, features)], sems.at[0, a]
                )
            )
            copies[-1].start()
        for a in range(stored):
            flat = up_ref[a].reshape(part, columns)
            for j in range(tiles):
                held[a, j * part : (j + 1) * part] = flat[:, j * lanes : (j + 1) * lanes]
            copies.append(
                pltpu.make_async_copy(
                    held.at[a],
                    o_ref.at[a, pl.ds(features, tiles * part)],
                    sems.at[1, a],
                )
            )
            copies[-1].start()
        for copy in copies:
            copy.wait()

    return pl.pallas_call(
        body,
        out_shape=jax.ShapeDtypeStruct((stored, features + tiles * part, lanes), BF),
        in_specs=[pl.BlockSpec(memory_space=pltpu.VMEM)] * 2,
        out_specs=ANY,
        scratch_shapes=[
            pltpu.VMEM((stored, tiles * part, lanes), BF),
            pltpu.SemaphoreType.DMA((2, stored)),
        ],
        compiler_params=params(60),
        cost_estimate=cost(0, 4 * down.size),
        name="pack_maps",
    )(down, up)


def plan_requests(table, adapters, lengths, here, n_z, stored):
    requests, known = adapters.shape[0], table.shape[0]
    shape = (requests, 128)

    def body(table_ref, adapter_ref, length_ref, here_ref, plan_ref):
        me = here_ref[0]
        request = lax.broadcasted_iota(jnp.int32, shape, 0)
        lane = lax.broadcasted_iota(jnp.int32, shape, 1)
        diagonal = request == lane

        def wide(ref, n):
            return jnp.pad(ref[...], ((0, 0), (0, 128 - n)))

        def down(a):
            return jnp.sum(jnp.where(diagonal, a, 0), axis=1, keepdims=True)

        def across(a):
            return jnp.sum(jnp.where(diagonal, a, 0), axis=0, keepdims=True)

        hit = (down(wide(adapter_ref, requests)) == lane) & (lane < known)
        slot = jnp.sum(jnp.where(hit, wide(table_ref, known), 0), 1, keepdims=True)
        owner = jnp.zeros_like(slot)
        for z in range(1, n_z):
            owner += jnp.where(slot >= z * stored, 1, 0)
        source = jnp.where(owner >= me, owner - me, n_z - 1 + me - owner)
        key = jnp.abs(owner - me) * 128 + request[:, :1]
        before = (across(key) < key) & (lane < requests)
        place = jnp.sum(jnp.where(before, 1, 0), axis=1, keepdims=True)
        at = place == lane

        def placed(a):
            return jnp.sum(jnp.where(at, a, 0), axis=0, keepdims=True)

        plan_ref[ORDER : ORDER + 1] = placed(request)
        plan_ref[SOURCE : SOURCE + 1] = placed(source)
        plan_ref[ROW : ROW + 1] = placed(slot - owner * stored)
        plan_ref[LENGTH : LENGTH + 1] = placed(down(wide(length_ref, requests)))

    vmem = pl.BlockSpec(memory_space=pltpu.VMEM)
    return pl.pallas_call(
        body,
        out_shape=jax.ShapeDtypeStruct((8, 128), jnp.int32),
        in_specs=[vmem, vmem, vmem, pl.BlockSpec(memory_space=SMEM)],
        out_specs=vmem,
        cost_estimate=cost(0, 1 << 20),
        name="plan_requests",
    )(table[None, :], adapters[None, :], lengths[None, :], here)


def split_weight(plan, slots, hidden, weight, count, prefill):
    features, _, columns = weight.shape
    n_t = slots.shape[0]
    n_x = n_t // 2
    width = columns // n_t
    rows, half = 512, 128
    steps = features // rows

    def body(plan_ref, slot_ref, *rest):
        x_refs, (w_ref, o_ref, *send_refs, keep_ref, total) = rest[:count], rest[count:]
        step = pl.program_id(0)
        above = pl.multiple_of(step * rows, rows)
        out_row = lax.broadcasted_iota(jnp.int32, (2 * half, 2 * half), 0)
        in_row = lax.broadcasted_iota(jnp.int32, (2 * half, 2 * half), 1)
        pick = in_row == 2 * (out_row % half) + out_row // half
        pick = pick.astype(F32).astype(BF)
        for b in range(rows // half):
            mixed = w_ref[b * half : (b + 1) * half].reshape(2 * half, columns)
            apart = jnp.dot(pick, mixed, preferred_element_type=F32).astype(BF)
            for t in range(n_t):
                for s in range(2):
                    o_ref[
                        slot_ref[t],
                        pl.ds(above + b * half, half),
                        s * width : (s + 1) * width,
                    ] = apart[s * half : (s + 1) * half, t * width : (t + 1) * width]

        @pl.when(step == 0)
        def _():
            total[...] = jnp.zeros_like(total)

        for r in range(count):
            for j in range(n_t):
                total[j, r * prefill : (r + 1) * prefill] += jnp.dot(
                    x_refs[r][...], o_ref[j, pl.ds(above, rows)], preferred_element_type=F32
                )

        @pl.when(step == steps - 1)
        def _():
            send_refs[0][...] = total[0].astype(BF)
            k = 1
            for j in range(1, n_x):
                for at, n in pieces_of(count):
                    rows_of = slice(at * prefill, (at + n) * prefill)
                    send_refs[k][...] = total[j, rows_of].astype(BF)
                    k += 1
            for j in range(n_x):
                keep_ref[j] = total[n_x + j].astype(BF)

    part = (count * prefill, 2 * width)
    outs = [part] + [
        (n * prefill, 2 * width) for _, n in pieces_of(count)
    ] * (n_x - 1)
    split, *sends, keep = pl.pallas_call(
        body,
        out_shape=(
            jax.ShapeDtypeStruct((n_t, features, 2 * width), BF),
            *[jax.ShapeDtypeStruct(out, BF) for out in outs],
            jax.ShapeDtypeStruct((n_x, *part), BF),
        ),
        grid_spec=pltpu.PrefetchScalarGridSpec(
            num_scalar_prefetch=2,
            grid=(steps,),
            in_specs=[
                pl.BlockSpec((prefill, rows), lambda i, p, s, r=r: (p[ORDER, r], i))
                for r in range(count)
            ]
            + [pl.BlockSpec((rows, 2, columns), lambda i, p, s: (i, 0, 0))],
            out_specs=(
                pl.BlockSpec(memory_space=pltpu.VMEM),
                *[pl.BlockSpec(out, lambda i, p, s: (0, 0)) for out in outs],
                pl.BlockSpec((n_x, *part), lambda i, p, s: (0, 0, 0)),
            ),
            scratch_shapes=[pltpu.VMEM((n_t, count * prefill, 2 * width), F32)],
        ),
        compiler_params=params(36),
        cost_estimate=cost(2 * count * prefill * features * 2 * columns, 8 * features * columns),
        name="split_weight",
    )(plan, slots, *[hidden] * count, weight)
    return split, sends, keep


def base_products(plan, hidden, weight, first, count, prefill, after):
    n_t, features, width = weight.shape
    n_x = n_t // 2
    short = prefill // 2
    n_after = len(after)

    def body(plan_ref, x_ref, *rest):
        w_ref = rest[0]
        *send_refs, keep_ref = rest[1 + n_after :]
        live = plan_ref[LENGTH, first + pl.program_id(0)]

        def products(rows):
            dead = jnp.zeros((prefill - rows, width), BF)
            for j in range(n_t):
                out = jnp.dot(
                    x_ref[:rows], w_ref[j], preferred_element_type=F32
                ).astype(BF)
                if rows < prefill:
                    out = jnp.concatenate([out, dead], 0)
                if j == 0:
                    send_refs[0][...] = out
                elif j >= n_x:
                    keep_ref[j - n_x] = out
                else:

                    spans = pieces_of(count)
                    for k, (at, n) in enumerate(spans, 1 + (j - 1) * len(spans)):
                        inside = (pl.program_id(0) >= at) & (pl.program_id(0) < at + n)

                        @pl.when(inside)
                        def _():
                            send_refs[k][...] = out

        @pl.when(live > short)
        def _():
            products(prefill)

        @pl.when(live <= short)
        def _():
            products(short)

    spans = [(0, count)] + pieces_of(count) * (n_x - 1)
    parts = [n for _, n in spans]
    block = (prefill, width)
    places = [
        lambda i, p, at=at, n=n: (jnp.clip(i - at, 0, n - 1), 0) for at, n in spans
    ]
    *sends, keep = pl.pallas_call(
        body,
        out_shape=(
            *[jax.ShapeDtypeStruct((n * prefill, width), BF) for n in parts],
            jax.ShapeDtypeStruct((n_x, count * prefill, width), BF),
        ),
        grid_spec=pltpu.PrefetchScalarGridSpec(
            num_scalar_prefetch=1,
            grid=(count,),
            in_specs=[
                pl.BlockSpec(
                    (prefill, features), lambda i, p: (p[ORDER, first + i], 0)
                ),
            ]
            + [pl.BlockSpec(memory_space=pltpu.VMEM)]
            + [ANY] * n_after,
            out_specs=(
                *[pl.BlockSpec(block, place) for place in places],
                pl.BlockSpec((n_x, prefill, width), lambda i, p: (0, i, 0)),
            ),
        ),
        compiler_params=params(24),
        cost_estimate=cost(2 * count * prefill * features * width * n_t, 2 * n_t * features * width),
        name="base_products",
    )(plan, hidden, weight, *after)
    return sends, keep


def pair_sum(one, others, index, after):
    _, rows, width = one.shape
    n_piece = len(others)

    def body(a_ref, *rest):
        b_refs = rest[:n_piece]
        o_ref, mine, theirs, total, sems, out_sems = rest[n_piece + len(after) :]
        copies, outs = [], []
        spans, at = [], 0
        for b_ref in b_refs:
            spans.append(pl.ds(at, b_ref.shape[0]))
            at += b_ref.shape[0]
        for k, span in enumerate(spans):
            copies.append(
                (
                    pltpu.make_async_copy(
                        a_ref.at[index, span], mine.at[span], sems.at[0, k]
                    ),
                    pltpu.make_async_copy(b_refs[k], theirs.at[span], sems.at[1, k]),
                )
            )
            for copy in copies[-1]:
                copy.start()
        for k, span in enumerate(spans):
            for copy in copies[k]:
                copy.wait()
            value = mine[span].astype(F32) + theirs[span].astype(F32)
            total[span] = value.astype(BF)
            outs.append(
                pltpu.make_async_copy(total.at[span], o_ref.at[span], out_sems.at[k])
            )
            outs[-1].start()
        for copy in outs:
            copy.wait()

    return pl.pallas_call(
        body,
        out_shape=jax.ShapeDtypeStruct((rows, width), BF),
        in_specs=[ANY] * (1 + n_piece + len(after)),
        out_specs=ANY,
        scratch_shapes=[pltpu.VMEM((rows, width), BF)] * 3
        + [pltpu.SemaphoreType.DMA((2, n_piece)), pltpu.SemaphoreType.DMA((n_piece,))],
        compiler_params=params(16),
        cost_estimate=cost(rows * width, 6 * rows * width),
        name="pair_sum",
    )(one, *others, *after)


def hold(arrays, after):
    n = len(arrays)

    def body(*refs):
        pass

    return pl.pallas_call(
        body,
        out_shape=[jax.ShapeDtypeStruct(a.shape, a.dtype) for a in arrays],
        in_specs=[ANY] * (n + len(after)),
        out_specs=[ANY] * n,
        input_output_aliases={i: i for i in range(n)},
        compiler_params=params(16),
        cost_estimate=cost(0, 1 << 20),
        name="hold",
    )(*arrays, *after)


def fetch(refs, source, row, part, target, sem):
    for codes, ref in refs:
        hit = source == codes[0]
        for code in codes[1:]:
            hit |= source == code

        @pl.when(hit)
        def _():
            pltpu.make_async_copy(ref.at[row, part], target, sem).start()


def rank_products(plan, hidden, maps, first, count, prefill, after):
    sources = list(maps)
    features, ranks = hidden.shape[1], maps[sources[0]].shape[2]
    n_map, n_after = len(maps), len(after)
    short = prefill // 2
    down = pl.ds(0, features)

    def body(plan_ref, x_ref, *rest):
        refs = list(zip(sources, rest[:n_map]))
        o_ref, rows, held, sems = rest[n_map + n_after :]
        copies = []
        for i in range(count):
            fetch(
                refs,
                plan_ref[SOURCE, first + i],
                plan_ref[ROW, first + i],
                down,
                held.at[i],
                sems.at[0, i],
            )
            at = pl.multiple_of(plan_ref[ORDER, first + i] * prefill, prefill)
            copies.append(
                pltpu.make_async_copy(
                    x_ref.at[pl.ds(at, prefill)], rows.at[i], sems.at[1, i]
                )
            )
            copies[-1].start()
        for i in range(count):
            pltpu.make_async_copy(
                rest[0].at[0, down], held.at[i], sems.at[0, i]
            ).wait()
            copies[i].wait()
            live = plan_ref[LENGTH, first + i]
            above, below = i * prefill, i * prefill + short

            @pl.when(live > short)
            def _():
                o_ref[above : above + prefill] = jnp.dot(
                    rows[i], held[i], preferred_element_type=F32
                ).astype(BF)

            @pl.when(live <= short)
            def _():
                o_ref[above:below] = jnp.dot(
                    rows[i, :short], held[i], preferred_element_type=F32
                ).astype(BF)
                o_ref[below : below + short] = jnp.zeros((short, ranks), BF)

    return pl.pallas_call(
        body,
        out_shape=jax.ShapeDtypeStruct((count * prefill, ranks), BF),
        grid_spec=pltpu.PrefetchScalarGridSpec(
            num_scalar_prefetch=1,
            grid=(),
            in_specs=[ANY] * (1 + n_map + n_after),
            out_specs=pl.BlockSpec(memory_space=pltpu.VMEM),
            scratch_shapes=[
                pltpu.VMEM((count, prefill, features), BF),
                pltpu.VMEM((count, features, ranks), BF),
                pltpu.SemaphoreType.DMA((2, count)),
            ],
        ),
        compiler_params=params(60),
        cost_estimate=cost(2 * count * prefill * features * ranks, 2 * count * features * (prefill + ranks)),
        name="rank_products",
    )(plan, hidden, *maps.values(), *after)


def finish(plan, bases, ranks, maps, before, first, count, prefill, shape):
    sources = list(maps)
    columns, depth = shape[2], ranks[0][2][0].shape[1] // 2
    _, packed, lanes = maps[sources[0]].shape
    tiles = columns // lanes
    extra = tiles * 2 * depth
    up_part = pl.ds(packed - extra, extra)
    half = prefill // 2
    n_map = len(maps)
    n_base = max(len(pieces) for _, _, pieces in bases)
    n_rank = max(len(pieces) for _, _, pieces in ranks)

    def body(plan_ref, *rest):
        base_refs, rank_refs = [], []
        for refs, pieces in ((base_refs, bases), (rank_refs, ranks)):
            for start, n, arrays in pieces:
                refs.append((start, n, rest[: len(arrays)]))
                rest = rest[len(arrays) :]
        map_refs = list(zip(sources, rest[:n_map]))
        o_ref, ups, base_rows, rank_rows, out_rows, sems, out_sems = rest[-7:]

        def start_pieces(refs, at, rows, sem):
            copies = []
            for start, n, arrays in refs:
                if start <= at < start + n:
                    block = pl.ds((at - start) * prefill, prefill)
                    for k, ref in enumerate(arrays):
                        source = ref.at[0, block] if len(ref.shape) == 3 else ref.at[block]
                        copies.append(pltpu.make_async_copy(source, rows.at[k], sem.at[k]))
                        copies[-1].start()
            return copies

        copies = []
        for i in range(count):
            at = first + i
            copies.append(
                start_pieces(base_refs, at, base_rows.at[i], sems.at[i])
                + start_pieces(
                    rank_refs, at, rank_rows.at[i], sems.at[i, pl.ds(n_base, n_rank)]
                )
            )
            fetch(
                map_refs,
                plan_ref[SOURCE, at],
                plan_ref[ROW, at],
                up_part,
                ups.at[i],
                sems.at[i, n_base + n_rank],
            )

        mix_row = lax.broadcasted_iota(jnp.int32, (2 * half, 2 * half), 0)
        mix_column = lax.broadcasted_iota(jnp.int32, (2 * half, 2 * half), 1)
        mix = mix_column == mix_row // 2 + half * (mix_row % 2)
        mix = mix.astype(F32).astype(BF)
        token = lax.broadcasted_iota(jnp.int32, (half, 2 * columns), 0)

        def rows_for(i, live, b):
            rows = slice(b * half, (b + 1) * half)
            rank = rank_rows[i, 0, rows].astype(F32)
            for k in range(1, n_rank):
                rank += rank_rows[i, k, rows].astype(F32)
            rank = rank.astype(BF)
            up = jnp.concatenate(
                [ups[i, j * 2 * depth : (j + 1) * 2 * depth] for j in range(tiles)], 1
            )
            total = jnp.concatenate(
                [
                    jnp.dot(
                        rank[:, s * depth : (s + 1) * depth],
                        up[s * depth : (s + 1) * depth],
                        preferred_element_type=F32,
                    )
                    for s in range(2)
                ],
                1,
            )
            for k in range(n_base):
                total += base_rows[i, k, rows].astype(F32)
            total = jnp.where(token + b * half < live, total, 0.0).astype(BF)
            total = jnp.concatenate([total[:, :columns], total[:, columns:]], 0)
            total = jnp.dot(mix, total, preferred_element_type=F32).astype(BF)
            out_rows[i, rows] = total.reshape(half, 2, columns)

        outs = []
        for i in range(count):
            for copy in copies[i]:
                copy.wait()
            pltpu.make_async_copy(
                map_refs[0][1].at[0, up_part], ups.at[i], sems.at[i, n_base + n_rank]
            ).wait()
            live = plan_ref[LENGTH, first + i]
            rows_for(i, live, 0)

            @pl.when(live > half)
            def _():
                rows_for(i, live, 1)

            @pl.when(live <= half)
            def _():
                out_rows[i, half:] = jnp.zeros((half, 2, columns), BF)

            row = pl.multiple_of(plan_ref[ORDER, first + i] * prefill, prefill)
            outs.append(
                pltpu.make_async_copy(
                    out_rows.at[i], o_ref.at[pl.ds(row, prefill)], out_sems.at[i]
                )
            )
            outs[-1].start()
        for copy in outs:
            copy.wait()

    operands = [plan]
    for _, _, pieces in bases + ranks:
        operands += pieces
    operands += maps.values()
    aliases = {}
    if before is not None:
        aliases = {len(operands): 0}
        operands.append(before)
    return pl.pallas_call(
        body,
        out_shape=jax.ShapeDtypeStruct(shape, BF),
        grid_spec=pltpu.PrefetchScalarGridSpec(
            num_scalar_prefetch=1,
            grid=(),
            in_specs=[ANY] * (len(operands) - 1),
            out_specs=ANY,
            scratch_shapes=[
                pltpu.VMEM((count, extra, lanes), BF),
                pltpu.VMEM((count, n_base, prefill, 2 * columns), BF),
                pltpu.VMEM((count, n_rank, prefill, 2 * depth), BF),
                pltpu.VMEM((count, prefill, 2, columns), BF),
                pltpu.SemaphoreType.DMA((count, n_base + n_rank + 1)),
                pltpu.SemaphoreType.DMA((count,)),
            ],
        ),
        input_output_aliases=aliases,
        compiler_params=params(60),
        cost_estimate=cost(12 * count * prefill * prefill * 2 * columns, 20 * count * prefill * columns),
        name="finish",
    )(*operands)


def solution(mesh):
    n_z, n_t = mesh.shape["adapter"], mesh.shape["tensor"]
    n_x = n_t // 2

    def core_swap(a):
        return lax.ppermute(a, "tensor", [(t, t ^ 1) for t in range(n_t)])

    def chip_shift(a, k):
        return lax.ppermute(
            a,
            "tensor",
            [(2 * x + c, 2 * ((x + k) % n_x) + c) for x in range(n_x) for c in (0, 1)],
        )

    def leftward(a, hops=1):
        return lax.ppermute(a, "adapter", [(z, z - hops) for z in range(hops, n_z)])

    def rightward(a, hops=1):
        return lax.ppermute(a, "adapter", [(z - hops, z) for z in range(hops, n_z)])

    def per_device(hidden, weight, down, up, table, adapters, lengths):
        requests = adapters.shape[0]
        prefill = hidden.shape[0] // requests
        stored = down.shape[0]
        columns = up.shape[3]
        by_distance = n_z == RANK_CHUNKS
        z, t = lax.axis_index("adapter"), lax.axis_index("tensor")
        plan = plan_requests(
            table, adapters, lengths, jnp.reshape(z, (1,)), n_z, stored
        )

        downs = {0: pack_maps(down, up)}

        def relay(hops, after):
            left, right = downs[hops - 1], downs[0 if hops == 1 else n_z + hops - 2]
            if after:
                left, right = hold([left, right], after)
                downs[hops - 1], downs[n_z + hops - 2] = left, right
            downs[hops] = leftward(left)
            downs[n_z - 1 + hops] = rightward(right)

        relay(1, [])

        def within(maps, hops):
            keys = range(hops + 1), range(n_z, n_z + hops)
            return {(k,): maps[k] for part in keys for k in part}

        dest = jnp.arange(n_t, dtype=jnp.int32)
        away = (dest // 2 - t // 2 + n_x) % n_x
        slots = jnp.where(dest % 2 == t % 2, n_x + away, away)

        bases, pairs = [], []

        def send_on(first, count, sends, keep, after):
            got = [core_swap(part) for part in sends[1:]] + [core_swap(sends[0])]
            pieces = [keep, got.pop()]
            n_piece = len(pieces_of(count))
            for k in range(1, n_x):
                pairs.append(pair_sum(keep, got[(k - 1) * n_piece : k * n_piece], k, after))
                pieces.append(chip_shift(pairs[-1], k))
            bases.append((first, count, pieces))

        def base(chunk):
            first, count = sum(BASE_CHUNKS[:chunk]), BASE_CHUNKS[chunk]
            return (first, count) + base_products(
                plan, hidden, split, first, count, prefill, pairs[-1:]
            )

        ranks = []
        count = requests // RANK_CHUNKS

        def rank(chunk, after):
            hops = chunk if by_distance else n_z - 1
            part = rank_products(
                plan, hidden, within(downs, hops), chunk * count, count, prefill, after
            )
            pair = (part.astype(F32) + core_swap(part).astype(F32)).astype(BF)
            pieces = [pair] + [chip_shift(pair, k) for k in range(1, n_x)]
            ranks.append((chunk * count, count, pieces))
            return part

        shape = (requests * prefill, 2, columns)

        def write(out, first, last):
            held = [
                b
                for b in bases
                if b[0] < last * count and b[0] + b[1] > first * count
            ]
            return finish(
                plan,
                held,
                ranks[first:last],
                within(downs, last - 1 if by_distance else n_z - 1),
                out,
                first * count,
                (last - first) * count,
                prefill,
                shape,
            )

        split, sends, keep = split_weight(
            plan, slots, hidden, weight, BASE_CHUNKS[0], prefill
        )
        send_on(0, BASE_CHUNKS[0], sends, keep, [])
        second = base(1)
        if n_z > 2:
            relay(2, [second[3]])
        send_on(*second, [bases[0][2][-1]])
        third = base(2)
        part = third[3]
        if by_distance:
            part = rank(0, [third[3], bases[1][2][-1]])
        send_on(*third, [part, bases[1][2][-1]])
        fourth = base(3)
        for hops in range(3, n_z):
            relay(hops, [fourth[3]])
        part = fourth[3]
        if by_distance:
            part = rank(1, [fourth[3], bases[2][2][-1]])
        send_on(*fourth, [part, bases[2][2][-1]])
        for chunk in range(len(ranks), 3):
            part = rank(chunk, [pairs[-1]])
        out = write(None, 0, 2)
        out = write(out, 2, 3)
        rank(3, [out])
        return write(out, 3, 4)

    return jax.shard_map(
        per_device,
        mesh=mesh,
        in_specs=(
            P(("group", "adapter"), "tensor"),
            P("tensor", None, None),
            P(("group", "adapter"), "tensor", None),
            P(("group", "adapter"), None, None, "tensor"),
            P("group"),
            P(("group", "adapter")),
            P(("group", "adapter")),
        ),
        out_specs=P(("group", "adapter"), None, "tensor"),
        check_vma=False,
    )
```

```python
import jax
import jax.numpy as jnp
from jax import lax
from jax.experimental import pallas as pl
from jax.experimental.pallas import tpu as pltpu
from jax.sharding import PartitionSpec as P

BF = jnp.bfloat16
F32 = jnp.float32
BASE_CHUNKS = (3, 3, 3, 3)
RANK_CHUNKS = 4
SMEM = pltpu.SMEM
PIECE = 2


def pieces_of(count):
    return [(at, min(PIECE, count - at)) for at in range(0, count, PIECE)]


ANY = pl.BlockSpec(memory_space=pl.ANY)


def cost(flops, moved):
    return pl.CostEstimate(
        flops=int(flops * 0.01), bytes_accessed=int(moved * 0.01), transcendentals=0
    )


ORDER, SOURCE, ROW, LENGTH = range(4)


def params(mib=60):
    return pltpu.CompilerParams(vmem_limit_bytes=mib * 1024 * 1024)


def pack_maps(down, up):
    stored, features, lanes = down.shape
    _, sides, depth, columns = up.shape
    tiles = columns // lanes
    part = sides * depth

    def body(down_ref, up_ref, o_ref, held, sems):
        copies = []
        for a in range(stored):
            copies.append(
                pltpu.make_async_copy(
                    down_ref.at[a], o_ref.at[a, pl.ds(0, features)], sems.at[0, a]
                )
            )
            copies[-1].start()
        for a in range(stored):
            flat = up_ref[a].reshape(part, columns)
            for j in range(tiles):
                held[a, j * part : (j + 1) * part] = flat[:, j * lanes : (j + 1) * lanes]
            copies.append(
                pltpu.make_async_copy(
                    held.at[a],
                    o_ref.at[a, pl.ds(features, tiles * part)],
                    sems.at[1, a],
                )
            )
            copies[-1].start()
        for copy in copies:
            copy.wait()

    return pl.pallas_call(
        body,
        out_shape=jax.ShapeDtypeStruct((stored, features + tiles * part, lanes), BF),
        in_specs=[pl.BlockSpec(memory_space=pltpu.VMEM)] * 2,
        out_specs=ANY,
        scratch_shapes=[
            pltpu.VMEM((stored, tiles * part, lanes), BF),
            pltpu.SemaphoreType.DMA((2, stored)),
        ],
        compiler_params=params(24),
        cost_estimate=cost(0, 4 * down.size),
        name="pack_maps",
    )(down, up)


def plan_requests(table, adapters, lengths, here, n_z, stored):
    requests, known = adapters.shape[0], table.shape[0]
    shape = (requests, 128)

    def body(table_ref, adapter_ref, length_ref, here_ref, plan_ref):
        me = here_ref[0]
        request = lax.broadcasted_iota(jnp.int32, shape, 0)
        lane = lax.broadcasted_iota(jnp.int32, shape, 1)
        diagonal = request == lane

        def wide(ref, n):
            return jnp.pad(ref[...], ((0, 0), (0, 128 - n)))

        def down(a):
            return jnp.sum(jnp.where(diagonal, a, 0), axis=1, keepdims=True)

        def across(a):
            return jnp.sum(jnp.where(diagonal, a, 0), axis=0, keepdims=True)

        hit = (down(wide(adapter_ref, requests)) == lane) & (lane < known)
        slot = jnp.sum(jnp.where(hit, wide(table_ref, known), 0), 1, keepdims=True)
        owner = jnp.zeros_like(slot)
        for z in range(1, n_z):
            owner += jnp.where(slot >= z * stored, 1, 0)
        source = jnp.where(owner >= me, owner - me, n_z - 1 + me - owner)
        key = jnp.abs(owner - me) * 128 + request[:, :1]
        before = (across(key) < key) & (lane < requests)
        place = jnp.sum(jnp.where(before, 1, 0), axis=1, keepdims=True)
        at = place == lane

        def placed(a):
            return jnp.sum(jnp.where(at, a, 0), axis=0, keepdims=True)

        plan_ref[ORDER : ORDER + 1] = placed(request)
        plan_ref[SOURCE : SOURCE + 1] = placed(source)
        plan_ref[ROW : ROW + 1] = placed(slot - owner * stored)
        plan_ref[LENGTH : LENGTH + 1] = placed(down(wide(length_ref, requests)))

    vmem = pl.BlockSpec(memory_space=pltpu.VMEM)
    return pl.pallas_call(
        body,
        out_shape=jax.ShapeDtypeStruct((8, 128), jnp.int32),
        in_specs=[vmem, vmem, vmem, pl.BlockSpec(memory_space=SMEM)],
        out_specs=vmem,
        cost_estimate=cost(0, 1 << 20),
        name="plan_requests",
    )(table[None, :], adapters[None, :], lengths[None, :], here)


def split_weight(plan, slots, hidden, weight, count, prefill):
    features, _, columns = weight.shape
    n_t = slots.shape[0]
    n_x = n_t // 2
    width = columns // n_t
    rows, half = 512, 128
    steps = features // rows

    def body(plan_ref, slot_ref, *rest):
        x_refs, (w_ref, o_ref, *send_refs, keep_ref, total) = rest[:count], rest[count:]
        step = pl.program_id(0)
        above = pl.multiple_of(step * rows, rows)
        out_row = lax.broadcasted_iota(jnp.int32, (2 * half, 2 * half), 0)
        in_row = lax.broadcasted_iota(jnp.int32, (2 * half, 2 * half), 1)
        pick = in_row == 2 * (out_row % half) + out_row // half
        pick = pick.astype(F32).astype(BF)
        for b in range(rows // half):
            mixed = w_ref[b * half : (b + 1) * half].reshape(2 * half, columns)
            apart = jnp.dot(pick, mixed, preferred_element_type=F32).astype(BF)
            for t in range(n_t):
                for s in range(2):
                    o_ref[
                        slot_ref[t],
                        pl.ds(above + b * half, half),
                        s * width : (s + 1) * width,
                    ] = apart[s * half : (s + 1) * half, t * width : (t + 1) * width]

        @pl.when(step == 0)
        def _():
            total[...] = jnp.zeros_like(total)

        for r in range(count):
            for j in range(n_t):
                total[j, r * prefill : (r + 1) * prefill] += jnp.dot(
                    x_refs[r][...], o_ref[j, pl.ds(above, rows)], preferred_element_type=F32
                )

        @pl.when(step == steps - 1)
        def _():
            send_refs[0][...] = total[0].astype(BF)
            k = 1
            for j in range(1, n_x):
                for at, n in pieces_of(count):
                    rows_of = slice(at * prefill, (at + n) * prefill)
                    send_refs[k][...] = total[j, rows_of].astype(BF)
                    k += 1
            for j in range(n_x):
                keep_ref[j] = total[n_x + j].astype(BF)

    part = (count * prefill, 2 * width)
    outs = [part] + [
        (n * prefill, 2 * width) for _, n in pieces_of(count)
    ] * (n_x - 1)
    split, *sends, keep = pl.pallas_call(
        body,
        out_shape=(
            jax.ShapeDtypeStruct((n_t, features, 2 * width), BF),
            *[jax.ShapeDtypeStruct(out, BF) for out in outs],
            jax.ShapeDtypeStruct((n_x, *part), BF),
        ),
        grid_spec=pltpu.PrefetchScalarGridSpec(
            num_scalar_prefetch=2,
            grid=(steps,),
            in_specs=[
                pl.BlockSpec((prefill, rows), lambda i, p, s, r=r: (p[ORDER, r], i))
                for r in range(count)
            ]
            + [pl.BlockSpec((rows, 2, columns), lambda i, p, s: (i, 0, 0))],
            out_specs=(
                pl.BlockSpec(memory_space=pltpu.VMEM),
                *[pl.BlockSpec(out, lambda i, p, s: (0, 0)) for out in outs],
                pl.BlockSpec((n_x, *part), lambda i, p, s: (0, 0, 0)),
            ),
            scratch_shapes=[pltpu.VMEM((n_t, count * prefill, 2 * width), F32)],
        ),
        compiler_params=params(46),
        cost_estimate=cost(2 * count * prefill * features * 2 * columns, 8 * features * columns),
        name="split_weight",
    )(plan, slots, *[hidden] * count, weight)
    return split, sends, keep


def base_products(plan, hidden, weight, first, count, prefill, after):
    n_t, features, width = weight.shape
    n_x = n_t // 2
    short = prefill // 2
    n_after = len(after)

    def body(plan_ref, x_ref, *rest):
        w_ref = rest[0]
        *send_refs, keep_ref = rest[1 + n_after :]
        live = plan_ref[LENGTH, first + pl.program_id(0)]

        def products(rows):
            dead = jnp.zeros((prefill - rows, width), BF)
            for j in range(n_t):
                out = jnp.dot(
                    x_ref[:rows], w_ref[j], preferred_element_type=F32
                ).astype(BF)
                if rows < prefill:
                    out = jnp.concatenate([out, dead], 0)
                if j == 0:
                    send_refs[0][...] = out
                elif j >= n_x:
                    keep_ref[j - n_x] = out
                else:

                    spans = pieces_of(count)
                    for k, (at, n) in enumerate(spans, 1 + (j - 1) * len(spans)):
                        inside = (pl.program_id(0) >= at) & (pl.program_id(0) < at + n)

                        @pl.when(inside)
                        def _():
                            send_refs[k][...] = out

        @pl.when(live > short)
        def _():
            products(prefill)

        @pl.when(live <= short)
        def _():
            products(short)

    spans = [(0, count)] + pieces_of(count) * (n_x - 1)
    parts = [n for _, n in spans]
    block = (prefill, width)
    places = [
        lambda i, p, at=at, n=n: (jnp.clip(i - at, 0, n - 1), 0) for at, n in spans
    ]
    *sends, keep = pl.pallas_call(
        body,
        out_shape=(
            *[jax.ShapeDtypeStruct((n * prefill, width), BF) for n in parts],
            jax.ShapeDtypeStruct((n_x, count * prefill, width), BF),
        ),
        grid_spec=pltpu.PrefetchScalarGridSpec(
            num_scalar_prefetch=1,
            grid=(count,),
            in_specs=[
                pl.BlockSpec(
                    (prefill, features), lambda i, p: (p[ORDER, first + i], 0)
                ),
            ]
            + [pl.BlockSpec(memory_space=pltpu.VMEM)]
            + [ANY] * n_after,
            out_specs=(
                *[pl.BlockSpec(block, place) for place in places],
                pl.BlockSpec((n_x, prefill, width), lambda i, p: (0, i, 0)),
            ),
        ),
        compiler_params=params(46),
        cost_estimate=cost(2 * count * prefill * features * width * n_t, 2 * n_t * features * width),
        name="base_products",
    )(plan, hidden, weight, *after)
    return sends, keep


def pair_sum(one, others, index, after):
    _, rows, width = one.shape
    n_piece = len(others)

    def body(a_ref, *rest):
        b_refs = rest[:n_piece]
        o_ref, mine, theirs, total, sems, out_sems = rest[n_piece + len(after) :]
        copies, outs = [], []
        spans, at = [], 0
        for b_ref in b_refs:
            spans.append(pl.ds(at, b_ref.shape[0]))
            at += b_ref.shape[0]
        for k, span in enumerate(spans):
            copies.append(
                (
                    pltpu.make_async_copy(
                        a_ref.at[index, span], mine.at[span], sems.at[0, k]
                    ),
                    pltpu.make_async_copy(b_refs[k], theirs.at[span], sems.at[1, k]),
                )
            )
            for copy in copies[-1]:
                copy.start()
        for k, span in enumerate(spans):
            for copy in copies[k]:
                copy.wait()
            value = mine[span].astype(F32) + theirs[span].astype(F32)
            total[span] = value.astype(BF)
            outs.append(
                pltpu.make_async_copy(total.at[span], o_ref.at[span], out_sems.at[k])
            )
            outs[-1].start()
        for copy in outs:
            copy.wait()

    return pl.pallas_call(
        body,
        out_shape=jax.ShapeDtypeStruct((rows, width), BF),
        in_specs=[ANY] * (1 + n_piece + len(after)),
        out_specs=ANY,
        scratch_shapes=[pltpu.VMEM((rows, width), BF)] * 3
        + [pltpu.SemaphoreType.DMA((2, n_piece)), pltpu.SemaphoreType.DMA((n_piece,))],
        compiler_params=params(12),
        cost_estimate=cost(rows * width, 6 * rows * width),
        name="pair_sum",
    )(one, *others, *after)


def hold(arrays, after):
    n = len(arrays)

    def body(*refs):
        pass

    return pl.pallas_call(
        body,
        out_shape=[jax.ShapeDtypeStruct(a.shape, a.dtype) for a in arrays],
        in_specs=[ANY] * (n + len(after)),
        out_specs=[ANY] * n,
        input_output_aliases={i: i for i in range(n)},
        compiler_params=params(8),
        cost_estimate=cost(0, 1 << 20),
        name="hold",
    )(*arrays, *after)


def fetch(refs, source, row, part, target, sem):
    for codes, ref in refs:
        hit = source == codes[0]
        for code in codes[1:]:
            hit |= source == code

        @pl.when(hit)
        def _():
            pltpu.make_async_copy(ref.at[row, part], target, sem).start()


def rank_products(plan, hidden, maps, first, count, prefill, after):
    sources = list(maps)
    features, ranks = hidden.shape[1], maps[sources[0]].shape[2]
    n_map, n_after = len(maps), len(after)
    short = prefill // 2
    down = pl.ds(0, features)

    def body(plan_ref, x_ref, *rest):
        refs = list(zip(sources, rest[:n_map]))
        o_ref, rows, held, sems = rest[n_map + n_after :]
        copies = []
        for i in range(count):
            fetch(
                refs,
                plan_ref[SOURCE, first + i],
                plan_ref[ROW, first + i],
                down,
                held.at[i],
                sems.at[0, i],
            )
            at = pl.multiple_of(plan_ref[ORDER, first + i] * prefill, prefill)
            copies.append(
                pltpu.make_async_copy(
                    x_ref.at[pl.ds(at, prefill)], rows.at[i], sems.at[1, i]
                )
            )
            copies[-1].start()
        for i in range(count):
            pltpu.make_async_copy(
                rest[0].at[0, down], held.at[i], sems.at[0, i]
            ).wait()
            copies[i].wait()
            live = plan_ref[LENGTH, first + i]
            above, below = i * prefill, i * prefill + short

            @pl.when(live > short)
            def _():
                o_ref[above : above + prefill] = jnp.dot(
                    rows[i], held[i], preferred_element_type=F32
                ).astype(BF)

            @pl.when(live <= short)
            def _():
                o_ref[above:below] = jnp.dot(
                    rows[i, :short], held[i], preferred_element_type=F32
                ).astype(BF)
                o_ref[below : below + short] = jnp.zeros((short, ranks), BF)

    return pl.pallas_call(
        body,
        out_shape=jax.ShapeDtypeStruct((count * prefill, ranks), BF),
        grid_spec=pltpu.PrefetchScalarGridSpec(
            num_scalar_prefetch=1,
            grid=(),
            in_specs=[ANY] * (1 + n_map + n_after),
            out_specs=pl.BlockSpec(memory_space=pltpu.VMEM),
            scratch_shapes=[
                pltpu.VMEM((count, prefill, features), BF),
                pltpu.VMEM((count, features, ranks), BF),
                pltpu.SemaphoreType.DMA((2, count)),
            ],
        ),
        compiler_params=params(16),
        cost_estimate=cost(2 * count * prefill * features * ranks, 2 * count * features * (prefill + ranks)),
        name="rank_products",
    )(plan, hidden, *maps.values(), *after)


def finish(plan, bases, ranks, maps, before, first, count, prefill, shape):
    sources = list(maps)
    columns, depth = shape[2], ranks[0][2][0].shape[1] // 2
    _, packed, lanes = maps[sources[0]].shape
    tiles = columns // lanes
    extra = tiles * 2 * depth
    up_part = pl.ds(packed - extra, extra)
    half = prefill // 2
    n_map = len(maps)
    n_base = max(len(pieces) for _, _, pieces in bases)
    n_rank = max(len(pieces) for _, _, pieces in ranks)

    def body(plan_ref, *rest):
        base_refs, rank_refs = [], []
        for refs, pieces in ((base_refs, bases), (rank_refs, ranks)):
            for start, n, arrays in pieces:
                refs.append((start, n, rest[: len(arrays)]))
                rest = rest[len(arrays) :]
        map_refs = list(zip(sources, rest[:n_map]))
        o_ref, ups, base_rows, rank_rows, out_rows, sems, out_sems = rest[-7:]

        def start_pieces(refs, at, rows, sem):
            copies = []
            for start, n, arrays in refs:
                if start <= at < start + n:
                    block = pl.ds((at - start) * prefill, prefill)
                    for k, ref in enumerate(arrays):
                        source = ref.at[0, block] if len(ref.shape) == 3 else ref.at[block]
                        copies.append(pltpu.make_async_copy(source, rows.at[k], sem.at[k]))
                        copies[-1].start()
            return copies

        copies = []
        for i in range(count):
            at = first + i
            copies.append(
                start_pieces(base_refs, at, base_rows.at[i], sems.at[i])
                + start_pieces(
                    rank_refs, at, rank_rows.at[i], sems.at[i, pl.ds(n_base, n_rank)]
                )
            )
            fetch(
                map_refs,
                plan_ref[SOURCE, at],
                plan_ref[ROW, at],
                up_part,
                ups.at[i],
                sems.at[i, n_base + n_rank],
            )

        group = half // tiles
        mix_row = lax.broadcasted_iota(jnp.int32, (2 * half, 2 * half), 0)
        mix_column = lax.broadcasted_iota(jnp.int32, (2 * half, 2 * half), 1)
        mix_token, mix_tile = mix_row // (2 * tiles), mix_row // 2 % tiles
        mix = mix_column == (mix_row % 2 * tiles + mix_tile) * group + mix_token
        mix = mix.astype(F32).astype(BF)
        token = lax.broadcasted_iota(jnp.int32, (half, 2 * columns), 0)

        def rows_for(i, live, b):
            rows = slice(b * half, (b + 1) * half)
            rank = rank_rows[i, 0, rows].astype(F32)
            for k in range(1, n_rank):
                rank += rank_rows[i, k, rows].astype(F32)
            rank = rank.astype(BF)
            up = jnp.concatenate(
                [ups[i, j * 2 * depth : (j + 1) * 2 * depth] for j in range(tiles)], 1
            )
            total = jnp.concatenate(
                [
                    jnp.dot(
                        rank[:, s * depth : (s + 1) * depth],
                        up[s * depth : (s + 1) * depth],
                        preferred_element_type=F32,
                    )
                    for s in range(2)
                ],
                1,
            )
            for k in range(n_base):
                total += base_rows[i, k, rows].astype(F32)
            total = jnp.where(token + b * half < live, total, 0.0).astype(BF)
            parts = [
                jnp.concatenate(
                    [
                        total[g * group : (g + 1) * group, k * lanes : (k + 1) * lanes]
                        for k in range(2 * tiles)
                    ],
                    0,
                )
                for g in range(tiles)
            ]
            mixed = jnp.dot(
                mix, jnp.concatenate(parts, 1), preferred_element_type=F32
            ).astype(BF)
            for g in range(tiles):
                at = b * half * tiles + g * half
                out_rows[i, at : at + half] = mixed[
                    :, g * lanes : (g + 1) * lanes
                ].reshape(half, 2, lanes)

        outs = []
        for i in range(count):
            for copy in copies[i]:
                copy.wait()
            pltpu.make_async_copy(
                map_refs[0][1].at[0, up_part], ups.at[i], sems.at[i, n_base + n_rank]
            ).wait()
            live = plan_ref[LENGTH, first + i]
            rows_for(i, live, 0)

            @pl.when(live > half)
            def _():
                rows_for(i, live, 1)

            @pl.when(live <= half)
            def _():
                out_rows[i, half * tiles :] = jnp.zeros((half * tiles, 2, lanes), BF)

            block = prefill * tiles
            row = pl.multiple_of(plan_ref[ORDER, first + i] * block, block)
            outs.append(
                pltpu.make_async_copy(
                    out_rows.at[i], o_ref.at[pl.ds(row, block)], out_sems.at[i]
                )
            )
            outs[-1].start()
        for copy in outs:
            copy.wait()

    operands = [plan]
    for _, _, pieces in bases + ranks:
        operands += pieces
    operands += maps.values()
    aliases = {}
    if before is not None:
        aliases = {len(operands): 0}
        operands.append(before)
    return pl.pallas_call(
        body,
        out_shape=jax.ShapeDtypeStruct((shape[0] * tiles, 2, lanes), BF),
        grid_spec=pltpu.PrefetchScalarGridSpec(
            num_scalar_prefetch=1,
            grid=(),
            in_specs=[ANY] * (len(operands) - 1),
            out_specs=ANY,
            scratch_shapes=[
                pltpu.VMEM((count, extra, lanes), BF),
                pltpu.VMEM((count, n_base, prefill, 2 * columns), BF),
                pltpu.VMEM((count, n_rank, prefill, 2 * depth), BF),
                pltpu.VMEM((count, prefill * tiles, 2, lanes), BF),
                pltpu.SemaphoreType.DMA((count, n_base + n_rank + 1)),
                pltpu.SemaphoreType.DMA((count,)),
            ],
        ),
        input_output_aliases=aliases,
        compiler_params=params(60),
        cost_estimate=cost(12 * count * prefill * prefill * 2 * columns, 20 * count * prefill * columns),
        name="finish",
    )(*operands)


def solution(mesh):
    n_z, n_t = mesh.shape["adapter"], mesh.shape["tensor"]
    n_x = n_t // 2

    def core_swap(a):
        return lax.ppermute(a, "tensor", [(t, t ^ 1) for t in range(n_t)])

    def chip_shift(a, k):
        return lax.ppermute(
            a,
            "tensor",
            [(2 * x + c, 2 * ((x + k) % n_x) + c) for x in range(n_x) for c in (0, 1)],
        )

    def leftward(a, hops=1):
        return lax.ppermute(a, "adapter", [(z, z - hops) for z in range(hops, n_z)])

    def rightward(a, hops=1):
        return lax.ppermute(a, "adapter", [(z - hops, z) for z in range(hops, n_z)])

    def per_device(hidden, weight, down, up, table, adapters, lengths):
        requests = adapters.shape[0]
        prefill = hidden.shape[0] // requests
        stored = down.shape[0]
        columns = up.shape[3]
        by_distance = n_z == RANK_CHUNKS
        z, t = lax.axis_index("adapter"), lax.axis_index("tensor")
        plan = plan_requests(
            table, adapters, lengths, jnp.reshape(z, (1,)), n_z, stored
        )

        downs = {0: pack_maps(down, up)}

        def relay(hops, after):
            left, right = downs[hops - 1], downs[0 if hops == 1 else n_z + hops - 2]
            if after:
                left, right = hold([left, right], after)
                downs[hops - 1], downs[n_z + hops - 2] = left, right
            downs[hops] = leftward(left)
            downs[n_z - 1 + hops] = rightward(right)

        relay(1, [])

        def within(maps, hops):
            keys = range(hops + 1), range(n_z, n_z + hops)
            return {(k,): maps[k] for part in keys for k in part}

        dest = jnp.arange(n_t, dtype=jnp.int32)
        away = (dest // 2 - t // 2 + n_x) % n_x
        slots = jnp.where(dest % 2 == t % 2, n_x + away, away)

        bases, pairs = [], []

        def send_on(first, count, sends, keep, after):
            got = [core_swap(part) for part in sends[1:]] + [core_swap(sends[0])]
            pieces = [keep, got.pop()]
            n_piece = len(pieces_of(count))
            for k in range(1, n_x):
                pairs.append(pair_sum(keep, got[(k - 1) * n_piece : k * n_piece], k, after))
                pieces.append(chip_shift(pairs[-1], k))
            bases.append((first, count, pieces))

        def base(chunk):
            first, count = sum(BASE_CHUNKS[:chunk]), BASE_CHUNKS[chunk]
            return (first, count) + base_products(
                plan, hidden, split, first, count, prefill, pairs[-1:]
            )

        ranks = []
        count = requests // RANK_CHUNKS

        def rank(chunk, after):
            hops = chunk if by_distance else n_z - 1
            part = rank_products(
                plan, hidden, within(downs, hops), chunk * count, count, prefill, after
            )
            pair = (part.astype(F32) + core_swap(part).astype(F32)).astype(BF)
            pieces = [pair] + [chip_shift(pair, k) for k in range(1, n_x)]
            ranks.append((chunk * count, count, pieces))
            return part

        shape = (requests * prefill, 2, columns)

        def write(out, first, last):
            held = [
                b
                for b in bases
                if b[0] < last * count and b[0] + b[1] > first * count
            ]
            return finish(
                plan,
                held,
                ranks[first:last],
                within(downs, last - 1 if by_distance else n_z - 1),
                out,
                first * count,
                (last - first) * count,
                prefill,
                shape,
            )

        split, sends, keep = split_weight(
            plan, slots, hidden, weight, BASE_CHUNKS[0], prefill
        )
        send_on(0, BASE_CHUNKS[0], sends, keep, [])
        second = base(1)
        if n_z > 2:
            relay(2, [second[3]])
        send_on(*second, [bases[0][2][-1]])
        third = base(2)
        part = third[3]
        if by_distance:
            part = rank(0, [third[3], bases[1][2][-1]])
        send_on(*third, [part, bases[1][2][-1]])
        fourth = base(3)
        for hops in range(3, n_z):
            relay(hops, [fourth[3]])
        part = fourth[3]
        if by_distance:
            part = rank(1, [fourth[3], bases[2][2][-1]])
        send_on(*fourth, [part, bases[2][2][-1]])
        for chunk in range(len(ranks), 3):
            part = rank(chunk, [pairs[-1]])
        out = write(None, 0, 2)
        out = write(out, 2, 3)
        rank(3, [out])
        out = write(out, 3, 4)
        tiles = out.shape[0] // shape[0]
        out = out.reshape(shape[0], tiles, 2, columns // tiles)
        return out.transpose(0, 2, 1, 3).reshape(shape)

    return jax.shard_map(
        per_device,
        mesh=mesh,
        in_specs=(
            P(("group", "adapter"), "tensor"),
            P("tensor", None, None),
            P(("group", "adapter"), "tensor", None),
            P(("group", "adapter"), None, None, "tensor"),
            P("group"),
            P(("group", "adapter")),
            P(("group", "adapter")),
        ),
        out_specs=P(("group", "adapter"), None, "tensor"),
        check_vma=False,
    )
```

```python
import jax
import jax.numpy as jnp
from jax import lax
from jax.experimental import pallas as pl
from jax.experimental.pallas import tpu as pltpu
from jax.sharding import PartitionSpec as P

BF = jnp.bfloat16
F32 = jnp.float32
BASE_CHUNKS = (3, 3, 4, 2)
RANK_CHUNKS = 4
SMEM = pltpu.SMEM
PIECE = 2


def pieces_of(count):
    return [(at, min(PIECE, count - at)) for at in range(0, count, PIECE)]


ANY = pl.BlockSpec(memory_space=pl.ANY)
HBM = pl.BlockSpec(memory_space=pltpu.HBM)


def cost(flops, moved):
    return pl.CostEstimate(
        flops=int(flops * 0.01), bytes_accessed=int(moved * 0.01), transcendentals=0
    )


ORDER, SOURCE, ROW, LENGTH = range(4)


def params(mib=60):
    return pltpu.CompilerParams(vmem_limit_bytes=mib * 1024 * 1024)


def pack_maps(down, up):
    stored, features, lanes = down.shape
    _, sides, depth, columns = up.shape
    tiles = columns // lanes
    part = sides * depth

    def body(down_ref, up_ref, o_ref, held, sems):
        copies = []
        for a in range(stored):
            copies.append(
                pltpu.make_async_copy(
                    down_ref.at[a], o_ref.at[a, pl.ds(0, features)], sems.at[0, a]
                )
            )
            copies[-1].start()
        for a in range(stored):
            flat = up_ref[a].reshape(part, columns)
            for j in range(tiles):
                held[a, j * part : (j + 1) * part] = flat[:, j * lanes : (j + 1) * lanes]
            copies.append(
                pltpu.make_async_copy(
                    held.at[a],
                    o_ref.at[a, pl.ds(features, tiles * part)],
                    sems.at[1, a],
                )
            )
            copies[-1].start()
        for copy in copies:
            copy.wait()

    return pl.pallas_call(
        body,
        out_shape=jax.ShapeDtypeStruct((stored, features + tiles * part, lanes), BF),
        in_specs=[pl.BlockSpec(memory_space=pltpu.VMEM)] * 2,
        out_specs=HBM,
        scratch_shapes=[
            pltpu.VMEM((stored, tiles * part, lanes), BF),
            pltpu.SemaphoreType.DMA((2, stored)),
        ],
        compiler_params=params(24),
        cost_estimate=cost(0, 4 * down.size),
        name="pack_maps",
    )(down, up)


def plan_requests(table, adapters, lengths, here, n_z, stored):
    requests, known = adapters.shape[0], table.shape[0]
    shape = (requests, 128)

    def body(table_ref, adapter_ref, length_ref, here_ref, plan_ref):
        me = here_ref[0]
        request = lax.broadcasted_iota(jnp.int32, shape, 0)
        lane = lax.broadcasted_iota(jnp.int32, shape, 1)
        diagonal = request == lane

        def wide(ref, n):
            return jnp.pad(ref[...], ((0, 0), (0, 128 - n)))

        def down(a):
            return jnp.sum(jnp.where(diagonal, a, 0), axis=1, keepdims=True)

        def across(a):
            return jnp.sum(jnp.where(diagonal, a, 0), axis=0, keepdims=True)

        hit = (down(wide(adapter_ref, requests)) == lane) & (lane < known)
        slot = jnp.sum(jnp.where(hit, wide(table_ref, known), 0), 1, keepdims=True)
        owner = jnp.zeros_like(slot)
        for z in range(1, n_z):
            owner += jnp.where(slot >= z * stored, 1, 0)
        source = jnp.where(owner >= me, owner - me, n_z - 1 + me - owner)
        key = jnp.abs(owner - me) * 128 + request[:, :1]
        before = (across(key) < key) & (lane < requests)
        place = jnp.sum(jnp.where(before, 1, 0), axis=1, keepdims=True)
        at = place == lane

        def placed(a):
            return jnp.sum(jnp.where(at, a, 0), axis=0, keepdims=True)

        plan_ref[ORDER : ORDER + 1] = placed(request)
        plan_ref[SOURCE : SOURCE + 1] = placed(source)
        plan_ref[ROW : ROW + 1] = placed(slot - owner * stored)
        plan_ref[LENGTH : LENGTH + 1] = placed(down(wide(length_ref, requests)))

    vmem = pl.BlockSpec(memory_space=pltpu.VMEM)
    return pl.pallas_call(
        body,
        out_shape=jax.ShapeDtypeStruct((8, 128), jnp.int32),
        in_specs=[vmem, vmem, vmem, pl.BlockSpec(memory_space=SMEM)],
        out_specs=vmem,
        cost_estimate=cost(0, 1 << 20),
        name="plan_requests",
    )(table[None, :], adapters[None, :], lengths[None, :], here)


def split_weight(plan, slots, hidden, weight, count, prefill):
    features, _, columns = weight.shape
    n_t = slots.shape[0]
    n_x = n_t // 2
    width = columns // n_t
    rows, half = 512, 128
    steps = features // rows

    def body(plan_ref, slot_ref, *rest):
        x_refs, (w_ref, o_ref, *send_refs, keep_ref, total) = rest[:count], rest[count:]
        step = pl.program_id(0)
        above = pl.multiple_of(step * rows, rows)
        out_row = lax.broadcasted_iota(jnp.int32, (2 * half, 2 * half), 0)
        in_row = lax.broadcasted_iota(jnp.int32, (2 * half, 2 * half), 1)
        pick = in_row == 2 * (out_row % half) + out_row // half
        pick = pick.astype(F32).astype(BF)
        for b in range(rows // half):
            mixed = w_ref[b * half : (b + 1) * half].reshape(2 * half, columns)
            apart = jnp.dot(pick, mixed, preferred_element_type=F32).astype(BF)
            for t in range(n_t):
                for s in range(2):
                    o_ref[
                        slot_ref[t],
                        pl.ds(above + b * half, half),
                        s * width : (s + 1) * width,
                    ] = apart[s * half : (s + 1) * half, t * width : (t + 1) * width]

        @pl.when(step == 0)
        def _():
            total[...] = jnp.zeros_like(total)

        for r in range(count):
            for j in range(n_t):
                total[j, r * prefill : (r + 1) * prefill] += jnp.dot(
                    x_refs[r][...], o_ref[j, pl.ds(above, rows)], preferred_element_type=F32
                )

        @pl.when(step == steps - 1)
        def _():
            send_refs[0][...] = total[0].astype(BF)
            k = 1
            for j in range(1, n_x):
                for at, n in pieces_of(count):
                    rows_of = slice(at * prefill, (at + n) * prefill)
                    send_refs[k][...] = total[j, rows_of].astype(BF)
                    k += 1
            for j in range(n_x):
                keep_ref[j] = total[n_x + j].astype(BF)

    part = (count * prefill, 2 * width)
    outs = [part] + [
        (n * prefill, 2 * width) for _, n in pieces_of(count)
    ] * (n_x - 1)
    split, *sends, keep = pl.pallas_call(
        body,
        out_shape=(
            jax.ShapeDtypeStruct((n_t, features, 2 * width), BF),
            *[jax.ShapeDtypeStruct(out, BF) for out in outs],
            jax.ShapeDtypeStruct((n_x, *part), BF),
        ),
        grid_spec=pltpu.PrefetchScalarGridSpec(
            num_scalar_prefetch=2,
            grid=(steps,),
            in_specs=[
                pl.BlockSpec((prefill, rows), lambda i, p, s, r=r: (p[ORDER, r], i))
                for r in range(count)
            ]
            + [pl.BlockSpec((rows, 2, columns), lambda i, p, s: (i, 0, 0))],
            out_specs=(
                pl.BlockSpec(memory_space=pltpu.VMEM),
                *[pl.BlockSpec(out, lambda i, p, s: (0, 0)) for out in outs],
                pl.BlockSpec((n_x, *part), lambda i, p, s: (0, 0, 0)),
            ),
            scratch_shapes=[pltpu.VMEM((n_t, count * prefill, 2 * width), F32)],
        ),
        compiler_params=params(46),
        cost_estimate=cost(2 * count * prefill * features * 2 * columns, 8 * features * columns),
        name="split_weight",
    )(plan, slots, *[hidden] * count, weight)
    return split, sends, keep


def base_products(plan, hidden, weight, first, count, prefill, after):
    n_t, features, width = weight.shape
    n_x = n_t // 2
    short = prefill // 2
    n_after = len(after)

    def body(plan_ref, x_ref, *rest):
        w_ref = rest[0]
        *send_refs, keep_ref = rest[1 + n_after :]
        live = plan_ref[LENGTH, first + pl.program_id(0)]

        def products(rows):
            dead = jnp.zeros((prefill - rows, width), BF)
            for j in range(n_t):
                out = jnp.dot(
                    x_ref[:rows], w_ref[j], preferred_element_type=F32
                ).astype(BF)
                if rows < prefill:
                    out = jnp.concatenate([out, dead], 0)
                if j == 0:
                    send_refs[0][...] = out
                elif j >= n_x:
                    keep_ref[j - n_x] = out
                else:

                    spans = pieces_of(count)
                    for k, (at, n) in enumerate(spans, 1 + (j - 1) * len(spans)):
                        inside = (pl.program_id(0) >= at) & (pl.program_id(0) < at + n)

                        @pl.when(inside)
                        def _():
                            send_refs[k][...] = out

        @pl.when(live > short)
        def _():
            products(prefill)

        @pl.when(live <= short)
        def _():
            products(short)

    spans = [(0, count)] + pieces_of(count) * (n_x - 1)
    parts = [n for _, n in spans]
    block = (prefill, width)
    places = [
        lambda i, p, at=at, n=n: (jnp.clip(i - at, 0, n - 1), 0) for at, n in spans
    ]
    *sends, keep = pl.pallas_call(
        body,
        out_shape=(
            *[jax.ShapeDtypeStruct((n * prefill, width), BF) for n in parts],
            jax.ShapeDtypeStruct((n_x, count * prefill, width), BF),
        ),
        grid_spec=pltpu.PrefetchScalarGridSpec(
            num_scalar_prefetch=1,
            grid=(count,),
            in_specs=[
                pl.BlockSpec(
                    (prefill, features), lambda i, p: (p[ORDER, first + i], 0)
                ),
            ]
            + [pl.BlockSpec(memory_space=pltpu.VMEM)]
            + [ANY] * n_after,
            out_specs=(
                *[pl.BlockSpec(block, place) for place in places],
                pl.BlockSpec((n_x, prefill, width), lambda i, p: (0, i, 0)),
            ),
        ),
        compiler_params=params(46),
        cost_estimate=cost(2 * count * prefill * features * width * n_t, 2 * n_t * features * width),
        name="base_products",
    )(plan, hidden, weight, *after)
    return sends, keep


def pair_sum(one, others, index, after):
    _, rows, width = one.shape
    n_piece = len(others)

    def body(a_ref, *rest):
        b_refs = rest[:n_piece]
        o_ref, mine, theirs, total, sems, out_sems = rest[n_piece + len(after) :]
        copies, outs = [], []
        spans, at = [], 0
        for b_ref in b_refs:
            spans.append(pl.ds(at, b_ref.shape[0]))
            at += b_ref.shape[0]
        for k, span in enumerate(spans):
            copies.append(
                (
                    pltpu.make_async_copy(
                        a_ref.at[index, span], mine.at[span], sems.at[0, k]
                    ),
                    pltpu.make_async_copy(b_refs[k], theirs.at[span], sems.at[1, k]),
                )
            )
            for copy in copies[-1]:
                copy.start()
        for k, span in enumerate(spans):
            for copy in copies[k]:
                copy.wait()
            value = mine[span].astype(F32) + theirs[span].astype(F32)
            total[span] = value.astype(BF)
            outs.append(
                pltpu.make_async_copy(total.at[span], o_ref.at[span], out_sems.at[k])
            )
            outs[-1].start()
        for copy in outs:
            copy.wait()

    return pl.pallas_call(
        body,
        out_shape=jax.ShapeDtypeStruct((rows, width), BF),
        in_specs=[ANY] * (1 + n_piece + len(after)),
        out_specs=ANY,
        scratch_shapes=[pltpu.VMEM((rows, width), BF)] * 3
        + [pltpu.SemaphoreType.DMA((2, n_piece)), pltpu.SemaphoreType.DMA((n_piece,))],
        compiler_params=params(12),
        cost_estimate=cost(rows * width, 6 * rows * width),
        name="pair_sum",
    )(one, *others, *after)


def hold(arrays, after):
    n = len(arrays)

    def body(*refs):
        pass

    return pl.pallas_call(
        body,
        out_shape=[jax.ShapeDtypeStruct(a.shape, a.dtype) for a in arrays],
        in_specs=[HBM] * (n + len(after)),
        out_specs=[HBM] * n,
        input_output_aliases={i: i for i in range(n)},
        compiler_params=params(8),
        cost_estimate=cost(0, 1 << 20),
        name="hold",
    )(*arrays, *after)


def fetch(refs, source, row, part, target, sem):
    for codes, ref in refs:
        hit = source == codes[0]
        for code in codes[1:]:
            hit |= source == code

        @pl.when(hit)
        def _():
            pltpu.make_async_copy(ref.at[row, part], target, sem).start()


def rank_products(plan, hidden, maps, first, count, prefill, after):
    sources = list(maps)
    features, ranks = hidden.shape[1], maps[sources[0]].shape[2]
    n_map, n_after = len(maps), len(after)
    short = prefill // 2
    down = pl.ds(0, features)

    def body(plan_ref, x_ref, *rest):
        refs = list(zip(sources, rest[:n_map]))
        o_ref, rows, held, sems = rest[n_map + n_after :]
        copies = []
        for i in range(count):
            fetch(
                refs,
                plan_ref[SOURCE, first + i],
                plan_ref[ROW, first + i],
                down,
                held.at[i],
                sems.at[0, i],
            )
            at = pl.multiple_of(plan_ref[ORDER, first + i] * prefill, prefill)
            copies.append(
                pltpu.make_async_copy(
                    x_ref.at[pl.ds(at, prefill)], rows.at[i], sems.at[1, i]
                )
            )
            copies[-1].start()
        for i in range(count):
            pltpu.make_async_copy(
                rest[0].at[0, down], held.at[i], sems.at[0, i]
            ).wait()
            copies[i].wait()
            live = plan_ref[LENGTH, first + i]
            above, below = i * prefill, i * prefill + short

            @pl.when(live > short)
            def _():
                o_ref[above : above + prefill] = jnp.dot(
                    rows[i], held[i], preferred_element_type=F32
                ).astype(BF)

            @pl.when(live <= short)
            def _():
                o_ref[above:below] = jnp.dot(
                    rows[i, :short], held[i], preferred_element_type=F32
                ).astype(BF)
                o_ref[below : below + short] = jnp.zeros((short, ranks), BF)

    return pl.pallas_call(
        body,
        out_shape=jax.ShapeDtypeStruct((count * prefill, ranks), BF),
        grid_spec=pltpu.PrefetchScalarGridSpec(
            num_scalar_prefetch=1,
            grid=(),
            in_specs=[HBM] * (1 + n_map + n_after),
            out_specs=pl.BlockSpec(memory_space=pltpu.VMEM),
            scratch_shapes=[
                pltpu.VMEM((count, prefill, features), BF),
                pltpu.VMEM((count, features, ranks), BF),
                pltpu.SemaphoreType.DMA((2, count)),
            ],
        ),
        compiler_params=params(16),
        cost_estimate=cost(2 * count * prefill * features * ranks, 2 * count * features * (prefill + ranks)),
        name="rank_products",
    )(plan, hidden, *maps.values(), *after)


def finish(plan, bases, ranks, maps, before, first, count, prefill, shape):
    sources = list(maps)
    columns, depth = shape[2], ranks[0][2][0].shape[1] // 2
    _, packed, lanes = maps[sources[0]].shape
    tiles = columns // lanes
    extra = tiles * 2 * depth
    up_part = pl.ds(packed - extra, extra)
    half = prefill // 2
    n_map = len(maps)
    n_base = max(len(pieces) for _, _, pieces in bases)
    n_rank = max(len(pieces) for _, _, pieces in ranks)

    def body(plan_ref, *rest):
        base_refs, rank_refs = [], []
        for refs, pieces in ((base_refs, bases), (rank_refs, ranks)):
            for start, n, arrays in pieces:
                refs.append((start, n, rest[: len(arrays)]))
                rest = rest[len(arrays) :]
        map_refs = list(zip(sources, rest[:n_map]))
        o_ref, token_ref, ups, base_rows, rank_rows, out_rows, sems, out_sems = rest[-8:]
        token_ref[...] = jnp.zeros_like(token_ref)

        def start_pieces(refs, at, rows, sem):
            copies = []
            for start, n, arrays in refs:
                if start <= at < start + n:
                    block = pl.ds((at - start) * prefill, prefill)
                    for k, ref in enumerate(arrays):
                        source = ref.at[0, block] if len(ref.shape) == 3 else ref.at[block]
                        copies.append(pltpu.make_async_copy(source, rows.at[k], sem.at[k]))
                        copies[-1].start()
            return copies

        copies = []
        for i in range(count):
            at = first + i
            copies.append(
                start_pieces(base_refs, at, base_rows.at[i], sems.at[i])
                + start_pieces(
                    rank_refs, at, rank_rows.at[i], sems.at[i, pl.ds(n_base, n_rank)]
                )
            )
            fetch(
                map_refs,
                plan_ref[SOURCE, at],
                plan_ref[ROW, at],
                up_part,
                ups.at[i],
                sems.at[i, n_base + n_rank],
            )

        group = half // tiles
        mix_row = lax.broadcasted_iota(jnp.int32, (2 * half, 2 * half), 0)
        mix_column = lax.broadcasted_iota(jnp.int32, (2 * half, 2 * half), 1)
        mix_token, mix_tile = mix_row // (2 * tiles), mix_row // 2 % tiles
        mix = mix_column == (mix_row % 2 * tiles + mix_tile) * group + mix_token
        mix = mix.astype(F32).astype(BF)
        token = lax.broadcasted_iota(jnp.int32, (half, 2 * columns), 0)

        def rows_for(i, live, b):
            rows = slice(b * half, (b + 1) * half)
            rank = rank_rows[i, 0, rows].astype(F32)
            for k in range(1, n_rank):
                rank += rank_rows[i, k, rows].astype(F32)
            rank = rank.astype(BF)
            up = jnp.concatenate(
                [ups[i, j * 2 * depth : (j + 1) * 2 * depth] for j in range(tiles)], 1
            )
            total = jnp.concatenate(
                [
                    jnp.dot(
                        rank[:, s * depth : (s + 1) * depth],
                        up[s * depth : (s + 1) * depth],
                        preferred_element_type=F32,
                    )
                    for s in range(2)
                ],
                1,
            )
            for k in range(n_base):
                total += base_rows[i, k, rows].astype(F32)
            total = jnp.where(token + b * half < live, total, 0.0).astype(BF)
            parts = [
                jnp.concatenate(
                    [
                        total[g * group : (g + 1) * group, k * lanes : (k + 1) * lanes]
                        for k in range(2 * tiles)
                    ],
                    0,
                )
                for g in range(tiles)
            ]
            mixed = jnp.dot(
                mix, jnp.concatenate(parts, 1), preferred_element_type=F32
            ).astype(BF)
            for g in range(tiles):
                at = b * half * tiles + g * half
                out_rows[i, at : at + half] = mixed[
                    :, g * lanes : (g + 1) * lanes
                ].reshape(half, 2, lanes)

        outs = []
        for i in range(count):
            for copy in copies[i]:
                copy.wait()
            pltpu.make_async_copy(
                map_refs[0][1].at[0, up_part], ups.at[i], sems.at[i, n_base + n_rank]
            ).wait()
            live = plan_ref[LENGTH, first + i]
            rows_for(i, live, 0)

            @pl.when(live > half)
            def _():
                rows_for(i, live, 1)

            @pl.when(live <= half)
            def _():
                out_rows[i, half * tiles :] = jnp.zeros((half * tiles, 2, lanes), BF)

            block = prefill * tiles
            row = pl.multiple_of(plan_ref[ORDER, first + i] * block, block)
            outs.append(
                pltpu.make_async_copy(
                    out_rows.at[i], o_ref.at[pl.ds(row, block)], out_sems.at[i]
                )
            )
            outs[-1].start()
        for copy in outs:
            copy.wait()

    operands = [plan]
    for _, _, pieces in bases + ranks:
        operands += pieces
    operands += maps.values()
    aliases = {}
    if before is not None:
        aliases = {len(operands): 0}
        operands.append(before)
    return pl.pallas_call(
        body,
        out_shape=(
            jax.ShapeDtypeStruct((shape[0] * tiles, 2, lanes), BF),
            jax.ShapeDtypeStruct((8, 128), F32),
        ),
        grid_spec=pltpu.PrefetchScalarGridSpec(
            num_scalar_prefetch=1,
            grid=(),
            in_specs=[HBM] * (len(operands) - 1),
            out_specs=(HBM, pl.BlockSpec(memory_space=pltpu.VMEM)),
            scratch_shapes=[
                pltpu.VMEM((count, extra, lanes), BF),
                pltpu.VMEM((count, n_base, prefill, 2 * columns), BF),
                pltpu.VMEM((count, n_rank, prefill, 2 * depth), BF),
                pltpu.VMEM((count, prefill * tiles, 2, lanes), BF),
                pltpu.SemaphoreType.DMA((count, n_base + n_rank + 1)),
                pltpu.SemaphoreType.DMA((count,)),
            ],
        ),
        input_output_aliases=aliases,
        compiler_params=params(24),
        cost_estimate=cost(12 * count * prefill * prefill * 2 * columns, 20 * count * prefill * columns),
        name="finish",
    )(*operands)


def solution(mesh):
    n_z, n_t = mesh.shape["adapter"], mesh.shape["tensor"]
    n_x = n_t // 2

    def core_swap(a):
        return lax.ppermute(a, "tensor", [(t, t ^ 1) for t in range(n_t)])

    def chip_shift(a, k):
        return lax.ppermute(
            a,
            "tensor",
            [(2 * x + c, 2 * ((x + k) % n_x) + c) for x in range(n_x) for c in (0, 1)],
        )

    def leftward(a, hops=1):
        return lax.ppermute(a, "adapter", [(z, z - hops) for z in range(hops, n_z)])

    def rightward(a, hops=1):
        return lax.ppermute(a, "adapter", [(z - hops, z) for z in range(hops, n_z)])

    def per_device(hidden, weight, down, up, table, adapters, lengths):
        requests = adapters.shape[0]
        prefill = hidden.shape[0] // requests
        stored = down.shape[0]
        columns = up.shape[3]
        by_distance = n_z == RANK_CHUNKS
        z, t = lax.axis_index("adapter"), lax.axis_index("tensor")
        plan = plan_requests(
            table, adapters, lengths, jnp.reshape(z, (1,)), n_z, stored
        )

        downs = {0: pack_maps(down, up)}

        def relay(hops, after):
            left, right = downs[hops - 1], downs[0 if hops == 1 else n_z + hops - 2]
            if after:
                left, right = hold([left, right], after)
                downs[hops - 1], downs[n_z + hops - 2] = left, right
            downs[hops] = leftward(left)
            downs[n_z - 1 + hops] = rightward(right)

        relay(1, [])

        def within(maps, hops):
            keys = range(hops + 1), range(n_z, n_z + hops)
            return {(k,): maps[k] for part in keys for k in part}

        dest = jnp.arange(n_t, dtype=jnp.int32)
        away = (dest // 2 - t // 2 + n_x) % n_x
        slots = jnp.where(dest % 2 == t % 2, n_x + away, away)

        bases, pairs = [], []

        def send_on(first, count, sends, keep, after):
            got = [core_swap(part) for part in sends[1:]] + [core_swap(sends[0])]
            pieces = [keep, got.pop()]
            n_piece = len(pieces_of(count))
            for k in range(1, n_x):
                pairs.append(pair_sum(keep, got[(k - 1) * n_piece : k * n_piece], k, after))
                pieces.append(chip_shift(pairs[-1], k))
            bases.append((first, count, pieces))

        def base(chunk):
            first, count = sum(BASE_CHUNKS[:chunk]), BASE_CHUNKS[chunk]
            return (first, count) + base_products(
                plan, hidden, split, first, count, prefill, pairs[-1:]
            )

        ranks = []
        count = requests // RANK_CHUNKS

        def rank(chunk, after):
            hops = chunk if by_distance else n_z - 1
            part = rank_products(
                plan, hidden, within(downs, hops), chunk * count, count, prefill, after
            )
            pair = (part.astype(F32) + core_swap(part).astype(F32)).astype(BF)
            pieces = [pair] + [chip_shift(pair, k) for k in range(1, n_x)]
            ranks.append((chunk * count, count, pieces))
            return part

        shape = (requests * prefill, 2, columns)

        def write(out, first, last):
            held = [
                b
                for b in bases
                if b[0] < last * count and b[0] + b[1] > first * count
            ]
            return finish(
                plan,
                held,
                ranks[first:last],
                within(downs, last - 1 if by_distance else n_z - 1),
                out,
                first * count,
                (last - first) * count,
                prefill,
                shape,
            )

        split, sends, keep = split_weight(
            plan, slots, hidden, weight, BASE_CHUNKS[0], prefill
        )
        send_on(0, BASE_CHUNKS[0], sends, keep, [])
        second = base(1)
        if n_z > 2:
            relay(2, [second[3]])
        send_on(*second, [bases[0][2][-1]])
        third = base(2)
        part = third[3]
        if by_distance:
            part = rank(0, [third[3], bases[1][2][-1]])
        send_on(*third, [part, bases[1][2][-1]])
        fourth = base(3)
        for hops in range(3, n_z):
            relay(hops, [fourth[3]])
        part = fourth[3]
        if by_distance:
            part = rank(1, [fourth[3], bases[2][2][-1]])
        send_on(*fourth, [part, bases[2][2][-1]])
        for chunk in range(len(ranks), 3):
            part = rank(chunk, [pairs[-1]])
        out, _ = write(None, 0, 2)
        out, written = write(out, 2, 3)
        rank(3, [written])
        out, _ = write(out, 3, 4)
        tiles = out.shape[0] // shape[0]
        out = out.reshape(shape[0], tiles, 2, columns // tiles)
        return out.transpose(0, 2, 1, 3).reshape(shape)

    return jax.shard_map(
        per_device,
        mesh=mesh,
        in_specs=(
            P(("group", "adapter"), "tensor"),
            P("tensor", None, None),
            P(("group", "adapter"), "tensor", None),
            P(("group", "adapter"), None, None, "tensor"),
            P("group"),
            P(("group", "adapter")),
            P(("group", "adapter")),
        ),
        out_specs=P(("group", "adapter"), None, "tensor"),
        check_vma=False,
    )
```

```python
import jax
import jax.numpy as jnp
from jax import lax
from jax.experimental import pallas as pl
from jax.experimental.pallas import tpu as pltpu
from jax.sharding import PartitionSpec as P

BF = jnp.bfloat16
F32 = jnp.float32
BASE_CHUNKS = (3, 3, 4, 2)
RANK_CHUNKS = 4
SMEM = pltpu.SMEM
PIECE = 2


def pieces_of(count):
    return [(at, min(PIECE, count - at)) for at in range(0, count, PIECE)]


ANY = pl.BlockSpec(memory_space=pl.ANY)
HBM = pl.BlockSpec(memory_space=pltpu.HBM)


def cost(flops, moved):
    return pl.CostEstimate(
        flops=int(flops * 0.01), bytes_accessed=int(moved * 0.01), transcendentals=0
    )


ORDER, SOURCE, ROW, LENGTH = range(4)


def params(mib=60):
    return pltpu.CompilerParams(vmem_limit_bytes=mib * 1024 * 1024)


def pack_maps(down, up):
    stored, features, lanes = down.shape
    _, sides, depth, columns = up.shape
    tiles = columns // lanes
    part = sides * depth

    def body(down_ref, up_ref, o_ref, held, sems):
        copies = []
        for a in range(stored):
            copies.append(
                pltpu.make_async_copy(
                    down_ref.at[a], o_ref.at[a, pl.ds(0, features)], sems.at[0, a]
                )
            )
            copies[-1].start()
        for a in range(stored):
            flat = up_ref[a].reshape(part, columns)
            for j in range(tiles):
                held[a, j * part : (j + 1) * part] = flat[:, j * lanes : (j + 1) * lanes]
            copies.append(
                pltpu.make_async_copy(
                    held.at[a],
                    o_ref.at[a, pl.ds(features, tiles * part)],
                    sems.at[1, a],
                )
            )
            copies[-1].start()
        for copy in copies:
            copy.wait()

    return pl.pallas_call(
        body,
        out_shape=jax.ShapeDtypeStruct((stored, features + tiles * part, lanes), BF),
        in_specs=[pl.BlockSpec(memory_space=pltpu.VMEM)] * 2,
        out_specs=HBM,
        scratch_shapes=[
            pltpu.VMEM((stored, tiles * part, lanes), BF),
            pltpu.SemaphoreType.DMA((2, stored)),
        ],
        compiler_params=params(24),
        cost_estimate=cost(0, 4 * down.size),
        name="pack_maps",
    )(down, up)


def plan_requests(table, adapters, lengths, here, n_z, stored):
    requests, known = adapters.shape[0], table.shape[0]
    shape = (requests, 128)

    def body(table_ref, adapter_ref, length_ref, here_ref, plan_ref):
        me = here_ref[0]
        request = lax.broadcasted_iota(jnp.int32, shape, 0)
        lane = lax.broadcasted_iota(jnp.int32, shape, 1)
        diagonal = request == lane

        def wide(ref, n):
            return jnp.pad(ref[...], ((0, 0), (0, 128 - n)))

        def down(a):
            return jnp.sum(jnp.where(diagonal, a, 0), axis=1, keepdims=True)

        def across(a):
            return jnp.sum(jnp.where(diagonal, a, 0), axis=0, keepdims=True)

        hit = (down(wide(adapter_ref, requests)) == lane) & (lane < known)
        slot = jnp.sum(jnp.where(hit, wide(table_ref, known), 0), 1, keepdims=True)
        owner = jnp.zeros_like(slot)
        for z in range(1, n_z):
            owner += jnp.where(slot >= z * stored, 1, 0)
        source = jnp.where(owner >= me, owner - me, n_z - 1 + me - owner)
        key = jnp.abs(owner - me) * 128 + request[:, :1]
        before = (across(key) < key) & (lane < requests)
        place = jnp.sum(jnp.where(before, 1, 0), axis=1, keepdims=True)
        at = place == lane

        def placed(a):
            return jnp.sum(jnp.where(at, a, 0), axis=0, keepdims=True)

        plan_ref[ORDER : ORDER + 1] = placed(request)
        plan_ref[SOURCE : SOURCE + 1] = placed(source)
        plan_ref[ROW : ROW + 1] = placed(slot - owner * stored)
        plan_ref[LENGTH : LENGTH + 1] = placed(down(wide(length_ref, requests)))

    vmem = pl.BlockSpec(memory_space=pltpu.VMEM)
    return pl.pallas_call(
        body,
        out_shape=jax.ShapeDtypeStruct((8, 128), jnp.int32),
        in_specs=[vmem, vmem, vmem, pl.BlockSpec(memory_space=SMEM)],
        out_specs=vmem,
        cost_estimate=cost(0, 1 << 20),
        name="plan_requests",
    )(table[None, :], adapters[None, :], lengths[None, :], here)


def split_weight(plan, slots, hidden, weight, count, prefill):
    features, _, columns = weight.shape
    n_t = slots.shape[0]
    n_x = n_t // 2
    width = columns // n_t
    rows, half = 512, 128
    steps = features // rows

    def body(plan_ref, slot_ref, *rest):
        x_refs, (w_ref, o_ref, *send_refs, keep_ref, total) = rest[:count], rest[count:]
        step = pl.program_id(0)
        above = pl.multiple_of(step * rows, rows)
        out_row = lax.broadcasted_iota(jnp.int32, (2 * half, 2 * half), 0)
        in_row = lax.broadcasted_iota(jnp.int32, (2 * half, 2 * half), 1)
        pick = in_row == 2 * (out_row % half) + out_row // half
        pick = pick.astype(F32).astype(BF)
        for b in range(rows // half):
            mixed = w_ref[b * half : (b + 1) * half].reshape(2 * half, columns)
            apart = jnp.dot(pick, mixed, preferred_element_type=F32).astype(BF)
            for t in range(n_t):
                for s in range(2):
                    o_ref[
                        slot_ref[t],
                        pl.ds(above + b * half, half),
                        s * width : (s + 1) * width,
                    ] = apart[s * half : (s + 1) * half, t * width : (t + 1) * width]

        @pl.when(step == 0)
        def _():
            total[...] = jnp.zeros_like(total)

        for r in range(count):
            for j in range(n_t):
                total[j, r * prefill : (r + 1) * prefill] += jnp.dot(
                    x_refs[r][...], o_ref[j, pl.ds(above, rows)], preferred_element_type=F32
                )

        @pl.when(step == steps - 1)
        def _():
            send_refs[0][...] = total[0].astype(BF)
            k = 1
            for j in range(1, n_x):
                for at, n in pieces_of(count):
                    rows_of = slice(at * prefill, (at + n) * prefill)
                    send_refs[k][...] = total[j, rows_of].astype(BF)
                    k += 1
            for j in range(n_x):
                keep_ref[j] = total[n_x + j].astype(BF)

    part = (count * prefill, 2 * width)
    outs = [part] + [
        (n * prefill, 2 * width) for _, n in pieces_of(count)
    ] * (n_x - 1)
    split, *sends, keep = pl.pallas_call(
        body,
        out_shape=(
            jax.ShapeDtypeStruct((n_t, features, 2 * width), BF),
            *[jax.ShapeDtypeStruct(out, BF) for out in outs],
            jax.ShapeDtypeStruct((n_x, *part), BF),
        ),
        grid_spec=pltpu.PrefetchScalarGridSpec(
            num_scalar_prefetch=2,
            grid=(steps,),
            in_specs=[
                pl.BlockSpec((prefill, rows), lambda i, p, s, r=r: (p[ORDER, r], i))
                for r in range(count)
            ]
            + [pl.BlockSpec((rows, 2, columns), lambda i, p, s: (i, 0, 0))],
            out_specs=(
                pl.BlockSpec(memory_space=pltpu.VMEM),
                *[pl.BlockSpec(out, lambda i, p, s: (0, 0)) for out in outs],
                pl.BlockSpec((n_x, *part), lambda i, p, s: (0, 0, 0)),
            ),
            scratch_shapes=[pltpu.VMEM((n_t, count * prefill, 2 * width), F32)],
        ),
        compiler_params=params(46),
        cost_estimate=cost(2 * count * prefill * features * 2 * columns, 8 * features * columns),
        name="split_weight",
    )(plan, slots, *[hidden] * count, weight)
    return split, sends, keep


def base_products(plan, hidden, weight, first, count, prefill, after):
    n_t, features, width = weight.shape
    n_x = n_t // 2
    short = prefill // 2
    n_after = len(after)

    def body(plan_ref, x_ref, *rest):
        w_ref = rest[0]
        *send_refs, keep_ref = rest[1 + n_after :]
        live = plan_ref[LENGTH, first + pl.program_id(0)]

        def products(rows):
            dead = jnp.zeros((prefill - rows, width), BF)
            for j in range(n_t):
                out = jnp.dot(
                    x_ref[:rows], w_ref[j], preferred_element_type=F32
                ).astype(BF)
                if rows < prefill:
                    out = jnp.concatenate([out, dead], 0)
                if j == 0:
                    send_refs[0][...] = out
                elif j >= n_x:
                    keep_ref[j - n_x] = out
                else:

                    spans = pieces_of(count)
                    for k, (at, n) in enumerate(spans, 1 + (j - 1) * len(spans)):
                        inside = (pl.program_id(0) >= at) & (pl.program_id(0) < at + n)

                        @pl.when(inside)
                        def _():
                            send_refs[k][...] = out

        @pl.when(live > short)
        def _():
            products(prefill)

        @pl.when(live <= short)
        def _():
            products(short)

    spans = [(0, count)] + pieces_of(count) * (n_x - 1)
    parts = [n for _, n in spans]
    block = (prefill, width)
    places = [
        lambda i, p, at=at, n=n: (jnp.clip(i - at, 0, n - 1), 0) for at, n in spans
    ]
    *sends, keep = pl.pallas_call(
        body,
        out_shape=(
            *[jax.ShapeDtypeStruct((n * prefill, width), BF) for n in parts],
            jax.ShapeDtypeStruct((n_x, count * prefill, width), BF),
        ),
        grid_spec=pltpu.PrefetchScalarGridSpec(
            num_scalar_prefetch=1,
            grid=(count,),
            in_specs=[
                pl.BlockSpec(
                    (prefill, features), lambda i, p: (p[ORDER, first + i], 0)
                ),
            ]
            + [pl.BlockSpec(memory_space=pltpu.VMEM)]
            + [ANY] * n_after,
            out_specs=(
                *[pl.BlockSpec(block, place) for place in places],
                pl.BlockSpec((n_x, prefill, width), lambda i, p: (0, i, 0)),
            ),
        ),
        compiler_params=params(46),
        cost_estimate=cost(2 * count * prefill * features * width * n_t, 2 * n_t * features * width),
        name="base_products",
    )(plan, hidden, weight, *after)
    return sends, keep


def pair_sum(one, others, index, after):
    _, rows, width = one.shape
    n_piece = len(others)

    def body(a_ref, *rest):
        b_refs = rest[:n_piece]
        o_ref, mine, theirs, total, sems, out_sems = rest[n_piece + len(after) :]
        copies, outs = [], []
        spans, at = [], 0
        for b_ref in b_refs:
            spans.append(pl.ds(at, b_ref.shape[0]))
            at += b_ref.shape[0]
        for k, span in enumerate(spans):
            copies.append(
                (
                    pltpu.make_async_copy(
                        a_ref.at[index, span], mine.at[span], sems.at[0, k]
                    ),
                    pltpu.make_async_copy(b_refs[k], theirs.at[span], sems.at[1, k]),
                )
            )
            for copy in copies[-1]:
                copy.start()
        for k, span in enumerate(spans):
            for copy in copies[k]:
                copy.wait()
            value = mine[span].astype(F32) + theirs[span].astype(F32)
            total[span] = value.astype(BF)
            outs.append(
                pltpu.make_async_copy(total.at[span], o_ref.at[span], out_sems.at[k])
            )
            outs[-1].start()
        for copy in outs:
            copy.wait()

    return pl.pallas_call(
        body,
        out_shape=jax.ShapeDtypeStruct((rows, width), BF),
        in_specs=[ANY] * (1 + n_piece + len(after)),
        out_specs=ANY,
        scratch_shapes=[pltpu.VMEM((rows, width), BF)] * 3
        + [pltpu.SemaphoreType.DMA((2, n_piece)), pltpu.SemaphoreType.DMA((n_piece,))],
        compiler_params=params(12),
        cost_estimate=cost(rows * width, 6 * rows * width),
        name="pair_sum",
    )(one, *others, *after)


def hold(arrays, after):
    n = len(arrays)

    def body(*refs):
        pass

    return pl.pallas_call(
        body,
        out_shape=[jax.ShapeDtypeStruct(a.shape, a.dtype) for a in arrays],
        in_specs=[HBM] * (n + len(after)),
        out_specs=[HBM] * n,
        input_output_aliases={i: i for i in range(n)},
        compiler_params=params(8),
        cost_estimate=cost(0, 1 << 20),
        name="hold",
    )(*arrays, *after)


def fetch(refs, source, row, part, target, sem):
    for codes, ref in refs:
        hit = source == codes[0]
        for code in codes[1:]:
            hit |= source == code

        @pl.when(hit)
        def _():
            pltpu.make_async_copy(ref.at[row, part], target, sem).start()


def rank_products(plan, hidden, maps, first, count, prefill, after):
    sources = list(maps)
    features, ranks = hidden.shape[1], maps[sources[0]].shape[2]
    n_map, n_after = len(maps), len(after)
    short = prefill // 2
    down = pl.ds(0, features)

    def body(plan_ref, x_ref, *rest):
        refs = list(zip(sources, rest[:n_map]))
        o_ref, rows, held, sems = rest[n_map + n_after :]
        copies = []
        for i in range(count):
            fetch(
                refs,
                plan_ref[SOURCE, first + i],
                plan_ref[ROW, first + i],
                down,
                held.at[i],
                sems.at[0, i],
            )
            at = pl.multiple_of(plan_ref[ORDER, first + i] * prefill, prefill)
            copies.append(
                pltpu.make_async_copy(
                    x_ref.at[pl.ds(at, prefill)], rows.at[i], sems.at[1, i]
                )
            )
            copies[-1].start()
        for i in range(count):
            pltpu.make_async_copy(
                rest[0].at[0, down], held.at[i], sems.at[0, i]
            ).wait()
            copies[i].wait()
            live = plan_ref[LENGTH, first + i]
            above, below = i * prefill, i * prefill + short

            @pl.when(live > short)
            def _():
                o_ref[above : above + prefill] = jnp.dot(
                    rows[i], held[i], preferred_element_type=F32
                ).astype(BF)

            @pl.when(live <= short)
            def _():
                o_ref[above:below] = jnp.dot(
                    rows[i, :short], held[i], preferred_element_type=F32
                ).astype(BF)
                o_ref[below : below + short] = jnp.zeros((short, ranks), BF)

    return pl.pallas_call(
        body,
        out_shape=jax.ShapeDtypeStruct((count * prefill, ranks), BF),
        grid_spec=pltpu.PrefetchScalarGridSpec(
            num_scalar_prefetch=1,
            grid=(),
            in_specs=[HBM] * (1 + n_map + n_after),
            out_specs=pl.BlockSpec(memory_space=pltpu.VMEM),
            scratch_shapes=[
                pltpu.VMEM((count, prefill, features), BF),
                pltpu.VMEM((count, features, ranks), BF),
                pltpu.SemaphoreType.DMA((2, count)),
            ],
        ),
        compiler_params=params(16),
        cost_estimate=cost(2 * count * prefill * features * ranks, 2 * count * features * (prefill + ranks)),
        name="rank_products",
    )(plan, hidden, *maps.values(), *after)


def finish(plan, bases, ranks, maps, before, first, count, prefill, shape):
    sources = list(maps)
    columns, depth = shape[2], ranks[0][2][0].shape[1] // 2
    _, packed, lanes = maps[sources[0]].shape
    tiles = columns // lanes
    extra = tiles * 2 * depth
    up_part = pl.ds(packed - extra, extra)
    half = prefill // 2
    n_map = len(maps)
    n_base = max(len(pieces) for _, _, pieces in bases)
    n_rank = max(len(pieces) for _, _, pieces in ranks)

    def body(plan_ref, *rest):
        base_refs, rank_refs = [], []
        for refs, pieces in ((base_refs, bases), (rank_refs, ranks)):
            for start, n, arrays in pieces:
                refs.append((start, n, rest[: len(arrays)]))
                rest = rest[len(arrays) :]
        map_refs = list(zip(sources, rest[:n_map]))
        o_ref, token_ref, ups, base_rows, rank_rows, out_rows, sems, out_sems = rest[-8:]
        token_ref[...] = jnp.zeros_like(token_ref)

        def start_pieces(refs, at, rows, sem):
            copies = []
            for start, n, arrays in refs:
                if start <= at < start + n:
                    block = pl.ds((at - start) * prefill, prefill)
                    for k, ref in enumerate(arrays):
                        source = ref.at[0, block] if len(ref.shape) == 3 else ref.at[block]
                        copies.append(pltpu.make_async_copy(source, rows.at[k], sem.at[k]))
                        copies[-1].start()
            return copies

        copies = []
        for i in range(count):
            at = first + i
            copies.append(
                start_pieces(base_refs, at, base_rows.at[i], sems.at[i])
                + start_pieces(
                    rank_refs, at, rank_rows.at[i], sems.at[i, pl.ds(n_base, n_rank)]
                )
            )
            fetch(
                map_refs,
                plan_ref[SOURCE, at],
                plan_ref[ROW, at],
                up_part,
                ups.at[i],
                sems.at[i, n_base + n_rank],
            )

        group = half // tiles
        mix_row = lax.broadcasted_iota(jnp.int32, (2 * half, 2 * half), 0)
        mix_column = lax.broadcasted_iota(jnp.int32, (2 * half, 2 * half), 1)
        mix_token, mix_tile = mix_row // (2 * tiles), mix_row // 2 % tiles
        mix = mix_column == (mix_row % 2 * tiles + mix_tile) * group + mix_token
        mix = mix.astype(F32).astype(BF)
        token = lax.broadcasted_iota(jnp.int32, (half, 2 * columns), 0)

        def rows_for(i, live, b):
            rows = slice(b * half, (b + 1) * half)
            rank = rank_rows[i, 0, rows].astype(F32)
            for k in range(1, n_rank):
                rank += rank_rows[i, k, rows].astype(F32)
            rank = rank.astype(BF)
            up = jnp.concatenate(
                [ups[i, j * 2 * depth : (j + 1) * 2 * depth] for j in range(tiles)], 1
            )
            total = jnp.concatenate(
                [
                    jnp.dot(
                        rank[:, s * depth : (s + 1) * depth],
                        up[s * depth : (s + 1) * depth],
                        preferred_element_type=F32,
                    )
                    for s in range(2)
                ],
                1,
            )
            for k in range(n_base):
                total += base_rows[i, k, rows].astype(F32)
            total = jnp.where(token + b * half < live, total, 0.0).astype(BF)
            parts = [
                jnp.concatenate(
                    [
                        total[g * group : (g + 1) * group, k * lanes : (k + 1) * lanes]
                        for k in range(2 * tiles)
                    ],
                    0,
                )
                for g in range(tiles)
            ]
            mixed = jnp.dot(
                mix, jnp.concatenate(parts, 1), preferred_element_type=F32
            ).astype(BF)
            for g in range(tiles):
                at = b * half * tiles + g * half
                out_rows[i, at : at + half] = mixed[
                    :, g * lanes : (g + 1) * lanes
                ].reshape(half, 2, lanes)

        outs = []
        for i in range(count):
            for copy in copies[i]:
                copy.wait()
            pltpu.make_async_copy(
                map_refs[0][1].at[0, up_part], ups.at[i], sems.at[i, n_base + n_rank]
            ).wait()
            live = plan_ref[LENGTH, first + i]
            rows_for(i, live, 0)

            @pl.when(live > half)
            def _():
                rows_for(i, live, 1)

            @pl.when(live <= half)
            def _():
                out_rows[i, half * tiles :] = jnp.zeros((half * tiles, 2, lanes), BF)

            block = prefill * tiles
            row = pl.multiple_of(plan_ref[ORDER, first + i] * block, block)
            outs.append(
                pltpu.make_async_copy(
                    out_rows.at[i], o_ref.at[pl.ds(row, block)], out_sems.at[i]
                )
            )
            outs[-1].start()
        for copy in outs:
            copy.wait()

    operands = [plan]
    for _, _, pieces in bases + ranks:
        operands += pieces
    operands += maps.values()
    aliases = {}
    if before is not None:
        aliases = {len(operands): 0}
        operands.append(before)
    return pl.pallas_call(
        body,
        out_shape=(
            jax.ShapeDtypeStruct((shape[0] * tiles, 2, lanes), BF),
            jax.ShapeDtypeStruct((8, 128), F32),
        ),
        grid_spec=pltpu.PrefetchScalarGridSpec(
            num_scalar_prefetch=1,
            grid=(),
            in_specs=[HBM] * (len(operands) - 1),
            out_specs=(HBM, pl.BlockSpec(memory_space=pltpu.VMEM)),
            scratch_shapes=[
                pltpu.VMEM((count, extra, lanes), BF),
                pltpu.VMEM((count, n_base, prefill, 2 * columns), BF),
                pltpu.VMEM((count, n_rank, prefill, 2 * depth), BF),
                pltpu.VMEM((count, prefill * tiles, 2, lanes), BF),
                pltpu.SemaphoreType.DMA((count, n_base + n_rank + 1)),
                pltpu.SemaphoreType.DMA((count,)),
            ],
        ),
        input_output_aliases=aliases,
        compiler_params=params(24),
        cost_estimate=cost(12 * count * prefill * prefill * 2 * columns, 20 * count * prefill * columns),
        name="finish",
    )(*operands)


def solution(mesh):
    n_z, n_t = mesh.shape["adapter"], mesh.shape["tensor"]
    n_x = n_t // 2

    def core_swap(a):
        return lax.ppermute(a, "tensor", [(t, t ^ 1) for t in range(n_t)])

    def chip_shift(a, k):
        return lax.ppermute(
            a,
            "tensor",
            [(2 * x + c, 2 * ((x + k) % n_x) + c) for x in range(n_x) for c in (0, 1)],
        )

    def leftward(a, hops=1):
        return lax.ppermute(a, "adapter", [(z, z - hops) for z in range(hops, n_z)])

    def rightward(a, hops=1):
        return lax.ppermute(a, "adapter", [(z - hops, z) for z in range(hops, n_z)])

    def per_device(hidden, weight, down, up, table, adapters, lengths):
        requests = adapters.shape[0]
        prefill = hidden.shape[0] // requests
        stored = down.shape[0]
        columns = up.shape[3]
        by_distance = n_z == RANK_CHUNKS
        z, t = lax.axis_index("adapter"), lax.axis_index("tensor")
        plan = plan_requests(
            table, adapters, lengths, jnp.reshape(z, (1,)), n_z, stored
        )

        downs = {0: pack_maps(down, up)}

        def relay(hops, after):
            left, right = downs[hops - 1], downs[0 if hops == 1 else n_z + hops - 2]
            if after:
                left, right = hold([left, right], after)
                downs[hops - 1], downs[n_z + hops - 2] = left, right
            downs[hops] = leftward(left)
            downs[n_z - 1 + hops] = rightward(right)

        relay(1, [])

        def within(maps, hops):
            keys = range(hops + 1), range(n_z, n_z + hops)
            return {(k,): maps[k] for part in keys for k in part}

        dest = jnp.arange(n_t, dtype=jnp.int32)
        away = (dest // 2 - t // 2 + n_x) % n_x
        slots = jnp.where(dest % 2 == t % 2, n_x + away, away)

        bases, pairs = [], []

        def send_on(first, count, sends, keep, after):
            got = [core_swap(part) for part in sends[1:]] + [core_swap(sends[0])]
            pieces = [keep, got.pop()]
            n_piece = len(pieces_of(count))
            for k in range(1, n_x):
                pairs.append(pair_sum(keep, got[(k - 1) * n_piece : k * n_piece], k, after))
                pieces.append(chip_shift(pairs[-1], k))
            bases.append((first, count, pieces))

        def base(chunk):
            first, count = sum(BASE_CHUNKS[:chunk]), BASE_CHUNKS[chunk]
            return (first, count) + base_products(
                plan, hidden, split, first, count, prefill, pairs[-1:]
            )

        ranks = []
        count = requests // RANK_CHUNKS

        def rank(chunk, after):
            hops = chunk if by_distance else n_z - 1
            part = rank_products(
                plan, hidden, within(downs, hops), chunk * count, count, prefill, after
            )
            pair = (part.astype(F32) + core_swap(part).astype(F32)).astype(BF)
            pieces = [pair] + [chip_shift(pair, k) for k in range(1, n_x)]
            ranks.append((chunk * count, count, pieces))
            return part

        shape = (requests * prefill, 2, columns)

        def write(out, first, last):
            held = [
                b
                for b in bases
                if b[0] < last * count and b[0] + b[1] > first * count
            ]
            return finish(
                plan,
                held,
                ranks[first:last],
                within(downs, last - 1 if by_distance else n_z - 1),
                out,
                first * count,
                (last - first) * count,
                prefill,
                shape,
            )

        split, sends, keep = split_weight(
            plan, slots, hidden, weight, BASE_CHUNKS[0], prefill
        )
        send_on(0, BASE_CHUNKS[0], sends, keep, [])
        second = base(1)
        if n_z > 2:
            relay(2, [second[3]])
        send_on(*second, [bases[0][2][-1]])
        third = base(2)
        part = third[3]
        if by_distance:
            part = rank(0, [third[3], bases[1][2][-1]])
        send_on(*third, [part, bases[1][2][-1]])
        fourth = base(3)
        for hops in range(3, n_z):
            relay(hops, [fourth[3]])
        part = fourth[3]
        if by_distance:
            part = rank(1, [part])
            part = rank(2, [part, bases[2][2][-1]])
        send_on(*fourth, [part, bases[2][2][-1]])
        for chunk in range(len(ranks), 3):
            part = rank(chunk, [pairs[-1]])
        out, _ = write(None, 0, 2)
        out, written = write(out, 2, 3)
        rank(3, [written, bases[3][2][-1]])
        out, _ = write(out, 3, 4)
        tiles = out.shape[0] // shape[0]
        out = out.reshape(shape[0], tiles, 2, columns // tiles)
        return out.transpose(0, 2, 1, 3).reshape(shape)

    return jax.shard_map(
        per_device,
        mesh=mesh,
        in_specs=(
            P(("group", "adapter"), "tensor"),
            P("tensor", None, None),
            P(("group", "adapter"), "tensor", None),
            P(("group", "adapter"), None, None, "tensor"),
            P("group"),
            P(("group", "adapter")),
            P(("group", "adapter")),
        ),
        out_specs=P(("group", "adapter"), None, "tensor"),
        check_vma=False,
    )
```

```python
import jax
import jax.numpy as jnp
from jax import lax
from jax.experimental import pallas as pl
from jax.experimental.pallas import tpu as pltpu
from jax.sharding import PartitionSpec as P

BF = jnp.bfloat16
F32 = jnp.float32
BASE_CHUNKS = (3, 3, 4, 2)
RANK_CHUNKS = 4
SMEM = pltpu.SMEM
PIECE = 2


def pieces_of(count):
    return [(at, min(PIECE, count - at)) for at in range(0, count, PIECE)]


ANY = pl.BlockSpec(memory_space=pl.ANY)
HBM = pl.BlockSpec(memory_space=pltpu.HBM)


def cost(flops, moved):
    return pl.CostEstimate(
        flops=int(flops * 0.01), bytes_accessed=int(moved * 0.01), transcendentals=0
    )


ORDER, SOURCE, ROW, LENGTH = range(4)


def params(mib=60):
    return pltpu.CompilerParams(vmem_limit_bytes=mib * 1024 * 1024)


def pack_maps(down, up):
    stored, features, lanes = down.shape
    _, sides, depth, columns = up.shape
    tiles = columns // lanes
    part = sides * depth

    def body(down_ref, up_ref, o_ref, held, sems):
        copies = []
        for a in range(stored):
            copies.append(
                pltpu.make_async_copy(
                    down_ref.at[a], o_ref.at[a, pl.ds(0, features)], sems.at[0, a]
                )
            )
            copies[-1].start()
        for a in range(stored):
            flat = up_ref[a].reshape(part, columns)
            for j in range(tiles):
                held[a, j * part : (j + 1) * part] = flat[:, j * lanes : (j + 1) * lanes]
            copies.append(
                pltpu.make_async_copy(
                    held.at[a],
                    o_ref.at[a, pl.ds(features, tiles * part)],
                    sems.at[1, a],
                )
            )
            copies[-1].start()
        for copy in copies:
            copy.wait()

    return pl.pallas_call(
        body,
        out_shape=jax.ShapeDtypeStruct((stored, features + tiles * part, lanes), BF),
        in_specs=[pl.BlockSpec(memory_space=pltpu.VMEM)] * 2,
        out_specs=HBM,
        scratch_shapes=[
            pltpu.VMEM((stored, tiles * part, lanes), BF),
            pltpu.SemaphoreType.DMA((2, stored)),
        ],
        compiler_params=params(24),
        cost_estimate=cost(0, 4 * down.size),
        name="pack_maps",
    )(down, up)


def plan_requests(table, adapters, lengths, here, n_z, stored):
    requests, known = adapters.shape[0], table.shape[0]
    shape = (requests, 128)

    def body(table_ref, adapter_ref, length_ref, here_ref, plan_ref):
        me = here_ref[0]
        request = lax.broadcasted_iota(jnp.int32, shape, 0)
        lane = lax.broadcasted_iota(jnp.int32, shape, 1)
        diagonal = request == lane

        def wide(ref, n):
            return jnp.pad(ref[...], ((0, 0), (0, 128 - n)))

        def down(a):
            return jnp.sum(jnp.where(diagonal, a, 0), axis=1, keepdims=True)

        def across(a):
            return jnp.sum(jnp.where(diagonal, a, 0), axis=0, keepdims=True)

        hit = (down(wide(adapter_ref, requests)) == lane) & (lane < known)
        slot = jnp.sum(jnp.where(hit, wide(table_ref, known), 0), 1, keepdims=True)
        owner = jnp.zeros_like(slot)
        for z in range(1, n_z):
            owner += jnp.where(slot >= z * stored, 1, 0)
        source = jnp.where(owner >= me, owner - me, n_z - 1 + me - owner)
        key = jnp.abs(owner - me) * 128 + request[:, :1]
        before = (across(key) < key) & (lane < requests)
        place = jnp.sum(jnp.where(before, 1, 0), axis=1, keepdims=True)
        at = place == lane

        def placed(a):
            return jnp.sum(jnp.where(at, a, 0), axis=0, keepdims=True)

        plan_ref[ORDER : ORDER + 1] = placed(request)
        plan_ref[SOURCE : SOURCE + 1] = placed(source)
        plan_ref[ROW : ROW + 1] = placed(slot - owner * stored)
        plan_ref[LENGTH : LENGTH + 1] = placed(down(wide(length_ref, requests)))

    vmem = pl.BlockSpec(memory_space=pltpu.VMEM)
    return pl.pallas_call(
        body,
        out_shape=jax.ShapeDtypeStruct((8, 128), jnp.int32),
        in_specs=[vmem, vmem, vmem, pl.BlockSpec(memory_space=SMEM)],
        out_specs=vmem,
        cost_estimate=cost(0, 1 << 20),
        name="plan_requests",
    )(table[None, :], adapters[None, :], lengths[None, :], here)


def split_weight(plan, slots, hidden, weight, count, prefill):
    features, _, columns = weight.shape
    n_t = slots.shape[0]
    n_x = n_t // 2
    width = columns // n_t
    rows, half = 512, 128
    steps = features // rows

    def body(plan_ref, slot_ref, *rest):
        x_refs, (w_ref, o_ref, *send_refs, keep_ref, total) = rest[:count], rest[count:]
        step = pl.program_id(0)
        above = pl.multiple_of(step * rows, rows)
        out_row = lax.broadcasted_iota(jnp.int32, (2 * half, 2 * half), 0)
        in_row = lax.broadcasted_iota(jnp.int32, (2 * half, 2 * half), 1)
        pick = in_row == 2 * (out_row % half) + out_row // half
        pick = pick.astype(F32).astype(BF)
        for b in range(rows // half):
            mixed = w_ref[b * half : (b + 1) * half].reshape(2 * half, columns)
            apart = jnp.dot(pick, mixed, preferred_element_type=F32).astype(BF)
            for t in range(n_t):
                for s in range(2):
                    o_ref[
                        slot_ref[t],
                        pl.ds(above + b * half, half),
                        s * width : (s + 1) * width,
                    ] = apart[s * half : (s + 1) * half, t * width : (t + 1) * width]

        @pl.when(step == 0)
        def _():
            total[...] = jnp.zeros_like(total)

        for r in range(count):
            for j in range(n_t):
                total[j, r * prefill : (r + 1) * prefill] += jnp.dot(
                    x_refs[r][...], o_ref[j, pl.ds(above, rows)], preferred_element_type=F32
                )

        @pl.when(step == steps - 1)
        def _():
            send_refs[0][...] = total[0].astype(BF)
            k = 1
            for j in range(1, n_x):
                for at, n in pieces_of(count):
                    rows_of = slice(at * prefill, (at + n) * prefill)
                    send_refs[k][...] = total[j, rows_of].astype(BF)
                    k += 1
            for j in range(n_x):
                keep_ref[j] = total[n_x + j].astype(BF)

    part = (count * prefill, 2 * width)
    outs = [part] + [
        (n * prefill, 2 * width) for _, n in pieces_of(count)
    ] * (n_x - 1)
    split, *sends, keep = pl.pallas_call(
        body,
        out_shape=(
            jax.ShapeDtypeStruct((n_t, features, 2 * width), BF),
            *[jax.ShapeDtypeStruct(out, BF) for out in outs],
            jax.ShapeDtypeStruct((n_x, *part), BF),
        ),
        grid_spec=pltpu.PrefetchScalarGridSpec(
            num_scalar_prefetch=2,
            grid=(steps,),
            in_specs=[
                pl.BlockSpec((prefill, rows), lambda i, p, s, r=r: (p[ORDER, r], i))
                for r in range(count)
            ]
            + [pl.BlockSpec((rows, 2, columns), lambda i, p, s: (i, 0, 0))],
            out_specs=(
                pl.BlockSpec(memory_space=pltpu.VMEM),
                *[pl.BlockSpec(out, lambda i, p, s: (0, 0)) for out in outs],
                pl.BlockSpec((n_x, *part), lambda i, p, s: (0, 0, 0)),
            ),
            scratch_shapes=[pltpu.VMEM((n_t, count * prefill, 2 * width), F32)],
        ),
        compiler_params=params(46),
        cost_estimate=cost(2 * count * prefill * features * 2 * columns, 8 * features * columns),
        name="split_weight",
    )(plan, slots, *[hidden] * count, weight)
    return split, sends, keep


def base_products(plan, hidden, weight, first, count, prefill, after):
    n_t, features, width = weight.shape
    n_x = n_t // 2
    short = prefill // 2
    n_after = len(after)

    def body(plan_ref, x_ref, *rest):
        w_ref = rest[0]
        *send_refs, keep_ref = rest[1 + n_after :]
        live = plan_ref[LENGTH, first + pl.program_id(0)]

        def products(rows):
            dead = jnp.zeros((prefill - rows, width), BF)
            for j in range(n_t):
                out = jnp.dot(
                    x_ref[:rows], w_ref[j], preferred_element_type=F32
                ).astype(BF)
                if rows < prefill:
                    out = jnp.concatenate([out, dead], 0)
                if j == 0:
                    send_refs[0][...] = out
                elif j >= n_x:
                    keep_ref[j - n_x] = out
                else:

                    spans = pieces_of(count)
                    for k, (at, n) in enumerate(spans, 1 + (j - 1) * len(spans)):
                        inside = (pl.program_id(0) >= at) & (pl.program_id(0) < at + n)

                        @pl.when(inside)
                        def _():
                            send_refs[k][...] = out

        @pl.when(live > short)
        def _():
            products(prefill)

        @pl.when(live <= short)
        def _():
            products(short)

    spans = [(0, count)] + pieces_of(count) * (n_x - 1)
    parts = [n for _, n in spans]
    block = (prefill, width)
    places = [
        lambda i, p, at=at, n=n: (jnp.clip(i - at, 0, n - 1), 0) for at, n in spans
    ]
    *sends, keep = pl.pallas_call(
        body,
        out_shape=(
            *[jax.ShapeDtypeStruct((n * prefill, width), BF) for n in parts],
            jax.ShapeDtypeStruct((n_x, count * prefill, width), BF),
        ),
        grid_spec=pltpu.PrefetchScalarGridSpec(
            num_scalar_prefetch=1,
            grid=(count,),
            in_specs=[
                pl.BlockSpec(
                    (prefill, features), lambda i, p: (p[ORDER, first + i], 0)
                ),
            ]
            + [pl.BlockSpec(memory_space=pltpu.VMEM)]
            + [ANY] * n_after,
            out_specs=(
                *[pl.BlockSpec(block, place) for place in places],
                pl.BlockSpec((n_x, prefill, width), lambda i, p: (0, i, 0)),
            ),
        ),
        compiler_params=params(46),
        cost_estimate=cost(2 * count * prefill * features * width * n_t, 2 * n_t * features * width),
        name="base_products",
    )(plan, hidden, weight, *after)
    return sends, keep


def pair_sum(one, others, index, after):
    _, rows, width = one.shape
    n_piece = len(others)

    def body(a_ref, *rest):
        b_refs = rest[:n_piece]
        o_ref, mine, theirs, total, sems, out_sems = rest[n_piece + len(after) :]
        copies, outs = [], []
        spans, at = [], 0
        for b_ref in b_refs:
            spans.append(pl.ds(at, b_ref.shape[0]))
            at += b_ref.shape[0]
        for k, span in enumerate(spans):
            copies.append(
                (
                    pltpu.make_async_copy(
                        a_ref.at[index, span], mine.at[span], sems.at[0, k]
                    ),
                    pltpu.make_async_copy(b_refs[k], theirs.at[span], sems.at[1, k]),
                )
            )
            for copy in copies[-1]:
                copy.start()
        for k, span in enumerate(spans):
            for copy in copies[k]:
                copy.wait()
            value = mine[span].astype(F32) + theirs[span].astype(F32)
            total[span] = value.astype(BF)
            outs.append(
                pltpu.make_async_copy(total.at[span], o_ref.at[span], out_sems.at[k])
            )
            outs[-1].start()
        for copy in outs:
            copy.wait()

    return pl.pallas_call(
        body,
        out_shape=jax.ShapeDtypeStruct((rows, width), BF),
        in_specs=[ANY] * (1 + n_piece + len(after)),
        out_specs=ANY,
        scratch_shapes=[pltpu.VMEM((rows, width), BF)] * 3
        + [pltpu.SemaphoreType.DMA((2, n_piece)), pltpu.SemaphoreType.DMA((n_piece,))],
        compiler_params=params(12),
        cost_estimate=cost(rows * width, 6 * rows * width),
        name="pair_sum",
    )(one, *others, *after)


def hold(arrays, after):
    n = len(arrays)

    def body(*refs):
        pass

    return pl.pallas_call(
        body,
        out_shape=[jax.ShapeDtypeStruct(a.shape, a.dtype) for a in arrays],
        in_specs=[HBM] * (n + len(after)),
        out_specs=[HBM] * n,
        input_output_aliases={i: i for i in range(n)},
        compiler_params=params(8),
        cost_estimate=cost(0, 1 << 20),
        name="hold",
    )(*arrays, *after)


def fetch(refs, source, row, part, target, sem):
    for codes, ref in refs:
        hit = source == codes[0]
        for code in codes[1:]:
            hit |= source == code

        @pl.when(hit)
        def _():
            pltpu.make_async_copy(ref.at[row, part], target, sem).start()


def rank_products(plan, hidden, maps, first, count, prefill, after):
    sources = list(maps)
    features, ranks = hidden.shape[1], maps[sources[0]].shape[2]
    n_map, n_after = len(maps), len(after)
    short = prefill // 2
    down = pl.ds(0, features)

    def body(plan_ref, x_ref, *rest):
        refs = list(zip(sources, rest[:n_map]))
        o_ref, rows, held, sems = rest[n_map + n_after :]
        copies = []
        for i in range(count):
            fetch(
                refs,
                plan_ref[SOURCE, first + i],
                plan_ref[ROW, first + i],
                down,
                held.at[i],
                sems.at[0, i],
            )
            at = pl.multiple_of(plan_ref[ORDER, first + i] * prefill, prefill)
            copies.append(
                pltpu.make_async_copy(
                    x_ref.at[pl.ds(at, prefill)], rows.at[i], sems.at[1, i]
                )
            )
            copies[-1].start()
        for i in range(count):
            pltpu.make_async_copy(
                rest[0].at[0, down], held.at[i], sems.at[0, i]
            ).wait()
            copies[i].wait()
            live = plan_ref[LENGTH, first + i]
            above, below = i * prefill, i * prefill + short

            @pl.when(live > short)
            def _():
                o_ref[above : above + prefill] = jnp.dot(
                    rows[i], held[i], preferred_element_type=F32
                ).astype(BF)

            @pl.when(live <= short)
            def _():
                o_ref[above:below] = jnp.dot(
                    rows[i, :short], held[i], preferred_element_type=F32
                ).astype(BF)
                o_ref[below : below + short] = jnp.zeros((short, ranks), BF)

    return pl.pallas_call(
        body,
        out_shape=jax.ShapeDtypeStruct((count * prefill, ranks), BF),
        grid_spec=pltpu.PrefetchScalarGridSpec(
            num_scalar_prefetch=1,
            grid=(),
            in_specs=[HBM] * (1 + n_map + n_after),
            out_specs=pl.BlockSpec(memory_space=pltpu.VMEM),
            scratch_shapes=[
                pltpu.VMEM((count, prefill, features), BF),
                pltpu.VMEM((count, features, ranks), BF),
                pltpu.SemaphoreType.DMA((2, count)),
            ],
        ),
        compiler_params=params(16),
        cost_estimate=cost(2 * count * prefill * features * ranks, 2 * count * features * (prefill + ranks)),
        name="rank_products",
    )(plan, hidden, *maps.values(), *after)


def finish(plan, bases, ranks, maps, before, first, count, prefill, shape):
    sources = list(maps)
    columns, depth = shape[2], ranks[0][2][0].shape[1] // 2
    _, packed, lanes = maps[sources[0]].shape
    tiles = columns // lanes
    extra = tiles * 2 * depth
    up_part = pl.ds(packed - extra, extra)
    half = prefill // 2
    n_map = len(maps)
    n_base = max(len(pieces) for _, _, pieces in bases)
    n_rank = max(len(pieces) for _, _, pieces in ranks)

    def body(plan_ref, *rest):
        base_refs, rank_refs = [], []
        for refs, pieces in ((base_refs, bases), (rank_refs, ranks)):
            for start, n, arrays in pieces:
                refs.append((start, n, rest[: len(arrays)]))
                rest = rest[len(arrays) :]
        map_refs = list(zip(sources, rest[:n_map]))
        o_ref, token_ref, ups, base_rows, rank_rows, out_rows, sems, out_sems = rest[-8:]
        token_ref[...] = jnp.zeros_like(token_ref)

        def start_pieces(refs, at, rows, sem):
            copies = []
            for start, n, arrays in refs:
                if start <= at < start + n:
                    block = pl.ds((at - start) * prefill, prefill)
                    for k, ref in enumerate(arrays):
                        source = ref.at[0, block] if len(ref.shape) == 3 else ref.at[block]
                        copies.append(pltpu.make_async_copy(source, rows.at[k], sem.at[k]))
                        copies[-1].start()
            return copies

        copies = []
        for i in range(count):
            at = first + i
            copies.append(
                start_pieces(base_refs, at, base_rows.at[i], sems.at[i])
                + start_pieces(
                    rank_refs, at, rank_rows.at[i], sems.at[i, pl.ds(n_base, n_rank)]
                )
            )
            fetch(
                map_refs,
                plan_ref[SOURCE, at],
                plan_ref[ROW, at],
                up_part,
                ups.at[i],
                sems.at[i, n_base + n_rank],
            )

        group = half // tiles
        mix_row = lax.broadcasted_iota(jnp.int32, (2 * half, 2 * half), 0)
        mix_column = lax.broadcasted_iota(jnp.int32, (2 * half, 2 * half), 1)
        mix_token, mix_tile = mix_row // (2 * tiles), mix_row // 2 % tiles
        mix = mix_column == (mix_row % 2 * tiles + mix_tile) * group + mix_token
        mix = mix.astype(F32).astype(BF)
        token = lax.broadcasted_iota(jnp.int32, (half, 2 * columns), 0)

        def rows_for(i, live, b):
            rows = slice(b * half, (b + 1) * half)
            rank = rank_rows[i, 0, rows].astype(F32)
            for k in range(1, n_rank):
                rank += rank_rows[i, k, rows].astype(F32)
            rank = rank.astype(BF)
            up = jnp.concatenate(
                [ups[i, j * 2 * depth : (j + 1) * 2 * depth] for j in range(tiles)], 1
            )
            total = jnp.concatenate(
                [
                    jnp.dot(
                        rank[:, s * depth : (s + 1) * depth],
                        up[s * depth : (s + 1) * depth],
                        preferred_element_type=F32,
                    )
                    for s in range(2)
                ],
                1,
            )
            for k in range(n_base):
                total += base_rows[i, k, rows].astype(F32)
            total = jnp.where(token + b * half < live, total, 0.0).astype(BF)
            parts = [
                jnp.concatenate(
                    [
                        total[g * group : (g + 1) * group, k * lanes : (k + 1) * lanes]
                        for k in range(2 * tiles)
                    ],
                    0,
                )
                for g in range(tiles)
            ]
            mixed = jnp.dot(
                mix, jnp.concatenate(parts, 1), preferred_element_type=F32
            ).astype(BF)
            for g in range(tiles):
                at = b * half * tiles + g * half
                out_rows[i, at : at + half] = mixed[
                    :, g * lanes : (g + 1) * lanes
                ].reshape(half, 2, lanes)

        outs = []
        for i in range(count):
            for copy in copies[i]:
                copy.wait()
            pltpu.make_async_copy(
                map_refs[0][1].at[0, up_part], ups.at[i], sems.at[i, n_base + n_rank]
            ).wait()
            live = plan_ref[LENGTH, first + i]
            rows_for(i, live, 0)

            @pl.when(live > half)
            def _():
                rows_for(i, live, 1)

            @pl.when(live <= half)
            def _():
                out_rows[i, half * tiles :] = jnp.zeros((half * tiles, 2, lanes), BF)

            block = prefill * tiles
            row = pl.multiple_of(plan_ref[ORDER, first + i] * block, block)
            outs.append(
                pltpu.make_async_copy(
                    out_rows.at[i], o_ref.at[pl.ds(row, block)], out_sems.at[i]
                )
            )
            outs[-1].start()
        for copy in outs:
            copy.wait()

    operands = [plan]
    for _, _, pieces in bases + ranks:
        operands += pieces
    operands += maps.values()
    aliases = {}
    if before is not None:
        aliases = {len(operands): 0}
        operands.append(before)
    return pl.pallas_call(
        body,
        out_shape=(
            jax.ShapeDtypeStruct((shape[0] * tiles, 2, lanes), BF),
            jax.ShapeDtypeStruct((8, 128), F32),
        ),
        grid_spec=pltpu.PrefetchScalarGridSpec(
            num_scalar_prefetch=1,
            grid=(),
            in_specs=[HBM] * (len(operands) - 1),
            out_specs=(HBM, pl.BlockSpec(memory_space=pltpu.VMEM)),
            scratch_shapes=[
                pltpu.VMEM((count, extra, lanes), BF),
                pltpu.VMEM((count, n_base, prefill, 2 * columns), BF),
                pltpu.VMEM((count, n_rank, prefill, 2 * depth), BF),
                pltpu.VMEM((count, prefill * tiles, 2, lanes), BF),
                pltpu.SemaphoreType.DMA((count, n_base + n_rank + 1)),
                pltpu.SemaphoreType.DMA((count,)),
            ],
        ),
        input_output_aliases=aliases,
        compiler_params=params(24),
        cost_estimate=cost(12 * count * prefill * prefill * 2 * columns, 20 * count * prefill * columns),
        name="finish",
    )(*operands)


def solution(mesh):
    n_z, n_t = mesh.shape["adapter"], mesh.shape["tensor"]
    n_x = n_t // 2

    def core_swap(a):
        return lax.ppermute(a, "tensor", [(t, t ^ 1) for t in range(n_t)])

    def chip_shift(a, k):
        return lax.ppermute(
            a,
            "tensor",
            [(2 * x + c, 2 * ((x + k) % n_x) + c) for x in range(n_x) for c in (0, 1)],
        )

    def leftward(a, hops=1):
        return lax.ppermute(a, "adapter", [(z, z - hops) for z in range(hops, n_z)])

    def rightward(a, hops=1):
        return lax.ppermute(a, "adapter", [(z - hops, z) for z in range(hops, n_z)])

    def per_device(hidden, weight, down, up, table, adapters, lengths):
        requests = adapters.shape[0]
        prefill = hidden.shape[0] // requests
        stored = down.shape[0]
        columns = up.shape[3]
        by_distance = n_z == RANK_CHUNKS
        z, t = lax.axis_index("adapter"), lax.axis_index("tensor")
        plan = plan_requests(
            table, adapters, lengths, jnp.reshape(z, (1,)), n_z, stored
        )

        downs = {0: pack_maps(down, up)}

        def relay(hops, after):
            left, right = downs[hops - 1], downs[0 if hops == 1 else n_z + hops - 2]
            if after:
                left, right = hold([left, right], after)
                downs[hops - 1], downs[n_z + hops - 2] = left, right
            downs[hops] = leftward(left)
            downs[n_z - 1 + hops] = rightward(right)

        relay(1, [])

        def within(maps, hops):
            keys = range(hops + 1), range(n_z, n_z + hops)
            return {(k,): maps[k] for part in keys for k in part}

        dest = jnp.arange(n_t, dtype=jnp.int32)
        away = (dest // 2 - t // 2 + n_x) % n_x
        slots = jnp.where(dest % 2 == t % 2, n_x + away, away)

        bases, pairs = [], []

        def send_on(first, count, sends, keep, after):
            got = [core_swap(part) for part in sends[1:]] + [core_swap(sends[0])]
            pieces = [keep, got.pop()]
            n_piece = len(pieces_of(count))
            for k in range(1, n_x):
                pairs.append(pair_sum(keep, got[(k - 1) * n_piece : k * n_piece], k, after))
                pieces.append(chip_shift(pairs[-1], k))
            bases.append((first, count, pieces))

        def base(chunk):
            first, count = sum(BASE_CHUNKS[:chunk]), BASE_CHUNKS[chunk]
            return (first, count) + base_products(
                plan, hidden, split, first, count, prefill, pairs[-1:]
            )

        ranks = []
        count = requests // RANK_CHUNKS

        def rank(chunk, after):
            hops = chunk if by_distance else n_z - 1
            part = rank_products(
                plan, hidden, within(downs, hops), chunk * count, count, prefill, after
            )
            pair = (part.astype(F32) + core_swap(part).astype(F32)).astype(BF)
            pieces = [pair] + [chip_shift(pair, k) for k in range(1, n_x)]
            ranks.append((chunk * count, count, pieces))
            return part

        shape = (requests * prefill, 2, columns)

        def write(out, first, last):
            held = [
                b
                for b in bases
                if b[0] < last * count and b[0] + b[1] > first * count
            ]
            return finish(
                plan,
                held,
                ranks[first:last],
                within(downs, last - 1 if by_distance else n_z - 1),
                out,
                first * count,
                (last - first) * count,
                prefill,
                shape,
            )

        split, sends, keep = split_weight(
            plan, slots, hidden, weight, BASE_CHUNKS[0], prefill
        )
        send_on(0, BASE_CHUNKS[0], sends, keep, [])
        second = base(1)
        if n_z > 2:
            relay(2, [second[3]])
        send_on(*second, [bases[0][2][-1]])
        third = base(2)
        part = third[3]
        if by_distance:
            part = rank(0, [third[3], bases[1][2][-1]])
        send_on(*third, [part, bases[1][2][-1]])
        fourth = base(3)
        for hops in range(3, n_z):
            relay(hops, [fourth[3]])
        part = fourth[3]
        if by_distance:
            part = rank(1, [part])
            part = rank(2, [part, bases[2][2][-1]])
        summed = [pieces[-1] for _, _, pieces in ranks[:2]]
        send_on(*fourth, [part, bases[2][2][-1]] + summed)
        for chunk in range(len(ranks), 3):
            part = rank(chunk, [pairs[-1]])
        out, _ = write(None, 0, 2)
        out, written = write(out, 2, 3)
        rank(3, [written, bases[3][2][-1]])
        out, _ = write(out, 3, 4)
        tiles = out.shape[0] // shape[0]
        out = out.reshape(shape[0], tiles, 2, columns // tiles)
        return out.transpose(0, 2, 1, 3).reshape(shape)

    return jax.shard_map(
        per_device,
        mesh=mesh,
        in_specs=(
            P(("group", "adapter"), "tensor"),
            P("tensor", None, None),
            P(("group", "adapter"), "tensor", None),
            P(("group", "adapter"), None, None, "tensor"),
            P("group"),
            P(("group", "adapter")),
            P(("group", "adapter")),
        ),
        out_specs=P(("group", "adapter"), None, "tensor"),
        check_vma=False,
    )
```

```python
import jax
import jax.numpy as jnp
from jax import lax
from jax.experimental import pallas as pl
from jax.experimental.pallas import tpu as pltpu
from jax.sharding import PartitionSpec as P

BF = jnp.bfloat16
F32 = jnp.float32
BASE_CHUNKS = (3, 3, 4, 2)
RANK_CHUNKS = 4
SMEM = pltpu.SMEM
PIECE = 2


def pieces_of(count):
    return [(at, min(PIECE, count - at)) for at in range(0, count, PIECE)]


ANY = pl.BlockSpec(memory_space=pl.ANY)
HBM = pl.BlockSpec(memory_space=pltpu.HBM)


def cost(flops, moved):
    return pl.CostEstimate(
        flops=int(flops * 0.01), bytes_accessed=int(moved * 0.01), transcendentals=0
    )


ORDER, SOURCE, ROW, LENGTH = range(4)


def params(mib=60):
    return pltpu.CompilerParams(vmem_limit_bytes=mib * 1024 * 1024)


def pack_maps(down, up):
    stored, features, lanes = down.shape
    _, sides, depth, columns = up.shape
    tiles = columns // lanes
    part = sides * depth

    def body(down_ref, up_ref, o_ref, held, sems):
        copies = []
        for a in range(stored):
            copies.append(
                pltpu.make_async_copy(
                    down_ref.at[a], o_ref.at[a, pl.ds(0, features)], sems.at[0, a]
                )
            )
            copies[-1].start()
        for a in range(stored):
            flat = up_ref[a].reshape(part, columns)
            for j in range(tiles):
                held[a, j * part : (j + 1) * part] = flat[:, j * lanes : (j + 1) * lanes]
            copies.append(
                pltpu.make_async_copy(
                    held.at[a],
                    o_ref.at[a, pl.ds(features, tiles * part)],
                    sems.at[1, a],
                )
            )
            copies[-1].start()
        for copy in copies:
            copy.wait()

    return pl.pallas_call(
        body,
        out_shape=jax.ShapeDtypeStruct((stored, features + tiles * part, lanes), BF),
        in_specs=[pl.BlockSpec(memory_space=pltpu.VMEM)] * 2,
        out_specs=HBM,
        scratch_shapes=[
            pltpu.VMEM((stored, tiles * part, lanes), BF),
            pltpu.SemaphoreType.DMA((2, stored)),
        ],
        compiler_params=params(24),
        cost_estimate=cost(0, 4 * down.size),
        name="pack_maps",
    )(down, up)


def plan_requests(table, adapters, lengths, here, n_z, stored):
    requests, known = adapters.shape[0], table.shape[0]
    shape = (requests, 128)

    def body(table_ref, adapter_ref, length_ref, here_ref, plan_ref):
        me = here_ref[0]
        request = lax.broadcasted_iota(jnp.int32, shape, 0)
        lane = lax.broadcasted_iota(jnp.int32, shape, 1)
        diagonal = request == lane

        def wide(ref, n):
            return jnp.pad(ref[...], ((0, 0), (0, 128 - n)))

        def down(a):
            return jnp.sum(jnp.where(diagonal, a, 0), axis=1, keepdims=True)

        def across(a):
            return jnp.sum(jnp.where(diagonal, a, 0), axis=0, keepdims=True)

        hit = (down(wide(adapter_ref, requests)) == lane) & (lane < known)
        slot = jnp.sum(jnp.where(hit, wide(table_ref, known), 0), 1, keepdims=True)
        owner = jnp.zeros_like(slot)
        for z in range(1, n_z):
            owner += jnp.where(slot >= z * stored, 1, 0)
        source = jnp.where(owner >= me, owner - me, n_z - 1 + me - owner)
        key = jnp.abs(owner - me) * 128 + request[:, :1]
        before = (across(key) < key) & (lane < requests)
        place = jnp.sum(jnp.where(before, 1, 0), axis=1, keepdims=True)
        at = place == lane

        def placed(a):
            return jnp.sum(jnp.where(at, a, 0), axis=0, keepdims=True)

        plan_ref[ORDER : ORDER + 1] = placed(request)
        plan_ref[SOURCE : SOURCE + 1] = placed(source)
        plan_ref[ROW : ROW + 1] = placed(slot - owner * stored)
        plan_ref[LENGTH : LENGTH + 1] = placed(down(wide(length_ref, requests)))

    vmem = pl.BlockSpec(memory_space=pltpu.VMEM)
    return pl.pallas_call(
        body,
        out_shape=jax.ShapeDtypeStruct((8, 128), jnp.int32),
        in_specs=[vmem, vmem, vmem, pl.BlockSpec(memory_space=SMEM)],
        out_specs=vmem,
        cost_estimate=cost(0, 1 << 20),
        name="plan_requests",
    )(table[None, :], adapters[None, :], lengths[None, :], here)


def split_weight(plan, slots, hidden, weight, count, prefill):
    features, _, columns = weight.shape
    n_t = slots.shape[0]
    n_x = n_t // 2
    width = columns // n_t
    rows, half = 512, 128
    steps = features // rows

    def body(plan_ref, slot_ref, *rest):
        x_refs, (w_ref, o_ref, *send_refs, keep_ref, total) = rest[:count], rest[count:]
        step = pl.program_id(0)
        above = pl.multiple_of(step * rows, rows)
        out_row = lax.broadcasted_iota(jnp.int32, (2 * half, 2 * half), 0)
        in_row = lax.broadcasted_iota(jnp.int32, (2 * half, 2 * half), 1)
        pick = in_row == 2 * (out_row % half) + out_row // half
        pick = pick.astype(F32).astype(BF)
        for b in range(rows // half):
            mixed = w_ref[b * half : (b + 1) * half].reshape(2 * half, columns)
            apart = jnp.dot(pick, mixed, preferred_element_type=F32).astype(BF)
            for t in range(n_t):
                for s in range(2):
                    o_ref[
                        slot_ref[t],
                        pl.ds(above + b * half, half),
                        s * width : (s + 1) * width,
                    ] = apart[s * half : (s + 1) * half, t * width : (t + 1) * width]

        @pl.when(step == 0)
        def _():
            total[...] = jnp.zeros_like(total)

        for r in range(count):
            for j in range(n_t):
                total[j, r * prefill : (r + 1) * prefill] += jnp.dot(
                    x_refs[r][...], o_ref[j, pl.ds(above, rows)], preferred_element_type=F32
                )

        @pl.when(step == steps - 1)
        def _():
            send_refs[0][...] = total[0].astype(BF)
            k = 1
            for j in range(1, n_x):
                for at, n in pieces_of(count):
                    rows_of = slice(at * prefill, (at + n) * prefill)
                    send_refs[k][...] = total[j, rows_of].astype(BF)
                    k += 1
            for j in range(n_x):
                keep_ref[j] = total[n_x + j].astype(BF)

    part = (count * prefill, 2 * width)
    outs = [part] + [
        (n * prefill, 2 * width) for _, n in pieces_of(count)
    ] * (n_x - 1)
    split, *sends, keep = pl.pallas_call(
        body,
        out_shape=(
            jax.ShapeDtypeStruct((n_t, features, 2 * width), BF),
            *[jax.ShapeDtypeStruct(out, BF) for out in outs],
            jax.ShapeDtypeStruct((n_x, *part), BF),
        ),
        grid_spec=pltpu.PrefetchScalarGridSpec(
            num_scalar_prefetch=2,
            grid=(steps,),
            in_specs=[
                pl.BlockSpec((prefill, rows), lambda i, p, s, r=r: (p[ORDER, r], i))
                for r in range(count)
            ]
            + [pl.BlockSpec((rows, 2, columns), lambda i, p, s: (i, 0, 0))],
            out_specs=(
                pl.BlockSpec(memory_space=pltpu.VMEM),
                *[pl.BlockSpec(out, lambda i, p, s: (0, 0)) for out in outs],
                pl.BlockSpec((n_x, *part), lambda i, p, s: (0, 0, 0)),
            ),
            scratch_shapes=[pltpu.VMEM((n_t, count * prefill, 2 * width), F32)],
        ),
        compiler_params=params(46),
        cost_estimate=cost(2 * count * prefill * features * 2 * columns, 8 * features * columns),
        name="split_weight",
    )(plan, slots, *[hidden] * count, weight)
    return split, sends, keep


def base_products(plan, hidden, weight, first, count, prefill, after):
    n_t, features, width = weight.shape
    n_x = n_t // 2
    short = prefill // 2
    n_after = len(after)

    def body(plan_ref, x_ref, *rest):
        w_ref = rest[0]
        *send_refs, keep_ref = rest[1 + n_after :]
        live = plan_ref[LENGTH, first + pl.program_id(0)]

        def products(rows):
            dead = jnp.zeros((prefill - rows, width), BF)
            for j in range(n_t):
                out = jnp.dot(
                    x_ref[:rows], w_ref[j], preferred_element_type=F32
                ).astype(BF)
                if rows < prefill:
                    out = jnp.concatenate([out, dead], 0)
                if j == 0:
                    send_refs[0][...] = out
                elif j >= n_x:
                    keep_ref[j - n_x] = out
                else:

                    spans = pieces_of(count)
                    for k, (at, n) in enumerate(spans, 1 + (j - 1) * len(spans)):
                        inside = (pl.program_id(0) >= at) & (pl.program_id(0) < at + n)

                        @pl.when(inside)
                        def _():
                            send_refs[k][...] = out

        @pl.when(live > short)
        def _():
            products(prefill)

        @pl.when(live <= short)
        def _():
            products(short)

    spans = [(0, count)] + pieces_of(count) * (n_x - 1)
    parts = [n for _, n in spans]
    block = (prefill, width)
    places = [
        lambda i, p, at=at, n=n: (jnp.clip(i - at, 0, n - 1), 0) for at, n in spans
    ]
    *sends, keep = pl.pallas_call(
        body,
        out_shape=(
            *[jax.ShapeDtypeStruct((n * prefill, width), BF) for n in parts],
            jax.ShapeDtypeStruct((n_x, count * prefill, width), BF),
        ),
        grid_spec=pltpu.PrefetchScalarGridSpec(
            num_scalar_prefetch=1,
            grid=(count,),
            in_specs=[
                pl.BlockSpec(
                    (prefill, features), lambda i, p: (p[ORDER, first + i], 0)
                ),
            ]
            + [pl.BlockSpec(memory_space=pltpu.VMEM)]
            + [ANY] * n_after,
            out_specs=(
                *[pl.BlockSpec(block, place) for place in places],
                pl.BlockSpec((n_x, prefill, width), lambda i, p: (0, i, 0)),
            ),
        ),
        compiler_params=params(46),
        cost_estimate=cost(2 * count * prefill * features * width * n_t, 2 * n_t * features * width),
        name="base_products",
    )(plan, hidden, weight, *after)
    return sends, keep


def pair_sum(one, others, index, after):
    _, rows, width = one.shape
    n_piece = len(others)

    def body(a_ref, *rest):
        b_refs = rest[:n_piece]
        o_ref, mine, theirs, total, sems, out_sems = rest[n_piece + len(after) :]
        copies, outs = [], []
        spans, at = [], 0
        for b_ref in b_refs:
            spans.append(pl.ds(at, b_ref.shape[0]))
            at += b_ref.shape[0]
        for k, span in enumerate(spans):
            copies.append(
                (
                    pltpu.make_async_copy(
                        a_ref.at[index, span], mine.at[span], sems.at[0, k]
                    ),
                    pltpu.make_async_copy(b_refs[k], theirs.at[span], sems.at[1, k]),
                )
            )
            for copy in copies[-1]:
                copy.start()
        for k, span in enumerate(spans):
            for copy in copies[k]:
                copy.wait()
            value = mine[span].astype(F32) + theirs[span].astype(F32)
            total[span] = value.astype(BF)
            outs.append(
                pltpu.make_async_copy(total.at[span], o_ref.at[span], out_sems.at[k])
            )
            outs[-1].start()
        for copy in outs:
            copy.wait()

    return pl.pallas_call(
        body,
        out_shape=jax.ShapeDtypeStruct((rows, width), BF),
        in_specs=[ANY] * (1 + n_piece + len(after)),
        out_specs=ANY,
        scratch_shapes=[pltpu.VMEM((rows, width), BF)] * 3
        + [pltpu.SemaphoreType.DMA((2, n_piece)), pltpu.SemaphoreType.DMA((n_piece,))],
        compiler_params=params(12),
        cost_estimate=cost(rows * width, 6 * rows * width),
        name="pair_sum",
    )(one, *others, *after)


def hold(arrays, after):
    n = len(arrays)

    def body(*refs):
        pass

    return pl.pallas_call(
        body,
        out_shape=[jax.ShapeDtypeStruct(a.shape, a.dtype) for a in arrays],
        in_specs=[HBM] * (n + len(after)),
        out_specs=[HBM] * n,
        input_output_aliases={i: i for i in range(n)},
        compiler_params=params(8),
        cost_estimate=cost(0, 1 << 20),
        name="hold",
    )(*arrays, *after)


def fetch(refs, source, row, part, target, sem):
    for codes, ref in refs:
        hit = source == codes[0]
        for code in codes[1:]:
            hit |= source == code

        @pl.when(hit)
        def _():
            pltpu.make_async_copy(ref.at[row, part], target, sem).start()


def rank_products(plan, hidden, maps, first, count, prefill, after):
    sources = list(maps)
    features, ranks = hidden.shape[1], maps[sources[0]].shape[2]
    n_map, n_after = len(maps), len(after)
    short = prefill // 2
    down = pl.ds(0, features)

    def body(plan_ref, x_ref, *rest):
        refs = list(zip(sources, rest[:n_map]))
        o_ref, rows, held, sems = rest[n_map + n_after :]
        copies = []
        for i in range(count):
            fetch(
                refs,
                plan_ref[SOURCE, first + i],
                plan_ref[ROW, first + i],
                down,
                held.at[i],
                sems.at[0, i],
            )
            at = pl.multiple_of(plan_ref[ORDER, first + i] * prefill, prefill)
            copies.append(
                pltpu.make_async_copy(
                    x_ref.at[pl.ds(at, prefill)], rows.at[i], sems.at[1, i]
                )
            )
            copies[-1].start()
        for i in range(count):
            pltpu.make_async_copy(
                rest[0].at[0, down], held.at[i], sems.at[0, i]
            ).wait()
            copies[i].wait()
            live = plan_ref[LENGTH, first + i]
            above, below = i * prefill, i * prefill + short

            @pl.when(live > short)
            def _():
                o_ref[above : above + prefill] = jnp.dot(
                    rows[i], held[i], preferred_element_type=F32
                ).astype(BF)

            @pl.when(live <= short)
            def _():
                o_ref[above:below] = jnp.dot(
                    rows[i, :short], held[i], preferred_element_type=F32
                ).astype(BF)
                o_ref[below : below + short] = jnp.zeros((short, ranks), BF)

    return pl.pallas_call(
        body,
        out_shape=jax.ShapeDtypeStruct((count * prefill, ranks), BF),
        grid_spec=pltpu.PrefetchScalarGridSpec(
            num_scalar_prefetch=1,
            grid=(),
            in_specs=[HBM] * (1 + n_map + n_after),
            out_specs=pl.BlockSpec(memory_space=pltpu.VMEM),
            scratch_shapes=[
                pltpu.VMEM((count, prefill, features), BF),
                pltpu.VMEM((count, features, ranks), BF),
                pltpu.SemaphoreType.DMA((2, count)),
            ],
        ),
        compiler_params=params(16),
        cost_estimate=cost(2 * count * prefill * features * ranks, 2 * count * features * (prefill + ranks)),
        name="rank_products",
    )(plan, hidden, *maps.values(), *after)


def finish(plan, bases, ranks, maps, before, first, count, prefill, shape):
    sources = list(maps)
    columns, depth = shape[2], ranks[0][2][0].shape[1] // 2
    _, packed, lanes = maps[sources[0]].shape
    tiles = columns // lanes
    extra = tiles * 2 * depth
    up_part = pl.ds(packed - extra, extra)
    half = prefill // 2
    n_map = len(maps)
    n_base = max(len(pieces) for _, _, pieces in bases)
    n_rank = max(len(pieces) for _, _, pieces in ranks)

    def body(plan_ref, *rest):
        base_refs, rank_refs = [], []
        for refs, pieces in ((base_refs, bases), (rank_refs, ranks)):
            for start, n, arrays in pieces:
                refs.append((start, n, rest[: len(arrays)]))
                rest = rest[len(arrays) :]
        map_refs = list(zip(sources, rest[:n_map]))
        o_ref, token_ref, ups, base_rows, rank_rows, out_rows, sems, out_sems = rest[-8:]
        token_ref[...] = jnp.zeros_like(token_ref)

        def start_pieces(refs, at, rows, sem):
            copies = []
            for start, n, arrays in refs:
                if start <= at < start + n:
                    block = pl.ds((at - start) * prefill, prefill)
                    for k, ref in enumerate(arrays):
                        source = ref.at[0, block] if len(ref.shape) == 3 else ref.at[block]
                        copies.append(pltpu.make_async_copy(source, rows.at[k], sem.at[k]))
                        copies[-1].start()
            return copies

        copies = []
        for i in range(count):
            at = first + i
            copies.append(
                start_pieces(base_refs, at, base_rows.at[i], sems.at[i])
                + start_pieces(
                    rank_refs, at, rank_rows.at[i], sems.at[i, pl.ds(n_base, n_rank)]
                )
            )
            fetch(
                map_refs,
                plan_ref[SOURCE, at],
                plan_ref[ROW, at],
                up_part,
                ups.at[i],
                sems.at[i, n_base + n_rank],
            )

        group = half // tiles
        mix_row = lax.broadcasted_iota(jnp.int32, (2 * half, 2 * half), 0)
        mix_column = lax.broadcasted_iota(jnp.int32, (2 * half, 2 * half), 1)
        mix_token, mix_tile = mix_row // (2 * tiles), mix_row // 2 % tiles
        mix = mix_column == (mix_row % 2 * tiles + mix_tile) * group + mix_token
        mix = mix.astype(F32).astype(BF)
        token = lax.broadcasted_iota(jnp.int32, (half, 2 * columns), 0)

        def rows_for(i, live, b):
            rows = slice(b * half, (b + 1) * half)
            rank = rank_rows[i, 0, rows].astype(F32)
            for k in range(1, n_rank):
                rank += rank_rows[i, k, rows].astype(F32)
            rank = rank.astype(BF)
            up = jnp.concatenate(
                [ups[i, j * 2 * depth : (j + 1) * 2 * depth] for j in range(tiles)], 1
            )
            total = jnp.concatenate(
                [
                    jnp.dot(
                        rank[:, s * depth : (s + 1) * depth],
                        up[s * depth : (s + 1) * depth],
                        preferred_element_type=F32,
                    )
                    for s in range(2)
                ],
                1,
            )
            for k in range(n_base):
                total += base_rows[i, k, rows].astype(F32)
            total = jnp.where(token + b * half < live, total, 0.0).astype(BF)
            parts = [
                jnp.concatenate(
                    [
                        total[g * group : (g + 1) * group, k * lanes : (k + 1) * lanes]
                        for k in range(2 * tiles)
                    ],
                    0,
                )
                for g in range(tiles)
            ]
            mixed = jnp.dot(
                mix, jnp.concatenate(parts, 1), preferred_element_type=F32
            ).astype(BF)
            for g in range(tiles):
                at = b * half * tiles + g * half
                out_rows[i, at : at + half] = mixed[
                    :, g * lanes : (g + 1) * lanes
                ].reshape(half, 2, lanes)

        outs = []
        for i in range(count):
            for copy in copies[i]:
                copy.wait()
            pltpu.make_async_copy(
                map_refs[0][1].at[0, up_part], ups.at[i], sems.at[i, n_base + n_rank]
            ).wait()
            live = plan_ref[LENGTH, first + i]
            rows_for(i, live, 0)

            @pl.when(live > half)
            def _():
                rows_for(i, live, 1)

            @pl.when(live <= half)
            def _():
                out_rows[i, half * tiles :] = jnp.zeros((half * tiles, 2, lanes), BF)

            block = prefill * tiles
            row = pl.multiple_of(plan_ref[ORDER, first + i] * block, block)
            outs.append(
                pltpu.make_async_copy(
                    out_rows.at[i], o_ref.at[pl.ds(row, block)], out_sems.at[i]
                )
            )
            outs[-1].start()
        for copy in outs:
            copy.wait()

    operands = [plan]
    for _, _, pieces in bases + ranks:
        operands += pieces
    operands += maps.values()
    aliases = {}
    if before is not None:
        aliases = {len(operands): 0}
        operands.append(before)
    return pl.pallas_call(
        body,
        out_shape=(
            jax.ShapeDtypeStruct((shape[0] * tiles, 2, lanes), BF),
            jax.ShapeDtypeStruct((8, 128), F32),
        ),
        grid_spec=pltpu.PrefetchScalarGridSpec(
            num_scalar_prefetch=1,
            grid=(),
            in_specs=[HBM] * (len(operands) - 1),
            out_specs=(HBM, pl.BlockSpec(memory_space=pltpu.VMEM)),
            scratch_shapes=[
                pltpu.VMEM((count, extra, lanes), BF),
                pltpu.VMEM((count, n_base, prefill, 2 * columns), BF),
                pltpu.VMEM((count, n_rank, prefill, 2 * depth), BF),
                pltpu.VMEM((count, prefill * tiles, 2, lanes), BF),
                pltpu.SemaphoreType.DMA((count, n_base + n_rank + 1)),
                pltpu.SemaphoreType.DMA((count,)),
            ],
        ),
        input_output_aliases=aliases,
        compiler_params=params(24),
        cost_estimate=cost(12 * count * prefill * prefill * 2 * columns, 20 * count * prefill * columns),
        name="finish",
    )(*operands)


def solution(mesh):
    n_z, n_t = mesh.shape["adapter"], mesh.shape["tensor"]
    n_x = n_t // 2

    def core_swap(a):
        return lax.ppermute(a, "tensor", [(t, t ^ 1) for t in range(n_t)])

    def chip_shift(a, k):
        return lax.ppermute(
            a,
            "tensor",
            [(2 * x + c, 2 * ((x + k) % n_x) + c) for x in range(n_x) for c in (0, 1)],
        )

    def leftward(a, hops=1):
        return lax.ppermute(a, "adapter", [(z, z - hops) for z in range(hops, n_z)])

    def rightward(a, hops=1):
        return lax.ppermute(a, "adapter", [(z - hops, z) for z in range(hops, n_z)])

    def per_device(hidden, weight, down, up, table, adapters, lengths):
        requests = adapters.shape[0]
        prefill = hidden.shape[0] // requests
        stored = down.shape[0]
        columns = up.shape[3]
        by_distance = n_z == RANK_CHUNKS
        z, t = lax.axis_index("adapter"), lax.axis_index("tensor")
        plan = plan_requests(
            table, adapters, lengths, jnp.reshape(z, (1,)), n_z, stored
        )

        downs = {0: pack_maps(down, up)}

        def relay(hops, after):
            left, right = downs[hops - 1], downs[0 if hops == 1 else n_z + hops - 2]
            if after:
                left, right = hold([left, right], after)
                downs[hops - 1], downs[n_z + hops - 2] = left, right
            downs[hops] = leftward(left)
            downs[n_z - 1 + hops] = rightward(right)

        relay(1, [])

        def within(maps, hops):
            keys = range(hops + 1), range(n_z, n_z + hops)
            return {(k,): maps[k] for part in keys for k in part}

        dest = jnp.arange(n_t, dtype=jnp.int32)
        away = (dest // 2 - t // 2 + n_x) % n_x
        slots = jnp.where(dest % 2 == t % 2, n_x + away, away)

        bases, pairs = [], []

        def send_on(first, count, sends, keep, after):
            got = [core_swap(part) for part in sends[1:]] + [core_swap(sends[0])]
            pieces = [keep, got.pop()]
            n_piece = len(pieces_of(count))
            for k in range(1, n_x):
                pairs.append(pair_sum(keep, got[(k - 1) * n_piece : k * n_piece], k, after))
                pieces.append(chip_shift(pairs[-1], k))
            bases.append((first, count, pieces))

        def base(chunk):
            first, count = sum(BASE_CHUNKS[:chunk]), BASE_CHUNKS[chunk]
            return (first, count) + base_products(
                plan, hidden, split, first, count, prefill, pairs[-1:]
            )

        ranks = []
        count = requests // RANK_CHUNKS

        def rank(chunk, after):
            hops = chunk if by_distance else n_z - 1
            part = rank_products(
                plan, hidden, within(downs, hops), chunk * count, count, prefill, after
            )
            pair = (part.astype(F32) + core_swap(part).astype(F32)).astype(BF)
            pieces = [pair] + [chip_shift(pair, k) for k in range(1, n_x)]
            ranks.append((chunk * count, count, pieces))
            return part

        shape = (requests * prefill, 2, columns)

        def write(out, first, last):
            held = [
                b
                for b in bases
                if b[0] < last * count and b[0] + b[1] > first * count
            ]
            return finish(
                plan,
                held,
                ranks[first:last],
                within(downs, last - 1 if by_distance else n_z - 1),
                out,
                first * count,
                (last - first) * count,
                prefill,
                shape,
            )

        split, sends, keep = split_weight(
            plan, slots, hidden, weight, BASE_CHUNKS[0], prefill
        )
        send_on(0, BASE_CHUNKS[0], sends, keep, [])
        second = base(1)
        if n_z > 2:
            relay(2, [second[3]])
        send_on(*second, [bases[0][2][-1]])
        third = base(2)
        part = third[3]
        if by_distance:
            part = rank(0, [third[3], bases[1][2][-1]])
        send_on(*third, [part, bases[1][2][-1]])
        fourth = base(3)
        for hops in range(3, n_z):
            relay(hops, [fourth[3]])
        part = fourth[3]
        if by_distance:
            part = rank(1, [part])
            part = rank(2, [part, bases[2][2][-1]])
        summed = [pieces[-1] for _, _, pieces in ranks[:2]]
        send_on(*fourth, [part, bases[2][2][-1]] + summed)
        for chunk in range(len(ranks), 3):
            part = rank(chunk, [pairs[-1]])
        out, written = write(None, 0, 2)
        rank(3, [written, bases[3][2][-1]])
        out, _ = write(out, 2, 3)
        out, _ = write(out, 3, 4)
        tiles = out.shape[0] // shape[0]
        out = out.reshape(shape[0], tiles, 2, columns // tiles)
        return out.transpose(0, 2, 1, 3).reshape(shape)

    return jax.shard_map(
        per_device,
        mesh=mesh,
        in_specs=(
            P(("group", "adapter"), "tensor"),
            P("tensor", None, None),
            P(("group", "adapter"), "tensor", None),
            P(("group", "adapter"), None, None, "tensor"),
            P("group"),
            P(("group", "adapter")),
            P(("group", "adapter")),
        ),
        out_specs=P(("group", "adapter"), None, "tensor"),
        check_vma=False,
    )
```

```python
import jax
import jax.numpy as jnp
from jax import lax
from jax.experimental import pallas as pl
from jax.experimental.pallas import tpu as pltpu
from jax.sharding import PartitionSpec as P

BF = jnp.bfloat16
F32 = jnp.float32
BASE_CHUNKS = (3, 3, 4, 2)
RANK_CHUNKS = 4
SMEM = pltpu.SMEM
PIECE = 2


def pieces_of(count):
    return [(at, min(PIECE, count - at)) for at in range(0, count, PIECE)]


ANY = pl.BlockSpec(memory_space=pl.ANY)
HBM = pl.BlockSpec(memory_space=pltpu.HBM)


def cost(flops, moved):
    return pl.CostEstimate(
        flops=int(flops * 0.01), bytes_accessed=int(moved * 0.01), transcendentals=0
    )


ORDER, SOURCE, ROW, LENGTH = range(4)


def params(mib=60):
    return pltpu.CompilerParams(vmem_limit_bytes=mib * 1024 * 1024)


def pack_maps(down, up):
    stored, features, lanes = down.shape
    _, sides, depth, columns = up.shape
    tiles = columns // lanes
    part = sides * depth

    def body(down_ref, up_ref, o_ref, held, sems):
        copies = []
        for a in range(stored):
            copies.append(
                pltpu.make_async_copy(
                    down_ref.at[a], o_ref.at[a, pl.ds(0, features)], sems.at[0, a]
                )
            )
            copies[-1].start()
        for a in range(stored):
            flat = up_ref[a].reshape(part, columns)
            for j in range(tiles):
                held[a, j * part : (j + 1) * part] = flat[:, j * lanes : (j + 1) * lanes]
            copies.append(
                pltpu.make_async_copy(
                    held.at[a],
                    o_ref.at[a, pl.ds(features, tiles * part)],
                    sems.at[1, a],
                )
            )
            copies[-1].start()
        for copy in copies:
            copy.wait()

    return pl.pallas_call(
        body,
        out_shape=jax.ShapeDtypeStruct((stored, features + tiles * part, lanes), BF),
        in_specs=[pl.BlockSpec(memory_space=pltpu.VMEM)] * 2,
        out_specs=HBM,
        scratch_shapes=[
            pltpu.VMEM((stored, tiles * part, lanes), BF),
            pltpu.SemaphoreType.DMA((2, stored)),
        ],
        compiler_params=params(24),
        cost_estimate=cost(0, 4 * down.size),
        name="pack_maps",
    )(down, up)


def plan_requests(table, adapters, lengths, here, n_z, stored):
    requests, known = adapters.shape[0], table.shape[0]
    shape = (requests, 128)

    def body(table_ref, adapter_ref, length_ref, here_ref, plan_ref):
        me = here_ref[0]
        request = lax.broadcasted_iota(jnp.int32, shape, 0)
        lane = lax.broadcasted_iota(jnp.int32, shape, 1)
        diagonal = request == lane

        def wide(ref, n):
            return jnp.pad(ref[...], ((0, 0), (0, 128 - n)))

        def down(a):
            return jnp.sum(jnp.where(diagonal, a, 0), axis=1, keepdims=True)

        def across(a):
            return jnp.sum(jnp.where(diagonal, a, 0), axis=0, keepdims=True)

        hit = (down(wide(adapter_ref, requests)) == lane) & (lane < known)
        slot = jnp.sum(jnp.where(hit, wide(table_ref, known), 0), 1, keepdims=True)
        owner = jnp.zeros_like(slot)
        for z in range(1, n_z):
            owner += jnp.where(slot >= z * stored, 1, 0)
        source = jnp.where(owner >= me, owner - me, n_z - 1 + me - owner)
        key = jnp.abs(owner - me) * 128 + request[:, :1]
        before = (across(key) < key) & (lane < requests)
        place = jnp.sum(jnp.where(before, 1, 0), axis=1, keepdims=True)
        at = place == lane

        def placed(a):
            return jnp.sum(jnp.where(at, a, 0), axis=0, keepdims=True)

        plan_ref[ORDER : ORDER + 1] = placed(request)
        plan_ref[SOURCE : SOURCE + 1] = placed(source)
        plan_ref[ROW : ROW + 1] = placed(slot - owner * stored)
        plan_ref[LENGTH : LENGTH + 1] = placed(down(wide(length_ref, requests)))

    vmem = pl.BlockSpec(memory_space=pltpu.VMEM)
    return pl.pallas_call(
        body,
        out_shape=jax.ShapeDtypeStruct((8, 128), jnp.int32),
        in_specs=[vmem, vmem, vmem, pl.BlockSpec(memory_space=SMEM)],
        out_specs=vmem,
        cost_estimate=cost(0, 1 << 20),
        name="plan_requests",
    )(table[None, :], adapters[None, :], lengths[None, :], here)


def split_weight(plan, slots, hidden, weight, count, prefill):
    features, _, columns = weight.shape
    n_t = slots.shape[0]
    n_x = n_t // 2
    width = columns // n_t
    rows, half = 512, 128
    steps = features // rows

    def body(plan_ref, slot_ref, *rest):
        x_refs, (w_ref, o_ref, *send_refs, keep_ref, total) = rest[:count], rest[count:]
        step = pl.program_id(0)
        above = pl.multiple_of(step * rows, rows)
        out_row = lax.broadcasted_iota(jnp.int32, (2 * half, 2 * half), 0)
        in_row = lax.broadcasted_iota(jnp.int32, (2 * half, 2 * half), 1)
        pick = in_row == 2 * (out_row % half) + out_row // half
        pick = pick.astype(F32).astype(BF)
        for b in range(rows // half):
            mixed = w_ref[b * half : (b + 1) * half].reshape(2 * half, columns)
            apart = jnp.dot(pick, mixed, preferred_element_type=F32).astype(BF)
            for t in range(n_t):
                for s in range(2):
                    o_ref[
                        slot_ref[t],
                        pl.ds(above + b * half, half),
                        s * width : (s + 1) * width,
                    ] = apart[s * half : (s + 1) * half, t * width : (t + 1) * width]

        @pl.when(step == 0)
        def _():
            total[...] = jnp.zeros_like(total)

        for r in range(count):
            for j in range(n_t):
                total[j, r * prefill : (r + 1) * prefill] += jnp.dot(
                    x_refs[r][...], o_ref[j, pl.ds(above, rows)], preferred_element_type=F32
                )

        @pl.when(step == steps - 1)
        def _():
            send_refs[0][...] = total[0].astype(BF)
            k = 1
            for j in range(1, n_x):
                for at, n in pieces_of(count):
                    rows_of = slice(at * prefill, (at + n) * prefill)
                    send_refs[k][...] = total[j, rows_of].astype(BF)
                    k += 1
            for j in range(n_x):
                keep_ref[j] = total[n_x + j].astype(BF)

    part = (count * prefill, 2 * width)
    outs = [part] + [
        (n * prefill, 2 * width) for _, n in pieces_of(count)
    ] * (n_x - 1)
    split, *sends, keep = pl.pallas_call(
        body,
        out_shape=(
            jax.ShapeDtypeStruct((n_t, features, 2 * width), BF),
            *[jax.ShapeDtypeStruct(out, BF) for out in outs],
            jax.ShapeDtypeStruct((n_x, *part), BF),
        ),
        grid_spec=pltpu.PrefetchScalarGridSpec(
            num_scalar_prefetch=2,
            grid=(steps,),
            in_specs=[
                pl.BlockSpec((prefill, rows), lambda i, p, s, r=r: (p[ORDER, r], i))
                for r in range(count)
            ]
            + [pl.BlockSpec((rows, 2, columns), lambda i, p, s: (i, 0, 0))],
            out_specs=(
                pl.BlockSpec(memory_space=pltpu.VMEM),
                *[pl.BlockSpec(out, lambda i, p, s: (0, 0)) for out in outs],
                pl.BlockSpec((n_x, *part), lambda i, p, s: (0, 0, 0)),
            ),
            scratch_shapes=[pltpu.VMEM((n_t, count * prefill, 2 * width), F32)],
        ),
        compiler_params=params(46),
        cost_estimate=cost(2 * count * prefill * features * 2 * columns, 8 * features * columns),
        name="split_weight",
    )(plan, slots, *[hidden] * count, weight)
    return split, sends, keep


def base_products(plan, hidden, weight, first, count, prefill, after):
    n_t, features, width = weight.shape
    n_x = n_t // 2
    short = prefill // 2
    n_after = len(after)

    def body(plan_ref, x_ref, *rest):
        w_ref = rest[0]
        *send_refs, keep_ref = rest[1 + n_after :]
        live = plan_ref[LENGTH, first + pl.program_id(0)]

        def products(rows):
            dead = jnp.zeros((prefill - rows, width), BF)
            for j in range(n_t):
                out = jnp.dot(
                    x_ref[:rows], w_ref[j], preferred_element_type=F32
                ).astype(BF)
                if rows < prefill:
                    out = jnp.concatenate([out, dead], 0)
                if j == 0:
                    send_refs[0][...] = out
                elif j >= n_x:
                    keep_ref[j - n_x] = out
                else:

                    spans = pieces_of(count)
                    for k, (at, n) in enumerate(spans, 1 + (j - 1) * len(spans)):
                        inside = (pl.program_id(0) >= at) & (pl.program_id(0) < at + n)

                        @pl.when(inside)
                        def _():
                            send_refs[k][...] = out

        @pl.when(live > short)
        def _():
            products(prefill)

        @pl.when(live <= short)
        def _():
            products(short)

    spans = [(0, count)] + pieces_of(count) * (n_x - 1)
    parts = [n for _, n in spans]
    block = (prefill, width)
    places = [
        lambda i, p, at=at, n=n: (jnp.clip(i - at, 0, n - 1), 0) for at, n in spans
    ]
    *sends, keep = pl.pallas_call(
        body,
        out_shape=(
            *[jax.ShapeDtypeStruct((n * prefill, width), BF) for n in parts],
            jax.ShapeDtypeStruct((n_x, count * prefill, width), BF),
        ),
        grid_spec=pltpu.PrefetchScalarGridSpec(
            num_scalar_prefetch=1,
            grid=(count,),
            in_specs=[
                pl.BlockSpec(
                    (prefill, features), lambda i, p: (p[ORDER, first + i], 0)
                ),
            ]
            + [pl.BlockSpec(memory_space=pltpu.VMEM)]
            + [ANY] * n_after,
            out_specs=(
                *[pl.BlockSpec(block, place) for place in places],
                pl.BlockSpec((n_x, prefill, width), lambda i, p: (0, i, 0)),
            ),
        ),
        compiler_params=params(46),
        cost_estimate=cost(2 * count * prefill * features * width * n_t, 2 * n_t * features * width),
        name="base_products",
    )(plan, hidden, weight, *after)
    return sends, keep


def pair_sum(one, others, index, after):
    _, rows, width = one.shape
    n_piece = len(others)

    def body(a_ref, *rest):
        b_refs = rest[:n_piece]
        o_ref, mine, theirs, total, sems, out_sems = rest[n_piece + len(after) :]
        copies, outs = [], []
        spans, at = [], 0
        for b_ref in b_refs:
            spans.append(pl.ds(at, b_ref.shape[0]))
            at += b_ref.shape[0]
        for k, span in enumerate(spans):
            copies.append(
                (
                    pltpu.make_async_copy(
                        a_ref.at[index, span], mine.at[span], sems.at[0, k]
                    ),
                    pltpu.make_async_copy(b_refs[k], theirs.at[span], sems.at[1, k]),
                )
            )
            for copy in copies[-1]:
                copy.start()
        for k, span in enumerate(spans):
            for copy in copies[k]:
                copy.wait()
            value = mine[span].astype(F32) + theirs[span].astype(F32)
            total[span] = value.astype(BF)
            outs.append(
                pltpu.make_async_copy(total.at[span], o_ref.at[span], out_sems.at[k])
            )
            outs[-1].start()
        for copy in outs:
            copy.wait()

    return pl.pallas_call(
        body,
        out_shape=jax.ShapeDtypeStruct((rows, width), BF),
        in_specs=[ANY] * (1 + n_piece + len(after)),
        out_specs=ANY,
        scratch_shapes=[pltpu.VMEM((rows, width), BF)] * 3
        + [pltpu.SemaphoreType.DMA((2, n_piece)), pltpu.SemaphoreType.DMA((n_piece,))],
        compiler_params=params(12),
        cost_estimate=cost(rows * width, 6 * rows * width),
        name="pair_sum",
    )(one, *others, *after)


def hold(arrays, after):
    n = len(arrays)

    def body(*refs):
        pass

    return pl.pallas_call(
        body,
        out_shape=[jax.ShapeDtypeStruct(a.shape, a.dtype) for a in arrays],
        in_specs=[HBM] * (n + len(after)),
        out_specs=[HBM] * n,
        input_output_aliases={i: i for i in range(n)},
        compiler_params=params(8),
        cost_estimate=cost(0, 1 << 20),
        name="hold",
    )(*arrays, *after)


def fetch(refs, source, row, part, target, sem):
    for codes, ref in refs:
        hit = source == codes[0]
        for code in codes[1:]:
            hit |= source == code

        @pl.when(hit)
        def _():
            pltpu.make_async_copy(ref.at[row, part], target, sem).start()


def rank_products(plan, hidden, maps, first, count, prefill, after):
    sources = list(maps)
    features, ranks = hidden.shape[1], maps[sources[0]].shape[2]
    n_map, n_after = len(maps), len(after)
    short = prefill // 2
    down = pl.ds(0, features)

    def body(plan_ref, x_ref, *rest):
        refs = list(zip(sources, rest[:n_map]))
        o_ref, rows, held, sems = rest[n_map + n_after :]
        copies = []
        for i in range(count):
            fetch(
                refs,
                plan_ref[SOURCE, first + i],
                plan_ref[ROW, first + i],
                down,
                held.at[i],
                sems.at[0, i],
            )
            at = pl.multiple_of(plan_ref[ORDER, first + i] * prefill, prefill)
            copies.append(
                pltpu.make_async_copy(
                    x_ref.at[pl.ds(at, prefill)], rows.at[i], sems.at[1, i]
                )
            )
            copies[-1].start()
        for i in range(count):
            pltpu.make_async_copy(
                rest[0].at[0, down], held.at[i], sems.at[0, i]
            ).wait()
            copies[i].wait()
            live = plan_ref[LENGTH, first + i]
            above, below = i * prefill, i * prefill + short

            @pl.when(live > short)
            def _():
                o_ref[above : above + prefill] = jnp.dot(
                    rows[i], held[i], preferred_element_type=F32
                ).astype(BF)

            @pl.when(live <= short)
            def _():
                o_ref[above:below] = jnp.dot(
                    rows[i, :short], held[i], preferred_element_type=F32
                ).astype(BF)
                o_ref[below : below + short] = jnp.zeros((short, ranks), BF)

    return pl.pallas_call(
        body,
        out_shape=jax.ShapeDtypeStruct((count * prefill, ranks), BF),
        grid_spec=pltpu.PrefetchScalarGridSpec(
            num_scalar_prefetch=1,
            grid=(),
            in_specs=[HBM] * (1 + n_map + n_after),
            out_specs=pl.BlockSpec(memory_space=pltpu.VMEM),
            scratch_shapes=[
                pltpu.VMEM((count, prefill, features), BF),
                pltpu.VMEM((count, features, ranks), BF),
                pltpu.SemaphoreType.DMA((2, count)),
            ],
        ),
        compiler_params=params(16),
        cost_estimate=cost(2 * count * prefill * features * ranks, 2 * count * features * (prefill + ranks)),
        name="rank_products",
    )(plan, hidden, *maps.values(), *after)


def finish(plan, bases, ranks, maps, before, first, count, prefill, shape):
    sources = list(maps)
    columns, depth = shape[2], ranks[0][2][0].shape[1] // 2
    _, packed, lanes = maps[sources[0]].shape
    tiles = columns // lanes
    extra = tiles * 2 * depth
    up_part = pl.ds(packed - extra, extra)
    half = prefill // 2
    n_map = len(maps)
    n_base = max(len(pieces) for _, _, pieces in bases)
    n_rank = max(len(pieces) for _, _, pieces in ranks)

    def body(plan_ref, *rest):
        base_refs, rank_refs = [], []
        for refs, pieces in ((base_refs, bases), (rank_refs, ranks)):
            for start, n, arrays in pieces:
                refs.append((start, n, rest[: len(arrays)]))
                rest = rest[len(arrays) :]
        map_refs = list(zip(sources, rest[:n_map]))
        o_ref, token_ref, ups, base_rows, rank_rows, out_rows, sems, out_sems = rest[-8:]
        token_ref[...] = jnp.zeros_like(token_ref)

        def start_pieces(refs, at, rows, sem):
            copies = []
            for start, n, arrays in refs:
                if start <= at < start + n:
                    block = pl.ds((at - start) * prefill, prefill)
                    for k, ref in enumerate(arrays):
                        source = ref.at[0, block] if len(ref.shape) == 3 else ref.at[block]
                        copies.append(pltpu.make_async_copy(source, rows.at[k], sem.at[k]))
                        copies[-1].start()
            return copies

        copies = []
        for i in range(count):
            at = first + i
            copies.append(
                start_pieces(base_refs, at, base_rows.at[i], sems.at[i])
                + start_pieces(
                    rank_refs, at, rank_rows.at[i], sems.at[i, pl.ds(n_base, n_rank)]
                )
            )
            fetch(
                map_refs,
                plan_ref[SOURCE, at],
                plan_ref[ROW, at],
                up_part,
                ups.at[i],
                sems.at[i, n_base + n_rank],
            )

        group = half // tiles
        mix_row = lax.broadcasted_iota(jnp.int32, (2 * half, 2 * half), 0)
        mix_column = lax.broadcasted_iota(jnp.int32, (2 * half, 2 * half), 1)
        mix_token, mix_tile = mix_row // (2 * tiles), mix_row // 2 % tiles
        mix = mix_column == (mix_row % 2 * tiles + mix_tile) * group + mix_token
        mix = mix.astype(F32).astype(BF)
        token = lax.broadcasted_iota(jnp.int32, (half, 2 * columns), 0)

        def rows_for(i, live, b):
            rows = slice(b * half, (b + 1) * half)
            rank = rank_rows[i, 0, rows].astype(F32)
            for k in range(1, n_rank):
                rank += rank_rows[i, k, rows].astype(F32)
            rank = rank.astype(BF)
            up = jnp.concatenate(
                [ups[i, j * 2 * depth : (j + 1) * 2 * depth] for j in range(tiles)], 1
            )
            total = jnp.concatenate(
                [
                    jnp.dot(
                        rank[:, s * depth : (s + 1) * depth],
                        up[s * depth : (s + 1) * depth],
                        preferred_element_type=F32,
                    )
                    for s in range(2)
                ],
                1,
            )
            for k in range(n_base):
                total += base_rows[i, k, rows].astype(F32)
            total = jnp.where(token + b * half < live, total, 0.0).astype(BF)
            parts = [
                jnp.concatenate(
                    [
                        total[g * group : (g + 1) * group, k * lanes : (k + 1) * lanes]
                        for k in range(2 * tiles)
                    ],
                    0,
                )
                for g in range(tiles)
            ]
            mixed = jnp.dot(
                mix, jnp.concatenate(parts, 1), preferred_element_type=F32
            ).astype(BF)
            for g in range(tiles):
                at = b * half * tiles + g * half
                out_rows[i, at : at + half] = mixed[
                    :, g * lanes : (g + 1) * lanes
                ].reshape(half, 2, lanes)

        outs = []
        for i in range(count):
            for copy in copies[i]:
                copy.wait()
            pltpu.make_async_copy(
                map_refs[0][1].at[0, up_part], ups.at[i], sems.at[i, n_base + n_rank]
            ).wait()
            live = plan_ref[LENGTH, first + i]
            rows_for(i, live, 0)

            @pl.when(live > half)
            def _():
                rows_for(i, live, 1)

            @pl.when(live <= half)
            def _():
                out_rows[i, half * tiles :] = jnp.zeros((half * tiles, 2, lanes), BF)

            block = prefill * tiles
            row = pl.multiple_of(plan_ref[ORDER, first + i] * block, block)
            outs.append(
                pltpu.make_async_copy(
                    out_rows.at[i], o_ref.at[pl.ds(row, block)], out_sems.at[i]
                )
            )
            outs[-1].start()
        for copy in outs:
            copy.wait()

    operands = [plan]
    for _, _, pieces in bases + ranks:
        operands += pieces
    operands += maps.values()
    aliases = {}
    if before is not None:
        aliases = {len(operands): 0}
        operands.append(before)
    return pl.pallas_call(
        body,
        out_shape=(
            jax.ShapeDtypeStruct((shape[0] * tiles, 2, lanes), BF),
            jax.ShapeDtypeStruct((8, 128), F32),
        ),
        grid_spec=pltpu.PrefetchScalarGridSpec(
            num_scalar_prefetch=1,
            grid=(),
            in_specs=[HBM] * (len(operands) - 1),
            out_specs=(HBM, pl.BlockSpec(memory_space=pltpu.VMEM)),
            scratch_shapes=[
                pltpu.VMEM((count, extra, lanes), BF),
                pltpu.VMEM((count, n_base, prefill, 2 * columns), BF),
                pltpu.VMEM((count, n_rank, prefill, 2 * depth), BF),
                pltpu.VMEM((count, prefill * tiles, 2, lanes), BF),
                pltpu.SemaphoreType.DMA((count, n_base + n_rank + 1)),
                pltpu.SemaphoreType.DMA((count,)),
            ],
        ),
        input_output_aliases=aliases,
        compiler_params=params(24),
        cost_estimate=cost(12 * count * prefill * prefill * 2 * columns, 20 * count * prefill * columns),
        name="finish",
    )(*operands)


def solution(mesh):
    n_z, n_t = mesh.shape["adapter"], mesh.shape["tensor"]
    n_x = n_t // 2

    def core_swap(a):
        return lax.ppermute(a, "tensor", [(t, t ^ 1) for t in range(n_t)])

    def chip_shift(a, k):
        return lax.ppermute(
            a,
            "tensor",
            [(2 * x + c, 2 * ((x + k) % n_x) + c) for x in range(n_x) for c in (0, 1)],
        )

    def leftward(a, hops=1):
        return lax.ppermute(a, "adapter", [(z, z - hops) for z in range(hops, n_z)])

    def rightward(a, hops=1):
        return lax.ppermute(a, "adapter", [(z - hops, z) for z in range(hops, n_z)])

    def per_device(hidden, weight, down, up, table, adapters, lengths):
        requests = adapters.shape[0]
        prefill = hidden.shape[0] // requests
        stored = down.shape[0]
        columns = up.shape[3]
        by_distance = n_z == RANK_CHUNKS
        z, t = lax.axis_index("adapter"), lax.axis_index("tensor")
        plan = plan_requests(
            table, adapters, lengths, jnp.reshape(z, (1,)), n_z, stored
        )

        downs = {0: pack_maps(down, up)}

        def relay(hops, after):
            left, right = downs[hops - 1], downs[0 if hops == 1 else n_z + hops - 2]
            if after:
                left, right = hold([left, right], after)
                downs[hops - 1], downs[n_z + hops - 2] = left, right
            downs[hops] = leftward(left)
            downs[n_z - 1 + hops] = rightward(right)

        relay(1, [])

        def within(maps, hops):
            keys = range(hops + 1), range(n_z, n_z + hops)
            return {(k,): maps[k] for part in keys for k in part}

        dest = jnp.arange(n_t, dtype=jnp.int32)
        away = (dest // 2 - t // 2 + n_x) % n_x
        slots = jnp.where(dest % 2 == t % 2, n_x + away, away)

        bases, pairs = [], []

        def send_on(first, count, sends, keep, after):
            got = [core_swap(part) for part in sends[1:]] + [core_swap(sends[0])]
            pieces = [keep, got.pop()]
            n_piece = len(pieces_of(count))
            for k in range(1, n_x):
                pairs.append(pair_sum(keep, got[(k - 1) * n_piece : k * n_piece], k, after))
                pieces.append(chip_shift(pairs[-1], k))
            bases.append((first, count, pieces))

        def base(chunk):
            first, count = sum(BASE_CHUNKS[:chunk]), BASE_CHUNKS[chunk]
            return (first, count) + base_products(
                plan, hidden, split, first, count, prefill, pairs[-1:]
            )

        ranks = []
        count = requests // RANK_CHUNKS

        def rank(chunk, after):
            hops = chunk if by_distance else n_z - 1
            part = rank_products(
                plan, hidden, within(downs, hops), chunk * count, count, prefill, after
            )
            pair = (part.astype(F32) + core_swap(part).astype(F32)).astype(BF)
            pieces = [pair] + [chip_shift(pair, k) for k in range(1, n_x)]
            ranks.append((chunk * count, count, pieces))
            return part

        shape = (requests * prefill, 2, columns)

        def write(out, first, last):
            held = [
                b
                for b in bases
                if b[0] < last * count and b[0] + b[1] > first * count
            ]
            return finish(
                plan,
                held,
                ranks[first:last],
                within(downs, last - 1 if by_distance else n_z - 1),
                out,
                first * count,
                (last - first) * count,
                prefill,
                shape,
            )

        split, sends, keep = split_weight(
            plan, slots, hidden, weight, BASE_CHUNKS[0], prefill
        )
        send_on(0, BASE_CHUNKS[0], sends, keep, [])
        second = base(1)
        if n_z > 2:
            relay(2, [second[3]])
        send_on(*second, [bases[0][2][-1]])
        third = base(2)
        part = third[3]
        if by_distance:
            part = rank(0, [third[3], bases[1][2][-1]])
        send_on(*third, [part, bases[1][2][-1]])
        fourth = base(3)
        for hops in range(3, n_z):
            relay(hops, [fourth[3]])
        part = fourth[3]
        if by_distance:
            part = rank(1, [part])
            part = rank(2, [part, bases[2][2][-1]])
        summed = [pieces[-1] for _, _, pieces in ranks[:3]]
        send_on(*fourth, [part, bases[2][2][-1]] + summed)
        for chunk in range(len(ranks), 3):
            part = rank(chunk, [pairs[-1]])
        out, _ = write(None, 0, 2)
        out, written = write(out, 2, 3)
        rank(3, [written, bases[3][2][-1]])
        out, _ = write(out, 3, 4)
        tiles = out.shape[0] // shape[0]
        out = out.reshape(shape[0], tiles, 2, columns // tiles)
        return out.transpose(0, 2, 1, 3).reshape(shape)

    return jax.shard_map(
        per_device,
        mesh=mesh,
        in_specs=(
            P(("group", "adapter"), "tensor"),
            P("tensor", None, None),
            P(("group", "adapter"), "tensor", None),
            P(("group", "adapter"), None, None, "tensor"),
            P("group"),
            P(("group", "adapter")),
            P(("group", "adapter")),
        ),
        out_specs=P(("group", "adapter"), None, "tensor"),
        check_vma=False,
    )
```
